32 devices in a mesh: groups: 2 (over y), rows: 4 (over z), quad: 4 (over x, core).
Axes of the slice: x: 2, y: 2, z: 4, core: 2. Of those that a mesh axis runs over, the one named last changes fastest.
Arguments:
- sources: float32 [32, 256, 256], P(('groups', 'rows')), parts along dimension 0, may hold values from -6 to 6
- onsite: float32 [32, 256], P(('groups', 'rows')), parts along dimension 0, may hold values from -1.5 to 1.5
- strain: float32 [32, 256], P(('groups', 'rows')), parts along dimension 0, may hold values from 0.1 to 1.9
- present: int32 [32, 256], P(('groups', 'rows')), parts along dimension 0, may hold values 0 or 1
Outputs:
- moments: float32 [4, 2, 32, 256, 256], P('quad', None, ('groups', 'rows')), parts along dimension 2
- reduced: float32 [4, 2, 512, 256], P('quad', None, 'groups'), parts along dimension 2
The draws below stay inside these ranges and needn't reach their ends.
There are 2 independent parts, one for each index of `groups`. The reference program is written for one: setup_inputs(seed, part) draws one part's arguments, and reference() takes and returns one part's arrays. A program takes and returns all parts, laid end to end along the dimension named above; each array names one. Nothing has to cross between parts.
All inputs are finite; a program needn't handle non-finite values. No bound on the sum of `present` on one device may be relied on, other than what follows from the above.
Results may differ from the reference program's by a relative error of at most 0.00019.
Values sent between devices are 32-bit elements; how exact they have to be, the bound alone decides.
No kernel may reach another device: no remote copies, remote signals or barrier semaphores. Data moves between devices by JAX's collectives and lax.ppermute only.
A program may use at most 128 MiB of HBM per device.

```python
import math
import jax
import jax.numpy as jnp
from jax import lax

W = 256
NCOL = 256
TOTAL_PTS = 32
ITERS = 3
NLAT = 16
NPTS = 8
MOMS = 4
NORBS = 4096


def set_ends(array, own_key, least, top_value):
    dims = array.shape
    spot = [jax.random.randint(jax.random.fold_in(own_key, axis), (), 0, dims[axis]) for axis in range(len(dims))]
    array = array.at[tuple(spot)].set(least)
    longest = dims.index(max(dims))
    spot[longest] = (spot[longest] + 1) % dims[longest]
    return array.at[tuple(spot)].set(top_value)


def levels(stream_key, dims, pieces, least, top_value):
    def one(dim, blocks):
        steps = jax.random.uniform(jax.random.fold_in(jax.random.fold_in(stream_key, 6), dim), (blocks,), jnp.float32, least / len(pieces), top_value / len(pieces))
        return jnp.repeat(jnp.exp(steps), dims[dim] // blocks).reshape((-1,) + (1,) * (len(dims) - dim - 1))

    gain = one(*pieces[0])
    for cut in pieces[1:]:
        gain = gain * one(*cut)
    return gain


def scatter_about(key, shape, spread, limit, split=(), kind=jnp.bfloat16):
    array = spread * jax.random.normal(key, shape, jnp.float32)
    if split:
        array = array * levels(key, shape, split, -0.22, 0.18)
    return jnp.clip(array, -limit, limit).astype(kind)


def setup_inputs(seed: int = 0, part: int = 0) -> dict:
    key_of = jax.random.split(jax.random.key(seed), 5)
    part_splits = jax.random.split(jax.random.fold_in(key_of[4], part), 5)
    return {
        "sources": scatter_about(part_splits[0], (NLAT, W, NCOL), 1.0, 6.0, ((0, 4),), jnp.float32),
        "onsite": jnp.clip(jax.random.uniform(part_splits[1], (NLAT, W), jnp.float32, -1.5, 1.5) * levels(part_splits[1], (NLAT, W), ((0, 4),), -0.4, 0.0), -1.5, 1.5),
        "strain": jnp.clip(1.0 + 0.18 * jax.random.normal(part_splits[2], (NLAT, W), jnp.float32), 0.1, 1.9),
        "present": set_ends((jax.random.randint(part_splits[3], (NLAT, W), 0, 8) < 7).astype(jnp.int32), jax.random.fold_in(part_splits[3], 1), 0, 1),
    }


CENTER = 0.4
RADIUS = 1.0
HOPPING = 1.0


def hamiltonian(vector, onsite, scaled, upward):
    weighted = vector * scaled[:, :, None]
    padded_cols = jnp.pad(weighted, ((0, 0), (0, 0), (1, 1), (0, 0)))
    across = padded_cols[:, :, :-2] + padded_cols[:, :, 2:]
    padded_rows = jnp.pad(weighted, ((0, 0), (1, 1), (0, 0), (0, 0)))
    vertical = jnp.where(upward, padded_rows[:, 2:], padded_rows[:, :-2])
    return onsite[:, :, None] * vector - HOPPING * scaled[:, :, None] * (across + vertical)


def bilinear(first, second):
    real_part = jnp.sum(first[0] * second[0] - first[1] * second[1], axis=(0, 1))
    imag_part = jnp.sum(first[0] * second[1] + first[1] * second[0], axis=(0, 1))
    return real_part, imag_part


def divide(numerator, denominator):
    modulus = denominator[0] * denominator[0] + denominator[1] * denominator[1]
    real_part = (numerator[0] * denominator[0] + numerator[1] * denominator[1]) / modulus
    imag_part = (numerator[1] * denominator[0] - numerator[0] * denominator[1]) / modulus
    return real_part, imag_part


def combine(base, factor, operand):
    real_part = base[0] + factor[0] * operand[0] - factor[1] * operand[1]
    imag_part = base[1] + factor[0] * operand[1] + factor[1] * operand[0]
    return jnp.stack([real_part, imag_part])


def solve_point(sources, onsite, scaled, upward, shift_real, shift_imag):
    def operator(vector):
        applied = hamiltonian(vector, onsite, scaled, upward)
        real_part = shift_real * vector[0] - shift_imag * vector[1] - applied[0]
        imag_part = shift_real * vector[1] + shift_imag * vector[0] - applied[1]
        return jnp.stack([real_part, imag_part])

    initial = jnp.stack([sources, jnp.zeros_like(sources)])
    solution = jnp.zeros_like(initial)
    residual = initial
    search = initial
    norm_now = bilinear(residual, residual)
    for iteration in range(ITERS):
        applied = operator(search)
        curvature = bilinear(search, applied)
        step_size = divide(norm_now, curvature)
        solution = combine(solution, step_size, search)
        residual = combine(residual, (-step_size[0], -step_size[1]), applied)
        norm_next = bilinear(residual, residual)
        blend_ratio = divide(norm_next, norm_now)
        search = combine(residual, blend_ratio, search)
        norm_now = norm_next
    return solution


def reference(sources, onsite, strain, present):
    scaled = present.astype(jnp.float32) * strain
    row_index = jnp.arange(NLAT, dtype=jnp.int32)[:, None]
    site_index = jnp.arange(W, dtype=jnp.int32)[None, :]
    upward = ((row_index + site_index) % 2 == 0)[:, :, None]
    leading = TOTAL_PTS // 4 - NPTS // 2
    orders = jnp.arange(1, MOMS + 1, dtype=jnp.float32)
    moments = jnp.zeros((MOMS, 2, NLAT, W, NCOL), jnp.float32)
    for point in range(NPTS):
        angle = 2.0 * math.pi * (point + leading + 0.5) / TOTAL_PTS
        shift_real = CENTER + RADIUS * math.cos(angle)
        shift_imag = RADIUS * math.sin(angle)
        solution = solve_point(sources, onsite, scaled, upward, shift_real, shift_imag)
        weight_real = (RADIUS / NPTS) * jnp.cos(orders * angle)[:, None, None, None]
        weight_imag = (RADIUS / NPTS) * jnp.sin(orders * angle)[:, None, None, None]
        added = jnp.stack([weight_real * solution[0] - weight_imag * solution[1],
                           weight_real * solution[1] + weight_imag * solution[0]], axis=1)
        moments = moments + added
    flat_sources = sources.reshape(NLAT * W, NCOL)
    flat_moments = moments.reshape(MOMS, 2, NLAT * W, NCOL)
    reduced = jnp.einsum("nc,ksnd->kscd", flat_sources, flat_moments,
                         precision=lax.Precision.HIGHEST) / NORBS
    return moments, reduced
```

```python
import math

import jax
import jax.numpy as jnp
from jax import lax
from jax.sharding import PartitionSpec as P

TOTAL_PTS = 32
PTS_DEV = 2
CENTER = 0.4
RADIUS = 1.0
BOUND = 13.0


def shifted(value, step):
    n = lax.axis_size("rows")
    if step > 0:
        pairs = [(i, i + 1) for i in range(n - 1)]
    else:
        pairs = [(i + 1, i) for i in range(n - 1)]
    return lax.ppermute(value, "rows", pairs)


def extended(value):
    before = shifted(value[-1:], 1)
    after = shifted(value[:2], -1)
    return jnp.concatenate([before, value, after], axis=0)


def apply_h(v, onsite, scaled, upward):
    u = scaled[:, :, None] * v
    sides = jnp.pad(u, ((0, 0), (1, 1), (0, 0)))
    across = sides[:, :-2] + sides[:, 2:]
    rows = jnp.pad(u, ((1, 1), (0, 0), (0, 0)))
    vertical = jnp.where(upward, rows[2:], rows[:-2])
    return onsite[:, :, None] * v - scaled[:, :, None] * (across + vertical)


def ratio(top, bottom, good):
    return jnp.where(good, top / jnp.where(good, bottom, 1.0), 0.0)


def cmul(a, b):
    return (a[0] * b[0] - a[1] * b[1], a[0] * b[1] + a[1] * b[0])


def inverse(a):
    size = a[0] * a[0] + a[1] * a[1]
    return (a[0] / size, -a[1] / size)


def coefficients(mu, points, order):
    m0, m1, m2, m3, m4, m5 = mu
    tiny = jnp.float32(1e-7)
    ok0 = m0 > 0
    a0 = jnp.clip(ratio(m1, m0, ok0), -BOUND, BOUND)
    s11 = m2 - a0 * m1
    s12 = m3 - a0 * m2
    s13 = m4 - a0 * m3
    s14 = m5 - a0 * m4
    ok1 = ok0 & (s11 > tiny * m2)
    b1 = jnp.maximum(ratio(s11, m0, ok1), 0.0)
    g1 = ratio(s12, s11, ok1)
    a1 = jnp.clip(g1 - a0, -BOUND, BOUND)
    s22 = s13 - a1 * s12 - b1 * m2
    s23 = s14 - a1 * s13 - b1 * m3
    ok2 = ok1 & (s22 > tiny * m4)
    b2 = jnp.maximum(ratio(s22, s11, ok2), 0.0)
    a2 = jnp.clip(ratio(s23, s22, ok2) - g1, -BOUND, BOUND)
    leading = TOTAL_PTS // 4 - points // 2
    p = lax.broadcasted_iota(jnp.int32, (points, 1), 0).astype(jnp.float32)
    angle = 2.0 * math.pi * (p + leading + 0.5) / TOTAL_PTS
    zr = CENTER + RADIUS * jnp.cos(angle)
    zi = RADIUS * jnp.sin(angle)
    wr = RADIUS / points * jnp.cos(order * angle)
    wi = RADIUS / points * jnp.sin(order * angle)
    i2 = inverse((zr - a2, zi + 0.0 * a2))
    i1 = inverse((zr - a1 - b2 * i2[0], zi - b2 * i2[1]))
    y0 = inverse((zr - a0 - b1 * i1[0], zi - b1 * i1[1]))
    y0 = cmul((wr, wi), y0)
    y1 = cmul(y0, i1)
    y2 = cmul(y1, i2)
    out = []
    for part in range(2):
        t0, t1, t2 = (jnp.sum(y[part], axis=0) for y in (y0, y1, y2))
        out.append((t0 - a0 * t1 + (a0 * a1 - b1) * t2, t1 - (a0 + a1) * t2, t2))
    return out


def body(sources, onsite, strain, present):
    points = PTS_DEV * lax.axis_size("quad")
    order = (lax.axis_index("quad") + 1).astype(jnp.float32)
    scaled = present.astype(jnp.float32) * strain
    rows, sites, columns = sources.shape
    orbitals = rows * sites * lax.axis_size("rows")
    small = extended(jnp.stack([scaled, onsite], axis=-1))
    scaled_x, onsite_x = small[..., 0], small[..., 1]
    b = extended(sources)
    row = lax.broadcasted_iota(jnp.int32, (rows + 3, sites), 0) + 1
    site = lax.broadcasted_iota(jnp.int32, (rows + 3, sites), 1)
    upward = ((row + site) % 2 == 0)[:, :, None]
    w1 = apply_h(b, onsite_x, scaled_x, upward)
    w2 = apply_h(w1, onsite_x, scaled_x, upward)
    doubled = jnp.concatenate([jnp.zeros_like(w2[:1]), w2[1 : rows + 1], 2.0 * w2[rows + 1 : rows + 2], jnp.zeros_like(w2[:1])])
    w3 = apply_h(doubled, onsite_x, scaled_x, upward)
    b, w1, w2, w3 = (v[1 : rows + 1] for v in (b, w1, w2, w3))
    pairs = ((b, b), (b, w1), (w1, w1), (w1, w2), (w2, w2), (w2, w3))
    mu = jnp.stack([jnp.sum(x * y, axis=(0, 1)) for x, y in pairs])
    flat = [v.reshape(rows * sites, columns) for v in (b, w1, w2)]
    gram = jnp.stack([jnp.einsum("na,nb->ab", flat[0], v, precision=lax.Precision.HIGHEST) for v in flat])
    mu = lax.psum(mu, "rows")
    gram = lax.psum(gram, "rows")
    coefs = coefficients(mu, points, order)
    moments = jnp.stack([c[0] * b + c[1] * w1 + c[2] * w2 for c in coefs])
    reduced = jnp.stack([(c[0] * gram[0] + c[1] * gram[1] + c[2] * gram[2]) / orbitals for c in coefs])
    return moments[None], reduced[None]


def solution(mesh):
    in_specs = (
        P(("groups", "rows"), None, None),
        P(("groups", "rows"), None),
        P(("groups", "rows"), None),
        P(("groups", "rows"), None),
    )
    out_specs = (P("quad", None, ("groups", "rows"), None, None), P("quad", None, "groups", None))
    return jax.shard_map(body, mesh=mesh, in_specs=in_specs, out_specs=out_specs, check_vma=False)
```

```python
import functools
import math

import jax
import jax.numpy as jnp
from jax import lax
from jax.experimental import pallas as pl
from jax.experimental.pallas import tpu as pltpu
from jax.sharding import PartitionSpec as P

TOTAL_PTS = 32
PTS_DEV = 2
CENTER = 0.4
RADIUS = 1.0
BOUND = 13.0
LANES = 128
F32 = jnp.float32
BF16 = jnp.bfloat16
PARAMS = pltpu.CompilerParams(vmem_limit_bytes=32 * 1024 * 1024)
VMEM = pl.BlockSpec(memory_space=pltpu.VMEM)
SMEM = pl.BlockSpec(memory_space=pltpu.SMEM)
ANY = pl.BlockSpec(memory_space=pl.ANY)


def ratio(top, bottom, good):
    return jnp.where(good, top / jnp.where(good, bottom, 1.0), 0.0)


def cmul(a, b):
    return (a[0] * b[0] - a[1] * b[1], a[0] * b[1] + a[1] * b[0])


def inverse(a):
    size = a[0] * a[0] + a[1] * a[1]
    return (a[0] / size, -a[1] / size)


def coefficients(mu, points, order):
    m0, m1, m2, m3, m4, m5 = mu
    tiny = F32(1e-7)
    ok0 = m0 > 0
    a0 = jnp.clip(ratio(m1, m0, ok0), -BOUND, BOUND)
    s11 = m2 - a0 * m1
    s12 = m3 - a0 * m2
    s13 = m4 - a0 * m3
    s14 = m5 - a0 * m4
    ok1 = ok0 & (s11 > tiny * m2)
    b1 = jnp.maximum(ratio(s11, m0, ok1), 0.0)
    g1 = ratio(s12, s11, ok1)
    a1 = jnp.clip(g1 - a0, -BOUND, BOUND)
    s22 = s13 - a1 * s12 - b1 * m2
    s23 = s14 - a1 * s13 - b1 * m3
    ok2 = ok1 & (s22 > tiny * m4)
    b2 = jnp.maximum(ratio(s22, s11, ok2), 0.0)
    a2 = jnp.clip(ratio(s23, s22, ok2) - g1, -BOUND, BOUND)
    leading = TOTAL_PTS // 4 - points // 2
    p = lax.broadcasted_iota(jnp.int32, (points, m0.shape[1]), 0).astype(F32)
    angle = 2.0 * math.pi * (p + leading + 0.5) / TOTAL_PTS
    zr = CENTER + RADIUS * jnp.cos(angle)
    zi = RADIUS * jnp.sin(angle)
    wr = RADIUS / points * jnp.cos(order * angle)
    wi = RADIUS / points * jnp.sin(order * angle)
    i2 = inverse((zr - a2, zi))
    i1 = inverse((zr - a1 - b2 * i2[0], zi - b2 * i2[1]))
    y0 = inverse((zr - a0 - b1 * i1[0], zi - b1 * i1[1]))
    y0 = cmul((wr, wi), y0)
    y1 = cmul(y0, i1)
    y2 = cmul(y1, i2)
    out = []
    for part in range(2):
        t0, t1, t2 = (jnp.sum(y[part], axis=0, keepdims=True) for y in (y0, y1, y2))
        out.append((t0 - a0 * t1 + (a0 * a1 - b1) * t2, t1 - (a0 + a1) * t2, t2))
    return out


def spread(table_ref, parity, lane):
    half = table_ref.shape[0] // 2
    rows = table_ref[pl.ds(parity, half, stride=2), :]
    return jnp.broadcast_to(rows[:, lane : lane + 1], (half, LANES))


def horizontal(even, odd):
    size = even.shape[0]
    site = lax.broadcasted_iota(jnp.int32, even.shape, 0)
    left = jnp.where(site == 0, 0.0, pltpu.roll(odd, 1, 0))
    right = jnp.where(site == size - 1, 0.0, pltpu.roll(even, size - 1, 0))
    return odd + left, even + right


def site_table(onsite_ref, strain_ref, present_ref):
    scaled = present_ref[...].astype(F32) * strain_ref[...]
    return jnp.concatenate([scaled, onsite_ref[...]], axis=0)


def edges_kernel(half_ref, sources_ref, onsite_ref, strain_ref, present_ref, up_ref, down_ref, rows_ref, table_ref, sem):
    rows = sources_ref.shape[0]
    sites = sources_ref.shape[1]
    count = sites // 2
    columns = pl.ds(pl.multiple_of(half_ref[0] * LANES, LANES), LANES)
    copies = []
    for slot, row in enumerate((0, 1, rows - 1)):
        copy = pltpu.make_async_copy(sources_ref.at[row, :, columns], rows_ref.at[slot], sem.at[slot])
        copy.start()
        copies.append(copy)
    table = site_table(onsite_ref, strain_ref, present_ref)
    tail = table.shape[0]
    table_ref[:, :tail] = table.T
    for ref, blocks in ((up_ref, 2), (down_ref, 3)):
        for part in range(sites // LANES):
            ref[pl.ds(blocks * count + part * tail, tail), :] = table[:, part * LANES : (part + 1) * LANES]
    for copy in copies:
        copy.wait()
    for ref, block, slot, row, parity in (
        (down_ref, 0, 0, 0, 0),
        (down_ref, 1, 0, 0, 1),
        (down_ref, 2, 1, 1, 0),
        (up_ref, 0, 2, rows - 1, 0),
        (up_ref, 1, 2, rows - 1, 1),
    ):
        value = rows_ref[slot, pl.ds(parity, count, stride=2), :]
        ref[pl.ds(block * count, count), :] = value * spread(table_ref, parity, row)


def fold(value):
    return jnp.sum(value.reshape(value.shape[0] // 8, 8, value.shape[1]), axis=0)


def fields_kernel(
    parts, place_ref, sources_ref, onsite_ref, strain_ref, present_ref, below_ref, above_ref, *refs
):
    chunk_refs, (w_ref, full_ref, half_ref, table_ref, far_ref, left_hi, left_lo, right_hi, right_lo, gram_ref, sem) = (
        refs[:parts],
        refs[parts:],
    )
    rows, sites, _ = sources_ref.shape
    count = sites // 2
    half = place_ref[0]
    mine = place_ref[1]
    columns = pl.ds(pl.multiple_of(half * LANES, LANES), LANES)
    copy_half = pltpu.make_async_copy(sources_ref.at[:, :, columns], half_ref, sem.at[0])
    copies_full = [
        pltpu.make_async_copy(sources_ref.at[:, :, pl.ds(side * LANES, LANES)], full_ref.at[side], sem.at[1 + side])
        for side in range(2)
    ]
    copy_half.start()
    for copy in copies_full:
        copy.start()
    table = site_table(onsite_ref, strain_ref, present_ref)
    tail = table.shape[0]
    table_ref[:, :tail] = table.T
    for slot, (ref, blocks) in enumerate(((below_ref, 2), (above_ref, 3))):
        for part in range(sites // LANES):
            far_ref[slot, pl.ds(part * LANES, LANES), :tail] = ref[pl.ds(blocks * count + part * tail, tail), :].T
    top = rows - 1

    def block(ref, index):
        return ref[pl.ds(index * count, count), :]

    def bound_up(i, p):
        return (i + p) % 2 == 0

    copy_half.wait()
    keys = [(i, p) for i in range(rows) for p in range(2)]
    scale = {(i, p): spread(table_ref, p, i) for i, p in keys}
    level = {(i, p): spread(table_ref, p, rows + i) for i, p in keys}
    b = {(i, p): half_ref[i, pl.ds(p, count, stride=2), :] for i, p in keys}
    u0 = {k: scale[k] * b[k] for k in keys}
    below0 = [block(below_ref, p) for p in range(2)]
    above0 = [block(above_ref, p) for p in range(2)]
    above_next = block(above_ref, 2)

    def near(u, up_halo, down_halo):
        out = {}
        for i in range(rows):
            sums = horizontal(u[i, 0], u[i, 1])
            for p in range(2):
                if bound_up(i, p):
                    other = u[i + 1, p] if i < top else up_halo
                else:
                    other = u[i - 1, p] if i > 0 else down_halo
                out[i, p] = sums[p] if other is None else sums[p] + other
        return out

    n0 = near(u0, above0[1], below0[1])
    w1 = {k: level[k] * b[k] - scale[k] * n0[k] for k in keys}
    u1 = {k: scale[k] * w1[k] for k in keys}

    far_table = far_ref.at[0]
    scale_below = spread(far_table, 1, top)
    level_below = spread(far_table, 1, rows + top)
    sums = horizontal(below0[0], below0[1])
    below1 = level_below * below0[1] - scale_below * scale_below * (sums[1] + u0[0, 1])
    far_table = far_ref.at[1]
    square_above = [spread(far_table, p, 0) for p in range(2)]
    square_above = [x * x for x in square_above]
    level_above = [spread(far_table, p, rows) for p in range(2)]
    sums = horizontal(above0[0], above0[1])
    above1 = [
        level_above[0] * above0[0] - square_above[0] * (sums[0] + above_next),
        level_above[1] * above0[1] - square_above[1] * (sums[1] + u0[top, 1]),
    ]
    n1 = near(u1, above1[1], below1)
    w2 = {k: level[k] * w1[k] - scale[k] * n1[k] for k in keys}
    u2 = {k: scale[k] * w2[k] for k in keys}
    sums = horizontal(above1[0], above1[1])
    above2 = level_above[1] * above1[1] - square_above[1] * (sums[1] + u1[top, 1])
    n2 = near(u2, 2.0 * above2, None)

    def total(term):
        return jnp.sum(functools.reduce(jnp.add, [fold(term(k)) for k in keys]), axis=0, keepdims=True)

    mu = [
        total(lambda k: b[k] * b[k]),
        total(lambda k: b[k] * w1[k]),
        total(lambda k: w1[k] * w1[k]),
        total(lambda k: w1[k] * w2[k]),
        total(lambda k: w2[k] * w2[k]),
        total(lambda k: level[k] * w2[k] * w2[k] - u2[k] * n2[k]),
    ]
    mu = jnp.concatenate(mu + [jnp.zeros_like(mu[0])] * 2, axis=0)

    for index, (i, p) in enumerate(keys):
        w_ref[0, i, p] = w1[i, p]
        w_ref[1, i, p] = w2[i, p]
        at = pl.ds(index * count, count)
        for j, value in enumerate((b[i, p], w1[i, p], w2[i, p])):
            high = value.astype(BF16)
            right_hi[at, j * LANES : (j + 1) * LANES] = high
            right_lo[at, j * LANES : (j + 1) * LANES] = (value - high.astype(F32)).astype(BF16)
    for copy in copies_full:
        copy.wait()
    for index, (i, p) in enumerate(keys):
        at = pl.ds(index * count, count)
        for part in range(2):
            lanes = slice(part * LANES, (part + 1) * LANES)
            value = full_ref[part, i, pl.ds(p, count, stride=2), :]
            high = value.astype(BF16)
            left_hi[at, lanes] = high
            left_lo[at, lanes] = (value - high.astype(F32)).astype(BF16)

    def product(left, right):
        return lax.dot_general(left[...], right[...], (((0,), (0,)), ((), ())), preferred_element_type=F32)

    gram = product(left_hi, right_hi) + (product(left_hi, right_lo) + product(left_lo, right_hi))
    row = lax.broadcasted_iota(jnp.int32, (LANES, LANES), 0)
    lane = lax.broadcasted_iota(jnp.int32, (LANES, LANES), 1)
    for j in range(3):
        first = gram[:LANES, j * LANES : (j + 1) * LANES]
        second = gram[LANES:, j * LANES : (j + 1) * LANES]
        own = jnp.where(half == 0, first, second)
        cross = jnp.where(half == 0, second, first)
        gram_ref[pl.ds(j * LANES, LANES), :] = jnp.where(row < lane, own, cross)
    size = 3 * LANES // parts
    for part, ref in enumerate(chunk_refs):
        start = pl.multiple_of((mine ^ part) * size if parts > 1 else 0, 8)
        ref[pl.ds(0, size), :] = gram_ref[pl.ds(start, size), :]
        ref[pl.ds(size, 8), :] = mu


def moments_kernel(
    points, place_ref, sources_ref, w_ref, v_ref, mu_ref, nu_ref, out_ref, coef_ref, source_ref, made_ref, in_sem, out_sem
):
    half = place_ref[0]
    rows, sites, _ = sources_ref.shape
    count = sites // 2
    loads = {}
    for i in range(rows):
        for side in range(2):
            loads[i, side] = pltpu.make_async_copy(
                sources_ref.at[i, :, pl.ds(side * LANES, LANES)], source_ref.at[i, side], in_sem.at[i, side]
            )
            loads[i, side].start()
    first = jnp.where(half == 0, mu_ref[...], nu_ref[...])
    second = jnp.where(half == 0, nu_ref[...], mu_ref[...])
    mu = jnp.concatenate([first, second], axis=1)
    coefs = coefficients([mu[n : n + 1] for n in range(6)], points, (place_ref[2] + 1).astype(F32))
    lines = [line for part in coefs for line in part]
    coef_ref[...] = jnp.concatenate(lines + [jnp.zeros_like(lines[0])] * 2, axis=0)
    stores = []
    for i in range(rows):
        for side in range(2):
            loads[i, side].wait()
            lanes = slice(side * LANES, (side + 1) * LANES)
            for p in range(2):
                spots = pl.ds(p, count, stride=2)
                near = [jnp.where(half == side, w_ref[j, i, p], v_ref[j, i, p]) for j in range(2)]
                fields = [source_ref[i, side, spots, :]] + near
                for part in range(2):
                    terms = [lines[3 * part + j][:, lanes] * fields[j] for j in range(3)]
                    made_ref[part, i, side, spots, :] = terms[0] + terms[1] + terms[2]
            for part in range(2):
                copy = pltpu.make_async_copy(
                    made_ref.at[part, i, side],
                    out_ref.at[0, part, i, :, pl.ds(side * LANES, LANES)],
                    out_sem.at[part, i, side],
                )
                copy.start()
                stores.append(copy)
    for copy in stores:
        copy.wait()


def reduced_kernel(parts, orbitals, place_ref, coef_ref, mu_ref, nu_ref, *refs):
    own_refs, far_refs, (out_ref, own_tile, far_tile) = refs[:parts], refs[parts : 2 * parts], refs[2 * parts :]
    half = place_ref[0]
    mine = place_ref[1]
    size = 3 * LANES // parts
    for tile, chunk_refs in ((own_tile, own_refs), (far_tile, far_refs)):
        for part, ref in enumerate(chunk_refs):
            start = pl.multiple_of((mine ^ part) * size if parts > 1 else 0, 8)
            tile[pl.ds(start, size), :] = ref[pl.ds(0, size), :]
    row = lax.broadcasted_iota(jnp.int32, (LANES, LANES), 0)
    lane = lax.broadcasted_iota(jnp.int32, (LANES, LANES), 1)
    own_mu = mu_ref[...]
    far_mu = nu_ref[...]
    sums = {}
    for j in range(3):
        at = pl.ds(j * LANES, LANES)
        t0 = jnp.where(half == 0, own_tile[at, :], far_tile[at, :])
        t1 = jnp.where(half == 0, far_tile[at, :], own_tile[at, :])
        d0 = jnp.where(half == 0, own_mu[j : j + 1], far_mu[j : j + 1])
        d1 = jnp.where(half == 0, far_mu[j : j + 1], own_mu[j : j + 1])
        f0, f1 = t0.T, t1.T
        blocks = {
            (0, 0): jnp.where(row < lane, t0, jnp.where(row > lane, f0, d0)),
            (1, 1): jnp.where(row < lane, t1, jnp.where(row > lane, f1, d1)),
            (1, 0): jnp.where(row >= lane, t0, f1),
            (0, 1): jnp.where(row <= lane, f0, t1),
        }
        for (x, y), value in blocks.items():
            for part in range(2):
                coef = coef_ref[3 * part + j : 3 * part + j + 1, y * LANES : (y + 1) * LANES] * F32(1.0 / orbitals)
                term = coef * value
                sums[part, x, y] = term if j == 0 else sums[part, x, y] + term
    for (part, x, y), value in sums.items():
        out_ref[0, part, x * LANES : (x + 1) * LANES, y * LANES : (y + 1) * LANES] = value


def struct(*shape, dtype=F32):
    return jax.ShapeDtypeStruct(shape, dtype)


def body(sources, onsite, strain, present):
    n_rows = lax.axis_size("rows")
    n_quad = lax.axis_size("quad")
    points = PTS_DEV * n_quad
    mine = lax.axis_index("rows")
    quad = lax.axis_index("quad")
    place = jnp.stack([quad % 2, mine, quad]).astype(jnp.int32)
    rows, sites, columns = sources.shape
    count = sites // 2
    orbitals = rows * sites * n_rows
    tail = 2 * rows * (sites // LANES)
    up, down = pl.pallas_call(
        edges_kernel,
        out_shape=(struct(2 * count + tail, LANES), struct(3 * count + tail, LANES)),
        in_specs=[SMEM, ANY, VMEM, VMEM, VMEM],
        out_specs=(VMEM, VMEM),
        scratch_shapes=[
            pltpu.VMEM((3, sites, LANES), F32),
            pltpu.VMEM((sites, LANES), F32),
            pltpu.SemaphoreType.DMA((3,)),
        ],
        compiler_params=PARAMS,
        name="edges",
    )(place, sources, onsite, strain, present)
    below = lax.ppermute(up, "rows", [(i, i + 1) for i in range(n_rows - 1)])
    above = lax.ppermute(down, "rows", [(i + 1, i) for i in range(n_rows - 1)])

    pairwise = n_rows & (n_rows - 1) == 0 and (3 * LANES) % (8 * n_rows) == 0
    parts = n_rows if pairwise else 1
    size = 3 * LANES // parts
    *chunks, fields = pl.pallas_call(
        functools.partial(fields_kernel, parts),
        out_shape=(struct(size + 8, LANES),) * parts + (struct(2, rows, 2, count, LANES),),
        in_specs=[SMEM, ANY, VMEM, VMEM, VMEM, VMEM, VMEM],
        out_specs=(VMEM,) * (parts + 1),
        scratch_shapes=[
            pltpu.VMEM((2, rows, sites, LANES), F32),
            pltpu.VMEM((rows, sites, LANES), F32),
            pltpu.VMEM((sites, LANES), F32),
            pltpu.VMEM((2, sites, LANES), F32),
            pltpu.VMEM((rows * sites, columns), BF16),
            pltpu.VMEM((rows * sites, columns), BF16),
            pltpu.VMEM((rows * sites, 3 * LANES), BF16),
            pltpu.VMEM((rows * sites, 3 * LANES), BF16),
            pltpu.VMEM((3 * LANES, LANES), F32),
            pltpu.SemaphoreType.DMA((3,)),
        ],
        compiler_params=PARAMS,
        name="fields",
    )(place, sources, onsite, strain, present, below, above)

    def partner(value):
        return lax.ppermute(value, "quad", [(i, i ^ 1) for i in range(n_quad)])

    def across(value, mask):
        return lax.ppermute(value, "rows", [(i, i ^ mask) for i in range(n_rows)])

    far_fields = partner(fields)
    if pairwise:
        summed = chunks[0]
        for mask in range(1, n_rows):
            summed = summed + across(chunks[mask], mask)
        sums = [summed[:size]] + [across(summed[:size], mask) for mask in range(1, n_rows)]
    else:
        summed = lax.psum(chunks[0], "rows")
        sums = [summed[:size]]
    mu = summed[size:]
    far_mu = partner(mu)
    far_sums = [partner(value) for value in sums]

    moments, coefs = pl.pallas_call(
        functools.partial(moments_kernel, points),
        out_shape=(struct(1, 2, rows, sites, columns), struct(8, columns)),
        in_specs=[SMEM, ANY, VMEM, VMEM, VMEM, VMEM],
        out_specs=(ANY, VMEM),
        scratch_shapes=[
            pltpu.VMEM((rows, 2, sites, LANES), F32),
            pltpu.VMEM((2, rows, 2, sites, LANES), F32),
            pltpu.SemaphoreType.DMA((rows, 2)),
            pltpu.SemaphoreType.DMA((2, rows, 2)),
        ],
        compiler_params=PARAMS,
        name="moments",
    )(place, sources, fields, far_fields, mu, far_mu)
    reduced = pl.pallas_call(
        functools.partial(reduced_kernel, parts, orbitals),
        out_shape=struct(1, 2, columns, columns),
        in_specs=[SMEM] + [VMEM] * (3 + 2 * parts),
        out_specs=VMEM,
        scratch_shapes=[pltpu.VMEM((3 * LANES, LANES), F32), pltpu.VMEM((3 * LANES, LANES), F32)],
        compiler_params=PARAMS,
        name="reduced",
    )(place, coefs, mu, far_mu, *sums, *far_sums)
    return moments, reduced


def solution(mesh):
    in_specs = (
        P(("groups", "rows"), None, None),
        P(("groups", "rows"), None),
        P(("groups", "rows"), None),
        P(("groups", "rows"), None),
    )
    out_specs = (P("quad", None, ("groups", "rows"), None, None), P("quad", None, "groups", None))
    return jax.shard_map(body, mesh=mesh, in_specs=in_specs, out_specs=out_specs, check_vma=False)
```

```python
import functools
import math

import jax
import jax.numpy as jnp
from jax import lax
from jax.experimental import pallas as pl
from jax.experimental.pallas import tpu as pltpu
from jax.sharding import PartitionSpec as P

TOTAL_PTS = 32
PTS_DEV = 2
CENTER = 0.4
RADIUS = 1.0
BOUND = 13.0
LANES = 128
F32 = jnp.float32
BF16 = jnp.bfloat16
PARAMS = pltpu.CompilerParams(vmem_limit_bytes=32 * 1024 * 1024)
VMEM = pl.BlockSpec(memory_space=pltpu.VMEM)
HBM = pl.BlockSpec(memory_space=pltpu.HBM)
ANY = pl.BlockSpec(memory_space=pl.ANY)


def ratio(top, bottom, good):
    return jnp.where(good, top / jnp.where(good, bottom, 1.0), 0.0)


def cmul(a, b):
    return (a[0] * b[0] - a[1] * b[1], a[0] * b[1] + a[1] * b[0])


def inverse(a):
    size = a[0] * a[0] + a[1] * a[1]
    return (a[0] / size, -a[1] / size)


def coefficients(mu, points, order):
    m0, m1, m2, m3, m4, m5 = mu
    tiny = F32(1e-7)
    ok0 = m0 > 0
    a0 = jnp.clip(ratio(m1, m0, ok0), -BOUND, BOUND)
    s11 = m2 - a0 * m1
    s12 = m3 - a0 * m2
    s13 = m4 - a0 * m3
    s14 = m5 - a0 * m4
    ok1 = ok0 & (s11 > tiny * m2)
    b1 = jnp.maximum(ratio(s11, m0, ok1), 0.0)
    g1 = ratio(s12, s11, ok1)
    a1 = jnp.clip(g1 - a0, -BOUND, BOUND)
    s22 = s13 - a1 * s12 - b1 * m2
    s23 = s14 - a1 * s13 - b1 * m3
    ok2 = ok1 & (s22 > tiny * m4)
    b2 = jnp.maximum(ratio(s22, s11, ok2), 0.0)
    a2 = jnp.clip(ratio(s23, s22, ok2) - g1, -BOUND, BOUND)
    leading = TOTAL_PTS // 4 - points // 2
    p = lax.broadcasted_iota(jnp.int32, (points, m0.shape[1]), 0).astype(F32)
    angle = 2.0 * math.pi * (p + leading + 0.5) / TOTAL_PTS
    zr = CENTER + RADIUS * jnp.cos(angle)
    zi = RADIUS * jnp.sin(angle)
    wr = RADIUS / points * jnp.cos(order * angle)
    wi = RADIUS / points * jnp.sin(order * angle)
    i2 = inverse((zr - a2, zi))
    i1 = inverse((zr - a1 - b2 * i2[0], zi - b2 * i2[1]))
    y0 = inverse((zr - a0 - b1 * i1[0], zi - b1 * i1[1]))
    y0 = cmul((wr, wi), y0)
    y1 = cmul(y0, i1)
    y2 = cmul(y1, i2)
    out = []
    for part in range(2):
        t0, t1, t2 = (jnp.sum(y[part], axis=0, keepdims=True) for y in (y0, y1, y2))
        out.append((t0 - a0 * t1 + (a0 * a1 - b1) * t2, t1 - (a0 + a1) * t2, t2))
    return out


def spread(table_ref, parity, lane):
    half = table_ref.shape[0] // 2
    rows = table_ref[pl.ds(parity, half, stride=2), :]
    return jnp.broadcast_to(rows[:, lane : lane + 1], (half, LANES))


def horizontal(even, odd):
    size = even.shape[0]
    site = lax.broadcasted_iota(jnp.int32, even.shape, 0)
    left = jnp.where(site == 0, 0.0, pltpu.roll(odd, 1, 0))
    right = jnp.where(site == size - 1, 0.0, pltpu.roll(even, size - 1, 0))
    return odd + left, even + right


def site_table(onsite, strain, present):
    return jnp.concatenate([present.astype(F32) * strain, onsite], axis=0)


def bound_up(i, p):
    return (i + p) % 2 == 0


def fold(value):
    return jnp.sum(value.reshape(value.shape[0] // 8, 8, value.shape[1]), axis=0)


def total(terms):
    return jnp.sum(functools.reduce(jnp.add, [fold(term) for term in terms]), axis=0, keepdims=True)


def split(value):
    high = value.astype(BF16)
    return high, (value - high.astype(F32)).astype(BF16)


def edges_kernel(
    sources_ref, onsite_ref, strain_ref, present_ref, up_ref, down_ref, table_ref,
    rows_ref, onsite_in, strain_in, present_in, sem,
):
    rows, sites, _ = sources_ref.shape
    count = sites // 2
    columns = pl.ds(pl.multiple_of(lax.rem(lax.axis_index("quad"), 2) * LANES, LANES), LANES)
    pairs = [(onsite_ref, onsite_in), (strain_ref, strain_in), (present_ref, present_in)]
    for slot, row in enumerate((0, 1, rows - 1)):
        pairs.append((sources_ref.at[row, :, columns], rows_ref.at[slot]))
    copies = [pltpu.make_async_copy(src, dst, sem.at[k]) for k, (src, dst) in enumerate(pairs)]
    for copy in copies:
        copy.start()
    for copy in copies[:3]:
        copy.wait()
    table = site_table(onsite_in[...], strain_in[...], present_in[...])
    tail = table.shape[0]
    table_ref[:, :tail] = table.T
    for ref, blocks in ((up_ref, 2), (down_ref, 3)):
        for part in range(sites // LANES):
            ref[pl.ds(blocks * count + part * tail, tail), :] = table[:, part * LANES : (part + 1) * LANES]
    for copy in copies[3:]:
        copy.wait()
    for ref, block, slot, row, parity in (
        (down_ref, 0, 0, 0, 0),
        (down_ref, 1, 0, 0, 1),
        (down_ref, 2, 1, 1, 0),
        (up_ref, 0, 2, rows - 1, 0),
        (up_ref, 1, 2, rows - 1, 1),
    ):
        value = rows_ref[slot, pl.ds(parity, count, stride=2), :]
        ref[pl.ds(block * count, count), :] = value * spread(table_ref, parity, row)


def near(u, wanted, up_halo, down_halo, top):
    out = {}
    for i in wanted:
        sums = horizontal(u[i, 0], u[i, 1])
        for p in range(2):
            if bound_up(i, p):
                other = u[i + 1, p] if i < top else up_halo
            else:
                other = u[i - 1, p] if i > 0 else down_halo
            out[i, p] = sums[p] if other is None else sums[p] + other
    return out


def inner_kernel(sources_ref, table_ref, b_ref, w1_ref, w2_ref, mu_ref, gram_ref, left_hi_ref, left_lo_ref, full_ref, sem):
    rows, sites, _ = sources_ref.shape
    count = sites // 2
    top = rows - 1
    half = lax.rem(lax.axis_index("quad"), 2)
    copies = [
        pltpu.make_async_copy(sources_ref.at[:, :, pl.ds(side * LANES, LANES)], full_ref.at[side], sem.at[side])
        for side in range(2)
    ]
    for copy in copies:
        copy.start()
    for copy in copies:
        copy.wait()
    keys = [(i, p) for i in range(rows) for p in range(2)]
    for side in range(2):
        for i, p in keys:
            b_ref[side, i, p] = full_ref[side, i, pl.ds(p, count, stride=2), :]
    scale = {(i, p): spread(table_ref, p, i) for i, p in keys}
    level = {(i, p): spread(table_ref, p, rows + i) for i, p in keys}
    b = {(i, p): b_ref[half, i, p] for i, p in keys}
    u0 = {k: scale[k] * b[k] for k in keys}
    n0 = near(u0, range(rows), None, None, top)
    w1 = {k: level[k] * b[k] - scale[k] * n0[k] for k in keys}
    for i, p in keys:
        w1_ref[i, p] = w1[i, p]
    u1 = {k: scale[k] * w1[k] for k in keys}
    inside = [(i, p) for i, p in keys if 0 < i < top]
    n1 = near(u1, range(1, top), None, None, top)
    w2 = {k: level[k] * w1[k] - scale[k] * n1[k] for k in inside}
    for i, p in inside:
        w2_ref[i, p] = w2[i, p]
    mu = [
        total([b[k] * b[k] for k in keys]),
        total([b[k] * w1[k] for k in inside]),
        total([w1[k] * w1[k] for k in inside]),
        total([w1[k] * w2[k] for k in inside]),
        total([w2[k] * w2[k] for k in inside]),
    ]
    mu_ref[...] = jnp.concatenate(mu + [jnp.zeros_like(mu[0])] * 3, axis=0)
    order = inside + [k for k in keys if k not in inside]
    left = jnp.concatenate([jnp.concatenate([b_ref[0, i, p], b_ref[1, i, p]], axis=1) for i, p in order], axis=0)
    left_hi, left_lo = (x.T for x in split(left))
    own_hi, own_lo = split(jnp.concatenate([b[k] for k in order], axis=0))
    depth = len(inside) * count
    in_hi, in_lo = split(
        jnp.concatenate([jnp.concatenate([w1[k], w2[k]], axis=1) for k in inside], axis=0)
    )
    gram_ref[:, :LANES] = triple(left_hi, left_lo, own_hi, own_lo)
    gram_ref[:, LANES:] = triple(left_hi[:, :depth], left_lo[:, :depth], in_hi, in_lo)
    left_hi_ref[...] = left_hi[:, depth:]
    left_lo_ref[...] = left_lo[:, depth:]


def triple(left_hi, left_lo, right_hi, right_lo):
    def product(left, right):
        return jnp.dot(left, right, preferred_element_type=F32)

    return product(left_hi, right_hi) + (product(left_hi, right_lo) + product(left_lo, right_hi))


def outer_kernel(
    parts, b_ref, w1_ref, w2_ref, mu_in_ref, gram_ref, left_hi_ref, left_lo_ref, table_ref, below_ref, above_ref, *refs
):
    chunk_refs, (w_ref, far_ref, tile_ref) = refs[:parts], refs[parts:]
    _, rows, _, count, _ = b_ref.shape
    sites = 2 * count
    top = rows - 1
    half = lax.rem(lax.axis_index("quad"), 2)
    mine = lax.axis_index("rows")
    tail = 2 * rows
    for slot, (ref, blocks) in enumerate(((below_ref, 2), (above_ref, 3))):
        for part in range(sites // LANES):
            far_ref[slot, pl.ds(part * LANES, LANES), :tail] = ref[pl.ds(blocks * count + part * tail, tail), :].T

    def block(ref, index):
        return ref[pl.ds(index * count, count), :]

    outside = [(i, p) for i in (0, top) for p in range(2)]
    keys = [(i, p) for i in range(rows) for p in range(2)]
    used = [(i, p) for i in sorted({0, 1, top - 1, top}) for p in range(2)]
    scale = {(i, p): spread(table_ref, p, i) for i, p in keys}
    level = {(i, p): spread(table_ref, p, rows + i) for i, p in keys}
    b = {k: b_ref[half, k[0], k[1]] for k in outside}
    w1 = {k: w1_ref[k[0], k[1]] for k in keys}
    w2 = {k: w2_ref[k[0], k[1]] for k in keys if k not in outside}
    below0 = [block(below_ref, p) for p in range(2)]
    above0 = [block(above_ref, p) for p in range(2)]
    above_next = block(above_ref, 2)
    w1[0, 1] = w1[0, 1] - scale[0, 1] * below0[1]
    w1[top, 1] = w1[top, 1] - scale[top, 1] * above0[1]
    u1 = {k: scale[k] * w1[k] for k in used}
    edge = {k: scale[k] * b[k] for k in ((0, 1), (top, 1))}

    far_table = far_ref.at[0]
    scale_below = spread(far_table, 1, top)
    level_below = spread(far_table, 1, rows + top)
    sums = horizontal(below0[0], below0[1])
    below1 = level_below * below0[1] - scale_below * scale_below * (sums[1] + edge[0, 1])
    far_table = far_ref.at[1]
    square_above = [spread(far_table, p, 0) for p in range(2)]
    square_above = [x * x for x in square_above]
    level_above = [spread(far_table, p, rows) for p in range(2)]
    sums = horizontal(above0[0], above0[1])
    above1 = [
        level_above[0] * above0[0] - square_above[0] * (sums[0] + above_next),
        level_above[1] * above0[1] - square_above[1] * (sums[1] + edge[top, 1]),
    ]
    n1 = near(u1, (0, top), above1[1], below1, top)
    for k in outside:
        w2[k] = level[k] * w1[k] - scale[k] * n1[k]
    u2 = {k: scale[k] * w2[k] for k in keys}
    sums = horizontal(above1[0], above1[1])
    above2 = level_above[1] * above1[1] - square_above[1] * (sums[1] + u1[top, 1])
    n2 = near(u2, range(rows), 2.0 * above2, None, top)

    mu = [
        total([b[k] * w1[k] for k in outside]),
        total([w1[k] * w1[k] for k in outside]),
        total([w1[k] * w2[k] for k in outside]),
        total([w2[k] * w2[k] for k in outside]),
        total([level[k] * w2[k] * w2[k] - u2[k] * n2[k] for k in keys]),
    ]
    zero = jnp.zeros_like(mu[0])
    mu = mu_in_ref[...] + jnp.concatenate([zero] + mu + [zero] * 2, axis=0)
    for i, p in keys:
        w_ref[0, i, p] = w1[i, p]
        w_ref[1, i, p] = w2[i, p]
    right_hi, right_lo = split(
        jnp.concatenate([jnp.concatenate([w1[k], w2[k]], axis=1) for k in outside], axis=0)
    )
    more = triple(left_hi_ref[...], left_lo_ref[...], right_hi, right_lo)
    row = lax.broadcasted_iota(jnp.int32, (LANES, LANES), 0)
    lane = lax.broadcasted_iota(jnp.int32, (LANES, LANES), 1)
    for j in range(3):
        lanes = slice(j * LANES, (j + 1) * LANES)
        first, second = gram_ref[:LANES, lanes], gram_ref[LANES:, lanes]
        if j:
            lanes = slice((j - 1) * LANES, j * LANES)
            first, second = first + more[:LANES, lanes], second + more[LANES:, lanes]
        own = jnp.where(half == 0, first, second)
        cross = jnp.where(half == 0, second, first)
        tile_ref[pl.ds(j * LANES, LANES), :] = jnp.where(row < lane, own, cross)
    size = 3 * LANES // parts
    for part, ref in enumerate(chunk_refs):
        start = pl.multiple_of((mine ^ part) * size if parts > 1 else 0, 8)
        ref[pl.ds(0, size), :] = tile_ref[pl.ds(start, size), :]
        ref[pl.ds(size, 8), :] = mu


def moments_kernel(points, b_ref, w_ref, v_ref, mu_ref, nu_ref, out_ref, coef_ref, made_ref, out_sem):
    quad = lax.axis_index("quad")
    half = lax.rem(quad, 2)
    _, rows, _, count, _ = b_ref.shape
    first = jnp.where(half == 0, mu_ref[...], nu_ref[...])
    second = jnp.where(half == 0, nu_ref[...], mu_ref[...])
    mu = jnp.concatenate([first, second], axis=1)
    coefs = coefficients([mu[n : n + 1] for n in range(6)], points, (quad + 1).astype(F32))
    lines = [line for part in coefs for line in part]
    coef_ref[...] = jnp.concatenate(lines + [jnp.zeros_like(lines[0])] * 2, axis=0)
    stores = []
    for i in range(rows):
        for side in range(2):
            lanes = slice(side * LANES, (side + 1) * LANES)
            for p in range(2):
                fields = [b_ref[side, i, p]]
                fields += [jnp.where(half == side, w_ref[j, i, p], v_ref[j, i, p]) for j in range(2)]
                for part in range(2):
                    terms = [lines[3 * part + j][:, lanes] * fields[j] for j in range(3)]
                    made_ref[part, i, side, pl.ds(p, count, stride=2), :] = terms[0] + terms[1] + terms[2]
            for part in range(2):
                copy = pltpu.make_async_copy(
                    made_ref.at[part, i, side],
                    out_ref.at[0, part, i, :, pl.ds(side * LANES, LANES)],
                    out_sem.at[part, i, side],
                )
                copy.start()
                stores.append(copy)
    for copy in stores:
        copy.wait()


def reduced_kernel(parts, orbitals, coef_ref, mu_ref, nu_ref, *refs):
    own_refs, far_refs, (out_ref, own_tile, far_tile) = refs[:parts], refs[parts : 2 * parts], refs[2 * parts :]
    half = lax.rem(lax.axis_index("quad"), 2)
    mine = lax.axis_index("rows")
    size = 3 * LANES // parts
    for tile, chunk_refs in ((own_tile, own_refs), (far_tile, far_refs)):
        for part, ref in enumerate(chunk_refs):
            start = pl.multiple_of((mine ^ part) * size if parts > 1 else 0, 8)
            tile[pl.ds(start, size), :] = ref[pl.ds(0, size), :]
    row = lax.broadcasted_iota(jnp.int32, (LANES, LANES), 0)
    lane = lax.broadcasted_iota(jnp.int32, (LANES, LANES), 1)
    own_mu = mu_ref[...]
    far_mu = nu_ref[...]
    sums = {}
    for j in range(3):
        at = pl.ds(j * LANES, LANES)
        t0 = jnp.where(half == 0, own_tile[at, :], far_tile[at, :])
        t1 = jnp.where(half == 0, far_tile[at, :], own_tile[at, :])
        d0 = jnp.where(half == 0, own_mu[j : j + 1], far_mu[j : j + 1])
        d1 = jnp.where(half == 0, far_mu[j : j + 1], own_mu[j : j + 1])
        f0, f1 = t0.T, t1.T
        blocks = {
            (0, 0): jnp.where(row < lane, t0, jnp.where(row > lane, f0, d0)),
            (1, 1): jnp.where(row < lane, t1, jnp.where(row > lane, f1, d1)),
            (1, 0): jnp.where(row >= lane, t0, f1),
            (0, 1): jnp.where(row <= lane, f0, t1),
        }
        for (x, y), value in blocks.items():
            for part in range(2):
                coef = coef_ref[3 * part + j : 3 * part + j + 1, y * LANES : (y + 1) * LANES] * F32(1.0 / orbitals)
                term = coef * value
                sums[part, x, y] = term if j == 0 else sums[part, x, y] + term
    for (part, x, y), value in sums.items():
        out_ref[0, part, x * LANES : (x + 1) * LANES, y * LANES : (y + 1) * LANES] = value


def struct(*shape, dtype=F32):
    return jax.ShapeDtypeStruct(shape, dtype)


def cost(flops, nbytes):
    return pl.CostEstimate(flops=flops, bytes_accessed=nbytes, transcendentals=0)


def body(sources, onsite, strain, present):
    n_rows = lax.axis_size("rows")
    n_quad = lax.axis_size("quad")
    points = PTS_DEV * n_quad
    rows, sites, columns = sources.shape
    count = sites // 2
    orbitals = rows * sites * n_rows
    tail = 2 * rows * (sites // LANES)
    up, down, table = pl.pallas_call(
        edges_kernel,
        out_shape=(struct(2 * count + tail, LANES), struct(3 * count + tail, LANES), struct(sites, LANES)),
        in_specs=[HBM] * 4,
        out_specs=(VMEM, VMEM, VMEM),
        scratch_shapes=[
            pltpu.VMEM((3, sites, LANES), F32),
            pltpu.VMEM((rows, sites), F32),
            pltpu.VMEM((rows, sites), F32),
            pltpu.VMEM((rows, sites), jnp.int32),
            pltpu.SemaphoreType.DMA((6,)),
        ],
        compiler_params=PARAMS,
        name="edges",
    )(sources, onsite, strain, present)
    below = lax.ppermute(up, "rows", [(i, i + 1) for i in range(n_rows - 1)])
    above = lax.ppermute(down, "rows", [(i + 1, i) for i in range(n_rows - 1)])
    outer_depth = 4 * count
    inner = pl.pallas_call(
        inner_kernel,
        out_shape=(
            struct(2, rows, 2, count, LANES),
            struct(rows, 2, count, LANES),
            struct(rows, 2, count, LANES),
            struct(8, LANES),
            struct(columns, 3 * LANES),
            struct(columns, outer_depth, dtype=BF16),
            struct(columns, outer_depth, dtype=BF16),
        ),
        in_specs=[ANY, VMEM],
        out_specs=(VMEM,) * 7,
        scratch_shapes=[pltpu.VMEM((2, rows, sites, LANES), F32), pltpu.SemaphoreType.DMA((2,))],
        compiler_params=PARAMS,
        cost_estimate=cost(10**9, 8 * 2**20),
        name="inner",
    )(sources, table)
    b_all = inner[0]

    pairwise = n_rows & (n_rows - 1) == 0 and (3 * LANES) % (8 * n_rows) == 0
    parts = n_rows if pairwise else 1
    size = 3 * LANES // parts
    *chunks, fields = pl.pallas_call(
        functools.partial(outer_kernel, parts),
        out_shape=(struct(size + 8, LANES),) * parts + (struct(2, rows, 2, count, LANES),),
        in_specs=[VMEM] * 10,
        out_specs=(VMEM,) * (parts + 1),
        scratch_shapes=[pltpu.VMEM((2, sites, LANES), F32), pltpu.VMEM((3 * LANES, LANES), F32)],
        compiler_params=PARAMS,
        cost_estimate=cost(4 * 10**8, 4 * 2**20),
        name="outer",
    )(*inner, table, below, above)

    def partner(value):
        return lax.ppermute(value, "quad", [(i, i ^ 1) for i in range(n_quad)])

    def across(value, mask):
        return lax.ppermute(value, "rows", [(i, i ^ mask) for i in range(n_rows)])

    far_fields = partner(fields)
    if pairwise:
        summed = chunks[0]
        for mask in range(1, n_rows):
            summed = summed + across(chunks[mask], mask)
        sums = [summed[:size]] + [across(summed[:size], mask) for mask in range(1, n_rows)]
    else:
        summed = lax.psum(chunks[0], "rows")
        sums = [summed[:size]]
    mu = summed[size:]
    far_mu = partner(mu)
    far_sums = [partner(value) for value in sums]
    moments, coefs = pl.pallas_call(
        functools.partial(moments_kernel, points),
        out_shape=(struct(1, 2, rows, sites, columns), struct(8, columns)),
        in_specs=[VMEM] * 5,
        out_specs=(ANY, VMEM),
        scratch_shapes=[pltpu.VMEM((2, rows, 2, sites, LANES), F32), pltpu.SemaphoreType.DMA((2, rows, 2))],
        compiler_params=PARAMS,
        cost_estimate=cost(10**7, 8 * 2**20),
        name="moments",
    )(b_all, fields, far_fields, mu, far_mu)
    reduced = pl.pallas_call(
        functools.partial(reduced_kernel, parts, orbitals),
        out_shape=struct(1, 2, columns, columns),
        in_specs=[VMEM] * (3 + 2 * parts),
        out_specs=VMEM,
        scratch_shapes=[pltpu.VMEM((3 * LANES, LANES), F32), pltpu.VMEM((3 * LANES, LANES), F32)],
        compiler_params=PARAMS,
        cost_estimate=cost(10**6, 2**20),
        name="reduced",
    )(coefs, mu, far_mu, *sums, *far_sums)
    return moments, reduced


def solution(mesh):
    in_specs = (
        P(("groups", "rows"), None, None),
        P(("groups", "rows"), None),
        P(("groups", "rows"), None),
        P(("groups", "rows"), None),
    )
    out_specs = (P("quad", None, ("groups", "rows"), None, None), P("quad", None, "groups", None))
    return jax.shard_map(body, mesh=mesh, in_specs=in_specs, out_specs=out_specs, check_vma=False)
```

```python
import functools
import math

import jax
import jax.numpy as jnp
from jax import lax
from jax.experimental import pallas as pl
from jax.experimental.pallas import tpu as pltpu
from jax.sharding import PartitionSpec as P

TOTAL_PTS = 32
PTS_DEV = 2
CENTER = 0.4
RADIUS = 1.0
BOUND = 13.0
LANES = 128
F32 = jnp.float32
BF16 = jnp.bfloat16
PARAMS = pltpu.CompilerParams(vmem_limit_bytes=32 * 1024 * 1024)
VMEM = pl.BlockSpec(memory_space=pltpu.VMEM)
HBM = pl.BlockSpec(memory_space=pltpu.HBM)
ANY = pl.BlockSpec(memory_space=pl.ANY)


def ratio(top, bottom, good):
    return jnp.where(good, top / jnp.where(good, bottom, 1.0), 0.0)


def cmul(a, b):
    return (a[0] * b[0] - a[1] * b[1], a[0] * b[1] + a[1] * b[0])


def inverse(a):
    size = a[0] * a[0] + a[1] * a[1]
    return (a[0] / size, -a[1] / size)


def coefficients(mu, points, order):
    m0, m1, m2, m3, m4, m5 = mu
    tiny = F32(1e-7)
    ok0 = m0 > 0
    a0 = jnp.clip(ratio(m1, m0, ok0), -BOUND, BOUND)
    s11 = m2 - a0 * m1
    s12 = m3 - a0 * m2
    s13 = m4 - a0 * m3
    s14 = m5 - a0 * m4
    ok1 = ok0 & (s11 > tiny * m2)
    b1 = jnp.maximum(ratio(s11, m0, ok1), 0.0)
    g1 = ratio(s12, s11, ok1)
    a1 = jnp.clip(g1 - a0, -BOUND, BOUND)
    s22 = s13 - a1 * s12 - b1 * m2
    s23 = s14 - a1 * s13 - b1 * m3
    ok2 = ok1 & (s22 > tiny * m4)
    b2 = jnp.maximum(ratio(s22, s11, ok2), 0.0)
    a2 = jnp.clip(ratio(s23, s22, ok2) - g1, -BOUND, BOUND)
    leading = TOTAL_PTS // 4 - points // 2
    p = lax.broadcasted_iota(jnp.int32, (points, m0.shape[1]), 0).astype(F32)
    angle = 2.0 * math.pi * (p + leading + 0.5) / TOTAL_PTS
    zr = CENTER + RADIUS * jnp.cos(angle)
    zi = RADIUS * jnp.sin(angle)
    wr = RADIUS / points * jnp.cos(order * angle)
    wi = RADIUS / points * jnp.sin(order * angle)
    i2 = inverse((zr - a2, zi))
    i1 = inverse((zr - a1 - b2 * i2[0], zi - b2 * i2[1]))
    y0 = inverse((zr - a0 - b1 * i1[0], zi - b1 * i1[1]))
    y0 = cmul((wr, wi), y0)
    y1 = cmul(y0, i1)
    y2 = cmul(y1, i2)
    out = []
    for part in range(2):
        t0, t1, t2 = (jnp.sum(y[part], axis=0, keepdims=True) for y in (y0, y1, y2))
        out.append((t0 - a0 * t1 + (a0 * a1 - b1) * t2, t1 - (a0 + a1) * t2, t2))
    return out


def spread(table_ref, parity, lane):
    half = table_ref.shape[0] // 2
    rows = table_ref[pl.ds(parity, half, stride=2), :]
    return jnp.broadcast_to(rows[:, lane : lane + 1], (half, LANES))


def horizontal(even, odd):
    size = even.shape[0]
    site = lax.broadcasted_iota(jnp.int32, even.shape, 0)
    left = jnp.where(site == 0, 0.0, pltpu.roll(odd, 1, 0))
    right = jnp.where(site == size - 1, 0.0, pltpu.roll(even, size - 1, 0))
    return odd + left, even + right


def site_table(onsite, strain, present):
    return jnp.concatenate([present.astype(F32) * strain, onsite], axis=0)


def bound_up(i, p):
    return (i + p) % 2 == 0


def fold(value):
    return jnp.sum(value.reshape(value.shape[0] // 8, 8, value.shape[1]), axis=0)


def total(terms):
    return jnp.sum(functools.reduce(jnp.add, [fold(term) for term in terms]), axis=0, keepdims=True)


def split(value):
    high = value.astype(BF16)
    return high, (value - high.astype(F32)).astype(BF16)


def edges_kernel(
    sources_ref, onsite_ref, strain_ref, present_ref, first_ref, second_ref, table_ref,
    rows_ref, onsite_in, strain_in, present_in, sem,
):
    rows, sites, _ = sources_ref.shape
    count = sites // 2
    columns = pl.ds(pl.multiple_of(lax.rem(lax.axis_index("quad"), 2) * LANES, LANES), LANES)
    pairs = [(onsite_ref, onsite_in), (strain_ref, strain_in), (present_ref, present_in)]
    for slot, row in enumerate((0, 1, rows - 1)):
        pairs.append((sources_ref.at[row, :, columns], rows_ref.at[slot]))
    copies = [pltpu.make_async_copy(src, dst, sem.at[k]) for k, (src, dst) in enumerate(pairs)]
    for copy in copies:
        copy.start()
    for copy in copies[:3]:
        copy.wait()
    table = site_table(onsite_in[...], strain_in[...], present_in[...])
    tail = table.shape[0]
    table_ref[:, :tail] = table.T
    for part in range(sites // LANES):
        at = pl.ds(3 * count + part * tail, tail)
        first_ref[at, :] = second_ref[at, :] = table[:, part * LANES : (part + 1) * LANES]
    for copy in copies[3:]:
        copy.wait()

    def scaled(slot, row, parity):
        return rows_ref[slot, pl.ds(parity, count, stride=2), :] * spread(table_ref, parity, row)

    up = [scaled(2, rows - 1, 0), scaled(2, rows - 1, 1)]
    down = [scaled(0, 0, 0), scaled(0, 0, 1), scaled(1, 1, 0)]
    even = lax.rem(lax.axis_index("rows"), 2) == 0
    for block in range(3):
        at = pl.ds(block * count, count)
        first_ref[at, :] = jnp.where(even, up[min(block, 1)], down[block])
        second_ref[at, :] = jnp.where(even, down[block], up[min(block, 1)])


def near(u, wanted, up_halo, down_halo, top):
    out = {}
    for i in wanted:
        sums = horizontal(u[i, 0], u[i, 1])
        for p in range(2):
            if bound_up(i, p):
                other = u[i + 1, p] if i < top else up_halo
            else:
                other = u[i - 1, p] if i > 0 else down_halo
            out[i, p] = sums[p] if other is None else sums[p] + other
    return out


def inner_kernel(sources_ref, table_ref, b_ref, w1_ref, w2_ref, mu_ref, gram_ref, left_hi_ref, left_lo_ref, full_ref, sem):
    rows, sites, _ = sources_ref.shape
    count = sites // 2
    top = rows - 1
    half = lax.rem(lax.axis_index("quad"), 2)
    copies = [
        pltpu.make_async_copy(sources_ref.at[:, :, pl.ds(side * LANES, LANES)], full_ref.at[side], sem.at[side])
        for side in range(2)
    ]
    for copy in copies:
        copy.start()
    for copy in copies:
        copy.wait()
    keys = [(i, p) for i in range(rows) for p in range(2)]
    for side in range(2):
        for i, p in keys:
            b_ref[side, i, p] = full_ref[side, i, pl.ds(p, count, stride=2), :]
    scale = {(i, p): spread(table_ref, p, i) for i, p in keys}
    level = {(i, p): spread(table_ref, p, rows + i) for i, p in keys}
    b = {(i, p): b_ref[half, i, p] for i, p in keys}
    u0 = {k: scale[k] * b[k] for k in keys}
    n0 = near(u0, range(rows), None, None, top)
    w1 = {k: level[k] * b[k] - scale[k] * n0[k] for k in keys}
    for i, p in keys:
        w1_ref[i, p] = w1[i, p]
    u1 = {k: scale[k] * w1[k] for k in keys}
    inside = [(i, p) for i, p in keys if 0 < i < top]
    n1 = near(u1, range(1, top), None, None, top)
    w2 = {k: level[k] * w1[k] - scale[k] * n1[k] for k in inside}
    for i, p in inside:
        w2_ref[i, p] = w2[i, p]
    mu = [
        total([b[k] * b[k] for k in keys]),
        total([b[k] * w1[k] for k in inside]),
        total([w1[k] * w1[k] for k in inside]),
        total([w1[k] * w2[k] for k in inside]),
        total([w2[k] * w2[k] for k in inside]),
    ]
    mu_ref[...] = jnp.concatenate(mu + [jnp.zeros_like(mu[0])] * 3, axis=0)
    order = inside + [k for k in keys if k not in inside]
    left = jnp.concatenate([jnp.concatenate([b_ref[0, i, p], b_ref[1, i, p]], axis=1) for i, p in order], axis=0)
    left_hi, left_lo = (x.T for x in split(left))
    own_hi, own_lo = split(jnp.concatenate([b[k] for k in order], axis=0))
    depth = len(inside) * count
    in_hi, in_lo = split(
        jnp.concatenate([jnp.concatenate([w1[k], w2[k]], axis=1) for k in inside], axis=0)
    )
    gram_ref[:, :LANES] = triple(left_hi, left_lo, own_hi, own_lo)
    gram_ref[:, LANES:] = triple(left_hi[:, :depth], left_lo[:, :depth], in_hi, in_lo)
    left_hi_ref[...] = left_hi[:, depth:]
    left_lo_ref[...] = left_lo[:, depth:]


def triple(left_hi, left_lo, right_hi, right_lo):
    def product(left, right):
        return jnp.dot(left, right, preferred_element_type=F32)

    return product(left_hi, right_hi) + (product(left_hi, right_lo) + product(left_lo, right_hi))


def outer_kernel(
    parts, b_ref, w1_ref, w2_ref, mu_in_ref, gram_ref, left_hi_ref, left_lo_ref, table_ref, first_ref, second_ref, *refs
):
    chunk_refs, (w_ref, far_ref, tile_ref) = refs[:parts], refs[parts:]
    _, rows, _, count, _ = b_ref.shape
    sites = 2 * count
    top = rows - 1
    half = lax.rem(lax.axis_index("quad"), 2)
    mine = lax.axis_index("rows")
    tail = 2 * rows
    even = lax.rem(mine, 2) == 0

    def arrived(start, size):
        one, two = first_ref[pl.ds(start, size), :], second_ref[pl.ds(start, size), :]
        return jnp.where(even, two, one), jnp.where(even, one, two)

    for part in range(sites // LANES):
        for slot, value in enumerate(arrived(3 * count + part * tail, tail)):
            far_ref[slot, pl.ds(part * LANES, LANES), :tail] = value.T

    outside = [(i, p) for i in (0, top) for p in range(2)]
    keys = [(i, p) for i in range(rows) for p in range(2)]
    used = [(i, p) for i in sorted({0, 1, top - 1, top}) for p in range(2)]
    scale = {(i, p): spread(table_ref, p, i) for i, p in keys}
    level = {(i, p): spread(table_ref, p, rows + i) for i, p in keys}
    b = {k: b_ref[half, k[0], k[1]] for k in outside}
    w1 = {k: w1_ref[k[0], k[1]] for k in keys}
    w2 = {k: w2_ref[k[0], k[1]] for k in keys if k not in outside}
    below0, above0 = zip(arrived(0, count), arrived(count, count))
    above_next = arrived(2 * count, count)[1]
    w1[0, 1] = w1[0, 1] - scale[0, 1] * below0[1]
    w1[top, 1] = w1[top, 1] - scale[top, 1] * above0[1]
    u1 = {k: scale[k] * w1[k] for k in used}
    edge = {k: scale[k] * b[k] for k in ((0, 1), (top, 1))}

    far_table = far_ref.at[0]
    scale_below = spread(far_table, 1, top)
    level_below = spread(far_table, 1, rows + top)
    sums = horizontal(below0[0], below0[1])
    below1 = level_below * below0[1] - scale_below * scale_below * (sums[1] + edge[0, 1])
    far_table = far_ref.at[1]
    square_above = [spread(far_table, p, 0) for p in range(2)]
    square_above = [x * x for x in square_above]
    level_above = [spread(far_table, p, rows) for p in range(2)]
    sums = horizontal(above0[0], above0[1])
    above1 = [
        level_above[0] * above0[0] - square_above[0] * (sums[0] + above_next),
        level_above[1] * above0[1] - square_above[1] * (sums[1] + edge[top, 1]),
    ]
    n1 = near(u1, (0, top), above1[1], below1, top)
    for k in outside:
        w2[k] = level[k] * w1[k] - scale[k] * n1[k]
    u2 = {k: scale[k] * w2[k] for k in keys}
    sums = horizontal(above1[0], above1[1])
    above2 = level_above[1] * above1[1] - square_above[1] * (sums[1] + u1[top, 1])
    n2 = near(u2, range(rows), 2.0 * above2, None, top)

    mu = [
        total([b[k] * w1[k] for k in outside]),
        total([w1[k] * w1[k] for k in outside]),
        total([w1[k] * w2[k] for k in outside]),
        total([w2[k] * w2[k] for k in outside]),
        total([level[k] * w2[k] * w2[k] - u2[k] * n2[k] for k in keys]),
    ]
    zero = jnp.zeros_like(mu[0])
    mu = mu_in_ref[...] + jnp.concatenate([zero] + mu + [zero] * 2, axis=0)
    for i, p in keys:
        w_ref[0, i, p] = w1[i, p]
        w_ref[1, i, p] = w2[i, p]
    right_hi, right_lo = split(
        jnp.concatenate([jnp.concatenate([w1[k], w2[k]], axis=1) for k in outside], axis=0)
    )
    more = triple(left_hi_ref[...], left_lo_ref[...], right_hi, right_lo)
    row = lax.broadcasted_iota(jnp.int32, (LANES, LANES), 0)
    lane = lax.broadcasted_iota(jnp.int32, (LANES, LANES), 1)
    for j in range(3):
        lanes = slice(j * LANES, (j + 1) * LANES)
        first, second = gram_ref[:LANES, lanes], gram_ref[LANES:, lanes]
        if j:
            lanes = slice((j - 1) * LANES, j * LANES)
            first, second = first + more[:LANES, lanes], second + more[LANES:, lanes]
        own = jnp.where(half == 0, first, second)
        cross = jnp.where(half == 0, second, first)
        tile_ref[pl.ds(j * LANES, LANES), :] = jnp.where(row < lane, own, cross)
    size = 3 * LANES // parts
    for part, ref in enumerate(chunk_refs):
        start = pl.multiple_of((mine ^ part) * size if parts > 1 else 0, 8)
        ref[pl.ds(0, size), :] = tile_ref[pl.ds(start, size), :]
        ref[pl.ds(size, 8), :] = mu


def moments_kernel(points, b_ref, w_ref, v_ref, mu_ref, nu_ref, out_ref, coef_ref, made_ref, out_sem):
    quad = lax.axis_index("quad")
    half = lax.rem(quad, 2)
    _, rows, _, count, _ = b_ref.shape
    first = jnp.where(half == 0, mu_ref[...], nu_ref[...])
    second = jnp.where(half == 0, nu_ref[...], mu_ref[...])
    mu = jnp.concatenate([first, second], axis=1)
    coefs = coefficients([mu[n : n + 1] for n in range(6)], points, (quad + 1).astype(F32))
    lines = [line for part in coefs for line in part]
    coef_ref[...] = jnp.concatenate(lines + [jnp.zeros_like(lines[0])] * 2, axis=0)
    stores = []
    for i in range(rows):
        for side in range(2):
            lanes = slice(side * LANES, (side + 1) * LANES)
            for p in range(2):
                fields = [b_ref[side, i, p]]
                fields += [jnp.where(half == side, w_ref[j, i, p], v_ref[j, i, p]) for j in range(2)]
                for part in range(2):
                    terms = [lines[3 * part + j][:, lanes] * fields[j] for j in range(3)]
                    made_ref[part, i, side, pl.ds(p, count, stride=2), :] = terms[0] + terms[1] + terms[2]
            for part in range(2):
                copy = pltpu.make_async_copy(
                    made_ref.at[part, i, side],
                    out_ref.at[0, part, i, :, pl.ds(side * LANES, LANES)],
                    out_sem.at[part, i, side],
                )
                copy.start()
                stores.append(copy)
    for copy in stores:
        copy.wait()


def reduced_kernel(parts, orbitals, coef_ref, mu_ref, nu_ref, *refs):
    own_refs, far_refs, (out_ref, own_tile, far_tile) = refs[:parts], refs[parts : 2 * parts], refs[2 * parts :]
    half = lax.rem(lax.axis_index("quad"), 2)
    mine = lax.axis_index("rows")
    size = 3 * LANES // parts
    for tile, chunk_refs in ((own_tile, own_refs), (far_tile, far_refs)):
        for part, ref in zip([0, *range(parts - 1, 0, -1)], chunk_refs):
            start = pl.multiple_of((mine ^ part) * size if parts > 1 else 0, 8)
            tile[pl.ds(start, size), :] = ref[pl.ds(0, size), :]
    row = lax.broadcasted_iota(jnp.int32, (LANES, LANES), 0)
    lane = lax.broadcasted_iota(jnp.int32, (LANES, LANES), 1)
    own_mu = mu_ref[...]
    far_mu = nu_ref[...]
    sums = {}
    for j in range(3):
        at = pl.ds(j * LANES, LANES)
        t0 = jnp.where(half == 0, own_tile[at, :], far_tile[at, :])
        t1 = jnp.where(half == 0, far_tile[at, :], own_tile[at, :])
        d0 = jnp.where(half == 0, own_mu[j : j + 1], far_mu[j : j + 1])
        d1 = jnp.where(half == 0, far_mu[j : j + 1], own_mu[j : j + 1])
        f0, f1 = t0.T, t1.T
        blocks = {
            (0, 0): jnp.where(row < lane, t0, jnp.where(row > lane, f0, d0)),
            (1, 1): jnp.where(row < lane, t1, jnp.where(row > lane, f1, d1)),
            (1, 0): jnp.where(row >= lane, t0, f1),
            (0, 1): jnp.where(row <= lane, f0, t1),
        }
        for (x, y), value in blocks.items():
            for part in range(2):
                coef = coef_ref[3 * part + j : 3 * part + j + 1, y * LANES : (y + 1) * LANES] * F32(1.0 / orbitals)
                term = coef * value
                sums[part, x, y] = term if j == 0 else sums[part, x, y] + term
    for (part, x, y), value in sums.items():
        out_ref[0, part, x * LANES : (x + 1) * LANES, y * LANES : (y + 1) * LANES] = value


def struct(*shape, dtype=F32):
    return jax.ShapeDtypeStruct(shape, dtype)


def cost(flops, nbytes):
    return pl.CostEstimate(flops=flops, bytes_accessed=nbytes, transcendentals=0)


def body(sources, onsite, strain, present):
    n_rows = lax.axis_size("rows")
    n_quad = lax.axis_size("quad")
    points = PTS_DEV * n_quad
    rows, sites, columns = sources.shape
    count = sites // 2
    orbitals = rows * sites * n_rows
    tail = 2 * rows * (sites // LANES)
    first, second, table = pl.pallas_call(
        edges_kernel,
        out_shape=(struct(3 * count + tail, LANES), struct(3 * count + tail, LANES), struct(sites, LANES)),
        in_specs=[HBM] * 4,
        out_specs=(VMEM, VMEM, VMEM),
        scratch_shapes=[
            pltpu.VMEM((3, sites, LANES), F32),
            pltpu.VMEM((rows, sites), F32),
            pltpu.VMEM((rows, sites), F32),
            pltpu.VMEM((rows, sites), jnp.int32),
            pltpu.SemaphoreType.DMA((6,)),
        ],
        compiler_params=PARAMS,
        name="edges",
    )(*(pltpu.with_memory_space_constraint(x, pltpu.HBM) for x in (sources, onsite, strain, present)))
    halo = []
    for value, start in ((first, 0), (second, 1)):
        bonds = [(i, i + 1) for i in range(start, n_rows - 1, 2)]
        halo.append(lax.ppermute(value, "rows", bonds + [(j, i) for i, j in bonds]))
    outer_depth = 4 * count
    inner = pl.pallas_call(
        inner_kernel,
        out_shape=(
            struct(2, rows, 2, count, LANES),
            struct(rows, 2, count, LANES),
            struct(rows, 2, count, LANES),
            struct(8, LANES),
            struct(columns, 3 * LANES),
            struct(columns, outer_depth, dtype=BF16),
            struct(columns, outer_depth, dtype=BF16),
        ),
        in_specs=[ANY, VMEM],
        out_specs=(VMEM,) * 7,
        scratch_shapes=[pltpu.VMEM((2, rows, sites, LANES), F32), pltpu.SemaphoreType.DMA((2,))],
        compiler_params=PARAMS,
        cost_estimate=cost(10**9, 8 * 2**20),
        name="inner",
    )(sources, table)
    b_all = inner[0]

    pairwise = n_rows & (n_rows - 1) == 0 and (3 * LANES) % (8 * n_rows) == 0
    parts = n_rows if pairwise else 1
    far_first = list(range(parts - 1, 0, -1))
    size = 3 * LANES // parts
    *chunks, fields = pl.pallas_call(
        functools.partial(outer_kernel, parts),
        out_shape=(struct(size + 8, LANES),) * parts + (struct(2, rows, 2, count, LANES),),
        in_specs=[VMEM] * 10,
        out_specs=(VMEM,) * (parts + 1),
        scratch_shapes=[pltpu.VMEM((2, sites, LANES), F32), pltpu.VMEM((3 * LANES, LANES), F32)],
        compiler_params=PARAMS,
        cost_estimate=cost(4 * 10**8, 4 * 2**20),
        name="outer",
    )(*inner, table, *halo)

    def partner(value):
        return lax.ppermute(value, "quad", [(i, i ^ 1) for i in range(n_quad)])

    def across(value, mask):
        return lax.ppermute(value, "rows", [(i, i ^ mask) for i in range(n_rows)])

    far_fields = partner(fields)
    if pairwise:
        summed = chunks[0]
        for mask in far_first:
            summed = summed + across(chunks[mask], mask)
        sums = [summed[:size]] + [across(summed[:size], mask) for mask in far_first]
    else:
        summed = lax.psum(chunks[0], "rows")
        sums = [summed[:size]]
    far_summed = partner(summed)
    mu, far_mu = summed[size:], far_summed[size:]
    far_sums = [far_summed[:size]]
    moments, coefs = pl.pallas_call(
        functools.partial(moments_kernel, points),
        out_shape=(struct(1, 2, rows, sites, columns), struct(8, columns)),
        in_specs=[VMEM] * 5,
        out_specs=(ANY, VMEM),
        scratch_shapes=[pltpu.VMEM((2, rows, 2, sites, LANES), F32), pltpu.SemaphoreType.DMA((2, rows, 2))],
        compiler_params=PARAMS,
        cost_estimate=cost(10**7, 8 * 2**20),
        name="moments",
    )(b_all, fields, far_fields, mu, far_mu)
    *late, coefs = lax.optimization_barrier((*sums[2:], coefs))
    sums = sums[:2] + late
    far_sums += [partner(value) for value in sums[1:]]
    reduced = pl.pallas_call(
        functools.partial(reduced_kernel, parts, orbitals),
        out_shape=struct(1, 2, columns, columns),
        in_specs=[VMEM] * (3 + 2 * parts),
        out_specs=VMEM,
        scratch_shapes=[pltpu.VMEM((3 * LANES, LANES), F32), pltpu.VMEM((3 * LANES, LANES), F32)],
        compiler_params=PARAMS,
        cost_estimate=cost(10**6, 2**20),
        name="reduced",
    )(coefs, mu, far_mu, *sums, *far_sums)
    return moments, reduced


def solution(mesh):
    in_specs = (
        P(("groups", "rows"), None, None),
        P(("groups", "rows"), None),
        P(("groups", "rows"), None),
        P(("groups", "rows"), None),
    )
    out_specs = (P("quad", None, ("groups", "rows"), None, None), P("quad", None, "groups", None))
    return jax.shard_map(body, mesh=mesh, in_specs=in_specs, out_specs=out_specs, check_vma=False)
```

```python
import functools
import math

import jax
import jax.numpy as jnp
from jax import lax
from jax.experimental import pallas as pl
from jax.experimental.pallas import tpu as pltpu
from jax.sharding import PartitionSpec as P

TOTAL_PTS = 32
PTS_DEV = 2
CENTER = 0.4
RADIUS = 1.0
BOUND = 13.0
LANES = 128
F32 = jnp.float32
BF16 = jnp.bfloat16
PARAMS = pltpu.CompilerParams(vmem_limit_bytes=32 * 1024 * 1024)
VMEM = pl.BlockSpec(memory_space=pltpu.VMEM)
HBM = pl.BlockSpec(memory_space=pltpu.HBM)
ANY = pl.BlockSpec(memory_space=pl.ANY)


def ratio(top, bottom, good):
    return jnp.where(good, top / jnp.where(good, bottom, 1.0), 0.0)


def cmul(a, b):
    return (a[0] * b[0] - a[1] * b[1], a[0] * b[1] + a[1] * b[0])


def inverse(a):
    size = a[0] * a[0] + a[1] * a[1]
    return (a[0] / size, -a[1] / size)


def coefficients(mu, points, order):
    m0, m1, m2, m3, m4, m5 = mu
    tiny = F32(1e-7)
    ok0 = m0 > 0
    a0 = jnp.clip(ratio(m1, m0, ok0), -BOUND, BOUND)
    s11 = m2 - a0 * m1
    s12 = m3 - a0 * m2
    s13 = m4 - a0 * m3
    s14 = m5 - a0 * m4
    ok1 = ok0 & (s11 > tiny * m2)
    b1 = jnp.maximum(ratio(s11, m0, ok1), 0.0)
    g1 = ratio(s12, s11, ok1)
    a1 = jnp.clip(g1 - a0, -BOUND, BOUND)
    s22 = s13 - a1 * s12 - b1 * m2
    s23 = s14 - a1 * s13 - b1 * m3
    ok2 = ok1 & (s22 > tiny * m4)
    b2 = jnp.maximum(ratio(s22, s11, ok2), 0.0)
    a2 = jnp.clip(ratio(s23, s22, ok2) - g1, -BOUND, BOUND)
    leading = TOTAL_PTS // 4 - points // 2
    p = lax.broadcasted_iota(jnp.int32, (points, m0.shape[1]), 0).astype(F32)
    angle = 2.0 * math.pi * (p + leading + 0.5) / TOTAL_PTS
    zr = CENTER + RADIUS * jnp.cos(angle)
    zi = RADIUS * jnp.sin(angle)
    wr = RADIUS / points * jnp.cos(order * angle)
    wi = RADIUS / points * jnp.sin(order * angle)
    i2 = inverse((zr - a2, zi))
    i1 = inverse((zr - a1 - b2 * i2[0], zi - b2 * i2[1]))
    y0 = inverse((zr - a0 - b1 * i1[0], zi - b1 * i1[1]))
    y0 = cmul((wr, wi), y0)
    y1 = cmul(y0, i1)
    y2 = cmul(y1, i2)
    out = []
    for part in range(2):
        t0, t1, t2 = (jnp.sum(y[part], axis=0, keepdims=True) for y in (y0, y1, y2))
        out.append((t0 - a0 * t1 + (a0 * a1 - b1) * t2, t1 - (a0 + a1) * t2, t2))
    return out


def spread(table_ref, parity, lane):
    half = table_ref.shape[0] // 2
    rows = table_ref[pl.ds(parity, half, stride=2), :]
    return jnp.broadcast_to(rows[:, lane : lane + 1], (half, LANES))


def horizontal(even, odd):
    size = even.shape[0]
    site = lax.broadcasted_iota(jnp.int32, even.shape, 0)
    left = jnp.where(site == 0, 0.0, pltpu.roll(odd, 1, 0))
    right = jnp.where(site == size - 1, 0.0, pltpu.roll(even, size - 1, 0))
    return odd + left, even + right


def site_table(onsite, strain, present):
    return jnp.concatenate([present.astype(F32) * strain, onsite], axis=0)


def bound_up(i, p):
    return (i + p) % 2 == 0


def fold(value):
    return jnp.sum(value.reshape(value.shape[0] // 8, 8, value.shape[1]), axis=0)


def total(terms):
    return jnp.sum(functools.reduce(jnp.add, [fold(term) for term in terms]), axis=0, keepdims=True)


def split(value):
    high = value.astype(BF16)
    return high, (value - high.astype(F32)).astype(BF16)


def edges_kernel(
    sources_ref, onsite_ref, strain_ref, present_ref, first_ref, second_ref, table_ref,
    rows_ref, onsite_in, strain_in, present_in, sem,
):
    rows, sites, _ = sources_ref.shape
    count = sites // 2
    columns = pl.ds(pl.multiple_of(lax.rem(lax.axis_index("quad"), 2) * LANES, LANES), LANES)
    pairs = [(onsite_ref, onsite_in), (strain_ref, strain_in), (present_ref, present_in)]
    for slot, row in enumerate((0, 1, rows - 1, rows - 2)):
        pairs.append((sources_ref.at[row, :, columns], rows_ref.at[slot]))
    copies = [pltpu.make_async_copy(src, dst, sem.at[k]) for k, (src, dst) in enumerate(pairs)]
    for copy in copies:
        copy.start()
    for copy in copies[:3]:
        copy.wait()
    table = site_table(onsite_in[...], strain_in[...], present_in[...])
    tail = table.shape[0]
    table_ref[:, :tail] = table.T
    for part in range(sites // LANES):
        at = pl.ds(2 * count + shared(count) + part * tail, tail)
        first_ref[at, :] = second_ref[at, :] = table[:, part * LANES : (part + 1) * LANES]
    for copy in copies[3:]:
        copy.wait()

    def scaled(slot, row, parity):
        return rows_ref[slot, pl.ds(parity, count, stride=2), :] * spread(table_ref, parity, row)

    size = shared(count)
    up = [scaled(2, rows - 1, 0), scaled(2, rows - 1, 1), scaled(3, rows - 2, 0)[count - size :]]
    down = [scaled(0, 0, 0), scaled(0, 0, 1), scaled(1, 1, 0)[:size]]
    even = lax.rem(lax.axis_index("rows"), 2) == 0
    for block in range(3):
        at = pl.ds(block * count, up[block].shape[0])
        first_ref[at, :] = jnp.where(even, up[block], down[block])
        second_ref[at, :] = jnp.where(even, down[block], up[block])


def shared(count):
    return count // 2 + 8


def near(u, wanted, up_halo, down_halo, top):
    out = {}
    for i in wanted:
        sums = horizontal(u[i, 0], u[i, 1])
        for p in range(2):
            if bound_up(i, p):
                other = u[i + 1, p] if i < top else up_halo
            else:
                other = u[i - 1, p] if i > 0 else down_halo
            out[i, p] = sums[p] if other is None else sums[p] + other
    return out


def bonds(scale, w, wanted):
    u = {(i, p): scale[i, p] * w[i, p] for i in wanted for p in range(2)}
    out = {}
    for i in wanted:
        out[i, 0] = u[i, 0] * horizontal(u[i, 0], u[i, 1])[0]
        out[i, 1] = jnp.zeros_like(u[i, 1])
        for p in range(2):
            if bound_up(i, p) and (i + 1, p) in u:
                out[i, p] = out[i, p] + u[i, p] * u[i + 1, p]
    return out


def inner_kernel(sources_ref, table_ref, b_ref, w_ref, mu_ref, gram_ref, left_hi_ref, left_lo_ref, full_ref, sem):
    rows, sites, _ = sources_ref.shape
    count = sites // 2
    top = rows - 1
    half = lax.rem(lax.axis_index("quad"), 2)
    copies = [
        pltpu.make_async_copy(sources_ref.at[:, :, pl.ds(side * LANES, LANES)], full_ref.at[side], sem.at[side])
        for side in range(2)
    ]
    for copy in copies:
        copy.start()
    for copy in copies:
        copy.wait()
    keys = [(i, p) for i in range(rows) for p in range(2)]
    for side in range(2):
        for i, p in keys:
            b_ref[side, i, p] = full_ref[side, i, pl.ds(p, count, stride=2), :]
    scale = {(i, p): spread(table_ref, p, i) for i, p in keys}
    level = {(i, p): spread(table_ref, p, rows + i) for i, p in keys}
    b = {(i, p): b_ref[half, i, p] for i, p in keys}
    u0 = {k: scale[k] * b[k] for k in keys}
    n0 = near(u0, range(rows), None, None, top)
    w1 = {k: level[k] * b[k] - scale[k] * n0[k] for k in keys}
    for i, p in keys:
        w_ref[0, i, p] = w1[i, p]
    u1 = {k: scale[k] * w1[k] for k in keys}
    inside = [(i, p) for i, p in keys if 0 < i < top]
    n1 = near(u1, range(1, top), None, None, top)
    w2 = {k: level[k] * w1[k] - scale[k] * n1[k] for k in inside}
    for i, p in inside:
        w_ref[1, i, p] = w2[i, p]
    mu = [
        total([b[k] * b[k] for k in keys]),
        total([b[k] * w1[k] for k in inside]),
        total([w1[k] * w1[k] for k in inside]),
        total([w1[k] * w2[k] for k in inside]),
        total([w2[k] * w2[k] for k in inside]),
        total([level[k] * w2[k] * w2[k] - 2.0 * x for k, x in bonds(scale, w2, range(1, top)).items()]),
    ]
    mu_ref[...] = jnp.concatenate(mu + [jnp.zeros_like(mu[0])] * 2, axis=0)
    order = inside + [k for k in keys if k not in inside]
    left = jnp.concatenate([jnp.concatenate([b_ref[0, i, p], b_ref[1, i, p]], axis=1) for i, p in order], axis=0)
    left_hi, left_lo = (x.T for x in split(left))
    own_hi, own_lo = split(jnp.concatenate([b[k] for k in order], axis=0))
    depth = len(inside) * count
    in_hi, in_lo = split(
        jnp.concatenate([jnp.concatenate([w1[k], w2[k]], axis=1) for k in inside], axis=0)
    )
    gram_ref[:, :LANES] = triple(left_hi, left_lo, own_hi, own_lo)
    gram_ref[:, LANES:] = triple(left_hi[:, :depth], left_lo[:, :depth], in_hi, in_lo)
    left_hi_ref[...] = left_hi[:, depth:]
    left_lo_ref[...] = left_lo[:, depth:]


def triple(left_hi, left_lo, right_hi, right_lo):
    def product(left, right):
        return jnp.dot(left, right, preferred_element_type=F32)

    return product(left_hi, right_hi) + (product(left_hi, right_lo) + product(left_lo, right_hi))


def outer_kernel(
    parts, b_ref, w_in_ref, mu_in_ref, gram_ref, left_hi_ref, left_lo_ref, table_ref, first_ref, second_ref, *refs
):
    chunk_refs, (w_ref, far_ref, tile_ref) = refs[:parts], refs[parts:]
    _, rows, _, count, _ = b_ref.shape
    sites = 2 * count
    top = rows - 1
    half = lax.rem(lax.axis_index("quad"), 2)
    mine = lax.axis_index("rows")
    tail = 2 * rows
    even = lax.rem(mine, 2) == 0
    size = shared(count)

    def arrived(start, size):
        one, two = first_ref[pl.ds(start, size), :], second_ref[pl.ds(start, size), :]
        return jnp.where(even, two, one), jnp.where(even, one, two)

    for part in range(sites // LANES):
        for slot, value in enumerate(arrived(2 * count + size + part * tail, tail)):
            far_ref[slot, pl.ds(part * LANES, LANES), :tail] = value.T

    outside = [(i, p) for i in (0, top) for p in range(2)]
    scale = {(i, p): spread(table_ref, p, i) for i, p in outside}
    level = {(i, p): spread(table_ref, p, rows + i) for i, p in outside}
    b = {k: b_ref[half, k[0], k[1]] for k in outside}
    w1 = {k: w_in_ref[0, k[0], k[1]] for k in outside}
    below0, above0 = zip(arrived(0, count), arrived(count, count))
    w1[0, 1] = w1[0, 1] - scale[0, 1] * below0[1]
    w1[top, 1] = w1[top, 1] - scale[top, 1] * above0[1]
    u1 = {k: scale[k] * w1[k] for k in outside}
    beside = {0: (1, 0), top: (top - 1, 0)}
    beside_scale = {i: spread(table_ref, 0, k[0]) for i, k in beside.items()}

    missing = jnp.zeros((count - size, LANES), F32)
    low, high = arrived(2 * count, size)
    edge_next = {0: jnp.concatenate([missing, low], axis=0), top: jnp.concatenate([high, missing], axis=0)}
    edge_w2, far_w2 = {}, {}
    for i, halo, slot, row in ((0, below0, 0, top), (top, above0, 1, 0)):
        far_table = far_ref.at[slot]
        square = [spread(far_table, p, row) for p in range(2)]
        square = [x * x for x in square]
        far_level = [spread(far_table, p, rows + row) for p in range(2)]
        sums = horizontal(halo[0], halo[1])
        far1 = [
            far_level[0] * halo[0] - square[0] * (sums[0] + edge_next[i]),
            far_level[1] * halo[1] - square[1] * (sums[1] + scale[i, 1] * b[i, 1]),
        ]
        sums = horizontal(u1[i, 0], u1[i, 1])
        k = beside[i]
        edge_w2[i, 0] = level[i, 0] * w1[i, 0] - scale[i, 0] * (sums[0] + beside_scale[i] * w_in_ref[0, k[0], k[1]])
        edge_w2[i, 1] = level[i, 1] * w1[i, 1] - scale[i, 1] * (sums[1] + far1[1])
        sums = horizontal(far1[0], far1[1])
        far_w2[i] = far_level[1] * far1[1] - square[1] * (sums[1] + u1[i, 1])
    w2 = edge_w2
    site = lax.broadcasted_iota(jnp.int32, (count, LANES), 0)
    counted = {0: site >= count // 2, top: site < count // 2}
    pairs = bonds(scale, w2, (0,))
    pairs.update(bonds(scale, w2, (top,)))
    for i in (0, top):
        k = beside[i]
        inner_w2 = w_in_ref[1, k[0], k[1]]
        pairs[i, 0] = pairs[i, 0] + scale[i, 0] * w2[i, 0] * (beside_scale[i] * inner_w2)
        pairs[i, 1] = pairs[i, 1] + scale[i, 1] * w2[i, 1] * jnp.where(counted[i], far_w2[i], 0.0)

    mu = [
        total([b[k] * w1[k] for k in outside]),
        total([w1[k] * w1[k] for k in outside]),
        total([w1[k] * w2[k] for k in outside]),
        total([w2[k] * w2[k] for k in outside]),
        total([level[k] * w2[k] * w2[k] - 2.0 * pairs[k] for k in outside]),
    ]
    zero = jnp.zeros_like(mu[0])
    mu = mu_in_ref[...] + jnp.concatenate([zero] + mu + [zero] * 2, axis=0)
    for i, p in outside:
        w_ref[0, i, p] = w1[i, p]
        w_ref[1, i, p] = w2[i, p]
    right_hi, right_lo = split(
        jnp.concatenate([jnp.concatenate([w1[k], w2[k]], axis=1) for k in outside], axis=0)
    )
    more = triple(left_hi_ref[...], left_lo_ref[...], right_hi, right_lo)
    row = lax.broadcasted_iota(jnp.int32, (LANES, LANES), 0)
    lane = lax.broadcasted_iota(jnp.int32, (LANES, LANES), 1)
    for j in range(3):
        lanes = slice(j * LANES, (j + 1) * LANES)
        first, second = gram_ref[:LANES, lanes], gram_ref[LANES:, lanes]
        if j:
            lanes = slice((j - 1) * LANES, j * LANES)
            first, second = first + more[:LANES, lanes], second + more[LANES:, lanes]
        own = jnp.where(half == 0, first, second)
        cross = jnp.where(half == 0, second, first)
        tile_ref[pl.ds(j * LANES, LANES), :] = jnp.where(row < lane, own, cross)
    size = 3 * LANES // parts
    for part, ref in enumerate(chunk_refs):
        start = pl.multiple_of((mine ^ part) * size if parts > 1 else 0, 8)
        ref[pl.ds(0, size), :] = tile_ref[pl.ds(start, size), :]
        ref[pl.ds(size, 8), :] = mu


def moments_kernel(points, b_ref, w_ref, v_ref, mu_ref, nu_ref, out_ref, coef_ref, made_ref, out_sem):
    quad = lax.axis_index("quad")
    half = lax.rem(quad, 2)
    _, rows, _, count, _ = b_ref.shape
    first = jnp.where(half == 0, mu_ref[...], nu_ref[...])
    second = jnp.where(half == 0, nu_ref[...], mu_ref[...])
    mu = jnp.concatenate([first, second], axis=1)
    coefs = coefficients([mu[n : n + 1] for n in range(6)], points, (quad + 1).astype(F32))
    lines = [line for part in coefs for line in part]
    coef_ref[...] = jnp.concatenate(lines + [jnp.zeros_like(lines[0])] * 2, axis=0)
    stores = []
    for i in range(rows):
        for side in range(2):
            lanes = slice(side * LANES, (side + 1) * LANES)
            for p in range(2):
                fields = [b_ref[side, i, p]]
                fields += [jnp.where(half == side, w_ref[j, i, p], v_ref[j, i, p]) for j in range(2)]
                for part in range(2):
                    terms = [lines[3 * part + j][:, lanes] * fields[j] for j in range(3)]
                    made_ref[part, i, side, pl.ds(p, count, stride=2), :] = terms[0] + terms[1] + terms[2]
            for part in range(2):
                copy = pltpu.make_async_copy(
                    made_ref.at[part, i, side],
                    out_ref.at[0, part, i, :, pl.ds(side * LANES, LANES)],
                    out_sem.at[part, i, side],
                )
                copy.start()
                stores.append(copy)
    for copy in stores:
        copy.wait()


def reduced_kernel(parts, orbitals, coef_ref, mu_ref, nu_ref, *refs):
    own_refs, far_refs, (out_ref, own_tile, far_tile) = refs[:parts], refs[parts : 2 * parts], refs[2 * parts :]
    half = lax.rem(lax.axis_index("quad"), 2)
    mine = lax.axis_index("rows")
    size = 3 * LANES // parts
    for tile, chunk_refs in ((own_tile, own_refs), (far_tile, far_refs)):
        for part, ref in zip([0, *range(parts - 1, 0, -1)], chunk_refs):
            start = pl.multiple_of((mine ^ part) * size if parts > 1 else 0, 8)
            tile[pl.ds(start, size), :] = ref[pl.ds(0, size), :]
    row = lax.broadcasted_iota(jnp.int32, (LANES, LANES), 0)
    lane = lax.broadcasted_iota(jnp.int32, (LANES, LANES), 1)
    own_mu = mu_ref[...]
    far_mu = nu_ref[...]
    sums = {}
    for j in range(3):
        at = pl.ds(j * LANES, LANES)
        t0 = jnp.where(half == 0, own_tile[at, :], far_tile[at, :])
        t1 = jnp.where(half == 0, far_tile[at, :], own_tile[at, :])
        d0 = jnp.where(half == 0, own_mu[j : j + 1], far_mu[j : j + 1])
        d1 = jnp.where(half == 0, far_mu[j : j + 1], own_mu[j : j + 1])
        f0, f1 = t0.T, t1.T
        blocks = {
            (0, 0): jnp.where(row < lane, t0, jnp.where(row > lane, f0, d0)),
            (1, 1): jnp.where(row < lane, t1, jnp.where(row > lane, f1, d1)),
            (1, 0): jnp.where(row >= lane, t0, f1),
            (0, 1): jnp.where(row <= lane, f0, t1),
        }
        for (x, y), value in blocks.items():
            for part in range(2):
                coef = coef_ref[3 * part + j : 3 * part + j + 1, y * LANES : (y + 1) * LANES] * F32(1.0 / orbitals)
                term = coef * value
                sums[part, x, y] = term if j == 0 else sums[part, x, y] + term
    for (part, x, y), value in sums.items():
        out_ref[0, part, x * LANES : (x + 1) * LANES, y * LANES : (y + 1) * LANES] = value


def struct(*shape, dtype=F32):
    return jax.ShapeDtypeStruct(shape, dtype)


def cost(flops, nbytes):
    return pl.CostEstimate(flops=flops, bytes_accessed=nbytes, transcendentals=0)


def body(sources, onsite, strain, present):
    n_rows = lax.axis_size("rows")
    n_quad = lax.axis_size("quad")
    points = PTS_DEV * n_quad
    rows, sites, columns = sources.shape
    count = sites // 2
    orbitals = rows * sites * n_rows
    tail = 2 * rows * (sites // LANES)
    payload = 2 * count + shared(count) + tail
    first, second, table = pl.pallas_call(
        edges_kernel,
        out_shape=(struct(payload, LANES), struct(payload, LANES), struct(sites, LANES)),
        in_specs=[HBM] * 4,
        out_specs=(VMEM, VMEM, VMEM),
        scratch_shapes=[
            pltpu.VMEM((4, sites, LANES), F32),
            pltpu.VMEM((rows, sites), F32),
            pltpu.VMEM((rows, sites), F32),
            pltpu.VMEM((rows, sites), jnp.int32),
            pltpu.SemaphoreType.DMA((7,)),
        ],
        compiler_params=PARAMS,
        name="edges",
    )(*(pltpu.with_memory_space_constraint(x, pltpu.HBM) for x in (sources, onsite, strain, present)))
    halo = []
    for value, start in ((first, 0), (second, 1)):
        bonds = [(i, i + 1) for i in range(start, n_rows - 1, 2)]
        halo.append(lax.ppermute(value, "rows", bonds + [(j, i) for i, j in bonds]))
    outer_depth = 4 * count
    inner = pl.pallas_call(
        inner_kernel,
        out_shape=(
            struct(2, rows, 2, count, LANES),
            struct(2, rows, 2, count, LANES),
            struct(8, LANES),
            struct(columns, 3 * LANES),
            struct(columns, outer_depth, dtype=BF16),
            struct(columns, outer_depth, dtype=BF16),
        ),
        in_specs=[ANY, VMEM],
        out_specs=(VMEM,) * 6,
        scratch_shapes=[pltpu.VMEM((2, rows, sites, LANES), F32), pltpu.SemaphoreType.DMA((2,))],
        compiler_params=PARAMS,
        cost_estimate=cost(10**9, 8 * 2**20),
        name="inner",
    )(sources, table)
    b_all = inner[0]

    pairwise = n_rows & (n_rows - 1) == 0 and (3 * LANES) % (8 * n_rows) == 0
    parts = n_rows if pairwise else 1
    far_first = list(range(parts - 1, 0, -1))
    size = 3 * LANES // parts
    *chunks, fields = pl.pallas_call(
        functools.partial(outer_kernel, parts),
        out_shape=(struct(size + 8, LANES),) * parts + (struct(2, rows, 2, count, LANES),),
        in_specs=[VMEM] * 9,
        out_specs=(VMEM,) * (parts + 1),
        input_output_aliases={1: parts},
        scratch_shapes=[pltpu.VMEM((2, sites, LANES), F32), pltpu.VMEM((3 * LANES, LANES), F32)],
        compiler_params=PARAMS,
        cost_estimate=cost(4 * 10**8, 4 * 2**20),
        name="outer",
    )(*inner, table, *halo)

    def partner(value):
        return lax.ppermute(value, "quad", [(i, i ^ 1) for i in range(n_quad)])

    def across(value, mask):
        return lax.ppermute(value, "rows", [(i, i ^ mask) for i in range(n_rows)])

    far_fields = partner(fields)
    if pairwise:
        summed = chunks[0]
        for mask in far_first:
            summed = summed + across(chunks[mask], mask)
        sums = [summed[:size]] + [across(summed[:size], mask) for mask in far_first]
    else:
        summed = lax.psum(chunks[0], "rows")
        sums = [summed[:size]]
    far_summed = partner(summed)
    mu, far_mu = summed[size:], far_summed[size:]
    far_sums = [far_summed[:size]]
    moments, coefs = pl.pallas_call(
        functools.partial(moments_kernel, points),
        out_shape=(struct(1, 2, rows, sites, columns), struct(8, columns)),
        in_specs=[VMEM] * 5,
        out_specs=(ANY, VMEM),
        scratch_shapes=[pltpu.VMEM((2, rows, 2, sites, LANES), F32), pltpu.SemaphoreType.DMA((2, rows, 2))],
        compiler_params=PARAMS,
        cost_estimate=cost(10**7, 8 * 2**20),
        name="moments",
    )(b_all, fields, far_fields, mu, far_mu)
    *late, coefs = lax.optimization_barrier((*sums[2:], coefs))
    sums = sums[:2] + late
    far_sums += [partner(value) for value in sums[1:]]
    reduced = pl.pallas_call(
        functools.partial(reduced_kernel, parts, orbitals),
        out_shape=struct(1, 2, columns, columns),
        in_specs=[VMEM] * (3 + 2 * parts),
        out_specs=VMEM,
        scratch_shapes=[pltpu.VMEM((3 * LANES, LANES), F32), pltpu.VMEM((3 * LANES, LANES), F32)],
        compiler_params=PARAMS,
        cost_estimate=cost(10**6, 2**20),
        name="reduced",
    )(coefs, mu, far_mu, *sums, *far_sums)
    return moments, reduced


def solution(mesh):
    in_specs = (
        P(("groups", "rows"), None, None),
        P(("groups", "rows"), None),
        P(("groups", "rows"), None),
        P(("groups", "rows"), None),
    )
    out_specs = (P("quad", None, ("groups", "rows"), None, None), P("quad", None, "groups", None))
    return jax.shard_map(body, mesh=mesh, in_specs=in_specs, out_specs=out_specs, check_vma=False)
```

```python
import functools
import math

import jax
import jax.numpy as jnp
from jax import lax
from jax.experimental import pallas as pl
from jax.experimental.pallas import tpu as pltpu
from jax.sharding import PartitionSpec as P

TOTAL_PTS = 32
PTS_DEV = 2
CENTER = 0.4
RADIUS = 1.0
BOUND = 13.0
LANES = 128
F32 = jnp.float32
BF16 = jnp.bfloat16
PARAMS = pltpu.CompilerParams(vmem_limit_bytes=32 * 1024 * 1024)
VMEM = pl.BlockSpec(memory_space=pltpu.VMEM)
HBM = pl.BlockSpec(memory_space=pltpu.HBM)
ANY = pl.BlockSpec(memory_space=pl.ANY)


def ratio(top, bottom, good):
    return jnp.where(good, top / jnp.where(good, bottom, 1.0), 0.0)


def cmul(a, b):
    return (a[0] * b[0] - a[1] * b[1], a[0] * b[1] + a[1] * b[0])


def inverse(a):
    size = a[0] * a[0] + a[1] * a[1]
    return (a[0] / size, -a[1] / size)


def coefficients(mu, points, order):
    m0, m1, m2, m3, m4, m5 = mu
    tiny = F32(1e-7)
    ok0 = m0 > 0
    a0 = jnp.clip(ratio(m1, m0, ok0), -BOUND, BOUND)
    s11 = m2 - a0 * m1
    s12 = m3 - a0 * m2
    s13 = m4 - a0 * m3
    s14 = m5 - a0 * m4
    ok1 = ok0 & (s11 > tiny * m2)
    b1 = jnp.maximum(ratio(s11, m0, ok1), 0.0)
    g1 = ratio(s12, s11, ok1)
    a1 = jnp.clip(g1 - a0, -BOUND, BOUND)
    s22 = s13 - a1 * s12 - b1 * m2
    s23 = s14 - a1 * s13 - b1 * m3
    ok2 = ok1 & (s22 > tiny * m4)
    b2 = jnp.maximum(ratio(s22, s11, ok2), 0.0)
    a2 = jnp.clip(ratio(s23, s22, ok2) - g1, -BOUND, BOUND)
    leading = TOTAL_PTS // 4 - points // 2
    p = lax.broadcasted_iota(jnp.int32, (points, m0.shape[1]), 0).astype(F32)
    angle = 2.0 * math.pi * (p + leading + 0.5) / TOTAL_PTS
    zr = CENTER + RADIUS * jnp.cos(angle)
    zi = RADIUS * jnp.sin(angle)
    wr = RADIUS / points * jnp.cos(order * angle)
    wi = RADIUS / points * jnp.sin(order * angle)
    i2 = inverse((zr - a2, zi))
    i1 = inverse((zr - a1 - b2 * i2[0], zi - b2 * i2[1]))
    y0 = inverse((zr - a0 - b1 * i1[0], zi - b1 * i1[1]))
    y0 = cmul((wr, wi), y0)
    y1 = cmul(y0, i1)
    y2 = cmul(y1, i2)
    out = []
    for part in range(2):
        t0, t1, t2 = (jnp.sum(y[part], axis=0, keepdims=True) for y in (y0, y1, y2))
        out.append((t0 - a0 * t1 + (a0 * a1 - b1) * t2, t1 - (a0 + a1) * t2, t2))
    return out


def spread(table_ref, parity, lane):
    half = table_ref.shape[0] // 2
    rows = table_ref[pl.ds(parity, half, stride=2), :]
    return jnp.broadcast_to(rows[:, lane : lane + 1], (half, LANES))


def horizontal(even, odd):
    size = even.shape[0]
    site = lax.broadcasted_iota(jnp.int32, even.shape, 0)
    left = jnp.where(site == 0, 0.0, pltpu.roll(odd, 1, 0))
    right = jnp.where(site == size - 1, 0.0, pltpu.roll(even, size - 1, 0))
    return odd + left, even + right


def site_table(onsite, strain, present):
    return jnp.concatenate([present.astype(F32) * strain, onsite], axis=0)


def bound_up(i, p):
    return (i + p) % 2 == 0


def fold(value):
    return jnp.sum(value.reshape(value.shape[0] // 8, 8, value.shape[1]), axis=0)


def total(terms):
    return jnp.sum(functools.reduce(jnp.add, [fold(term) for term in terms]), axis=0, keepdims=True)


def split(value):
    high = value.astype(BF16)
    return high, (value - high.astype(F32)).astype(BF16)


def edges_kernel(
    sources_ref, onsite_ref, strain_ref, present_ref, first_ref, second_ref, table_ref,
    rows_ref, onsite_in, strain_in, present_in, sem,
):
    rows, sites, _ = sources_ref.shape
    count = sites // 2
    columns = pl.ds(pl.multiple_of(lax.rem(lax.axis_index("quad"), 2) * LANES, LANES), LANES)
    pairs = [(onsite_ref, onsite_in), (strain_ref, strain_in), (present_ref, present_in)]
    for slot, row in enumerate((0, 1, rows - 1, rows - 2)):
        pairs.append((sources_ref.at[row, :, columns], rows_ref.at[slot]))
    copies = [pltpu.make_async_copy(src, dst, sem.at[k]) for k, (src, dst) in enumerate(pairs)]
    for copy in copies:
        copy.start()
    for copy in copies[:3]:
        copy.wait()
    table = site_table(onsite_in[...], strain_in[...], present_in[...])
    tail = table.shape[0]
    table_ref[:, :tail] = table.T
    for part in range(sites // LANES):
        at = pl.ds(2 * count + shared(count) + part * tail, tail)
        first_ref[at, :] = second_ref[at, :] = table[:, part * LANES : (part + 1) * LANES]
    for copy in copies[3:]:
        copy.wait()

    def scaled(slot, row, parity):
        return rows_ref[slot, pl.ds(parity, count, stride=2), :] * spread(table_ref, parity, row)

    size = shared(count)
    up = [scaled(2, rows - 1, 0), scaled(2, rows - 1, 1), scaled(3, rows - 2, 0)[count - size :]]
    down = [scaled(0, 0, 0), scaled(0, 0, 1), scaled(1, 1, 0)[:size]]
    even = lax.rem(lax.axis_index("rows"), 2) == 0
    for block in range(3):
        at = pl.ds(block * count, up[block].shape[0])
        first_ref[at, :] = jnp.where(even, up[block], down[block])
        second_ref[at, :] = jnp.where(even, down[block], up[block])


def shared(count):
    return count // 2 + 8


def near(u, wanted, up_halo, down_halo, top):
    out = {}
    for i in wanted:
        sums = horizontal(u[i, 0], u[i, 1])
        for p in range(2):
            if bound_up(i, p):
                other = u[i + 1, p] if i < top else up_halo
            else:
                other = u[i - 1, p] if i > 0 else down_halo
            out[i, p] = sums[p] if other is None else sums[p] + other
    return out


def bonds(scale, w, wanted):
    u = {(i, p): scale[i, p] * w[i, p] for i in wanted for p in range(2)}
    out = {}
    for i in wanted:
        out[i, 0] = u[i, 0] * horizontal(u[i, 0], u[i, 1])[0]
        out[i, 1] = jnp.zeros_like(u[i, 1])
        for p in range(2):
            if bound_up(i, p) and (i + 1, p) in u:
                out[i, p] = out[i, p] + u[i, p] * u[i + 1, p]
    return out


def beside(i, top):
    return (1, 0) if i == 0 else (top - 1, 0)


def inner_kernel(sources_ref, table_ref, b_ref, w_ref, aid_ref, mu_ref, gram_ref, left_hi_ref, left_lo_ref, full_ref, sem):
    rows, sites, _ = sources_ref.shape
    count = sites // 2
    top = rows - 1
    half = lax.rem(lax.axis_index("quad"), 2)
    copies = [
        pltpu.make_async_copy(sources_ref.at[:, :, pl.ds(side * LANES, LANES)], full_ref.at[side], sem.at[side])
        for side in range(2)
    ]
    for copy in copies:
        copy.start()
    for copy in copies:
        copy.wait()
    keys = [(i, p) for i in range(rows) for p in range(2)]
    for side in range(2):
        for i, p in keys:
            b_ref[side, i, p] = full_ref[side, i, pl.ds(p, count, stride=2), :]
    scale = {(i, p): spread(table_ref, p, i) for i, p in keys}
    level = {(i, p): spread(table_ref, p, rows + i) for i, p in keys}
    b = {(i, p): b_ref[half, i, p] for i, p in keys}
    u0 = {k: scale[k] * b[k] for k in keys}
    n0 = near(u0, range(rows), None, None, top)
    w1 = {k: level[k] * b[k] - scale[k] * n0[k] for k in keys}
    for i, p in keys:
        w_ref[0, i, p] = w1[i, p]
    u1 = {k: scale[k] * w1[k] for k in keys}
    inside = [(i, p) for i, p in keys if 0 < i < top]
    n1 = near(u1, range(1, top), None, None, top)
    w2 = {k: level[k] * w1[k] - scale[k] * n1[k] for k in inside}
    for i, p in inside:
        w_ref[1, i, p] = w2[i, p]
    for index, i in enumerate((0, top)):
        for p in range(2):
            aid_ref[index, p] = scale[i, p]
            aid_ref[index, 2 + p] = level[i, p]
        k = beside(i, top)
        aid_ref[index, 4] = u0[i, 1]
        aid_ref[index, 5] = u1[k]
        aid_ref[index, 6] = scale[k] * w2[k]
    mu = [
        total([b[k] * b[k] for k in keys]),
        total([b[k] * w1[k] for k in inside]),
        total([w1[k] * w1[k] for k in inside]),
        total([w1[k] * w2[k] for k in inside]),
        total([w2[k] * w2[k] for k in inside]),
        total([level[k] * w2[k] * w2[k] - 2.0 * x for k, x in bonds(scale, w2, range(1, top)).items()]),
    ]
    mu_ref[...] = jnp.concatenate(mu + [jnp.zeros_like(mu[0])] * 2, axis=0)
    order = inside + [k for k in keys if k not in inside]
    left = jnp.concatenate([jnp.concatenate([b_ref[0, i, p], b_ref[1, i, p]], axis=1) for i, p in order], axis=0)
    left_hi, left_lo = (x.T for x in split(left))
    own_hi, own_lo = split(jnp.concatenate([b[k] for k in order], axis=0))
    depth = len(inside) * count
    in_hi, in_lo = split(
        jnp.concatenate([jnp.concatenate([w1[k], w2[k]], axis=1) for k in inside], axis=0)
    )
    gram_ref[:, :LANES] = triple(left_hi, left_lo, own_hi, own_lo)
    gram_ref[:, LANES:] = triple(left_hi[:, :depth], left_lo[:, :depth], in_hi, in_lo)
    left_hi_ref[...] = left_hi[:, depth:]
    left_lo_ref[...] = left_lo[:, depth:]


def triple(left_hi, left_lo, right_hi, right_lo):
    def product(left, right):
        return jnp.dot(left, right, preferred_element_type=F32)

    return product(left_hi, right_hi) + (product(left_hi, right_lo) + product(left_lo, right_hi))


def outer_kernel(
    parts, b_ref, w_in_ref, aid_ref, mu_in_ref, gram_ref, left_hi_ref, left_lo_ref, first_ref, second_ref, *refs
):
    chunk_refs, (w_ref, far_ref, tile_ref) = refs[:parts], refs[parts:]
    _, rows, _, count, _ = b_ref.shape
    sites = 2 * count
    top = rows - 1
    half = lax.rem(lax.axis_index("quad"), 2)
    mine = lax.axis_index("rows")
    tail = 2 * rows
    even = lax.rem(mine, 2) == 0
    size = shared(count)

    def arrived(start, size):
        one, two = first_ref[pl.ds(start, size), :], second_ref[pl.ds(start, size), :]
        return jnp.where(even, two, one), jnp.where(even, one, two)

    for part in range(sites // LANES):
        for slot, value in enumerate(arrived(2 * count + size + part * tail, tail)):
            far_ref[slot, pl.ds(part * LANES, LANES), :tail] = value.T

    outside = [(i, p) for i in (0, top) for p in range(2)]
    aid = {i: [aid_ref[index, n] for n in range(7)] for index, i in enumerate((0, top))}
    scale = {(i, p): aid[i][p] for i, p in outside}
    level = {(i, p): aid[i][2 + p] for i, p in outside}
    b = {k: b_ref[half, k[0], k[1]] for k in outside}
    w1 = {k: w_in_ref[0, k[0], k[1]] for k in outside}
    below0, above0 = zip(arrived(0, count), arrived(count, count))
    w1[0, 1] = w1[0, 1] - scale[0, 1] * below0[1]
    w1[top, 1] = w1[top, 1] - scale[top, 1] * above0[1]
    u1 = {k: scale[k] * w1[k] for k in outside}

    missing = jnp.zeros((count - size, LANES), F32)
    low, high = arrived(2 * count, size)
    edge_next = {0: jnp.concatenate([missing, low], axis=0), top: jnp.concatenate([high, missing], axis=0)}
    edge_w2, far_w2 = {}, {}
    for i, halo, slot, row in ((0, below0, 0, top), (top, above0, 1, 0)):
        far_table = far_ref.at[slot]
        square = [spread(far_table, p, row) for p in range(2)]
        square = [x * x for x in square]
        far_level = [spread(far_table, p, rows + row) for p in range(2)]
        sums = horizontal(halo[0], halo[1])
        far1 = [
            far_level[0] * halo[0] - square[0] * (sums[0] + edge_next[i]),
            far_level[1] * halo[1] - square[1] * (sums[1] + aid[i][4]),
        ]
        sums = horizontal(u1[i, 0], u1[i, 1])
        edge_w2[i, 0] = level[i, 0] * w1[i, 0] - scale[i, 0] * (sums[0] + aid[i][5])
        edge_w2[i, 1] = level[i, 1] * w1[i, 1] - scale[i, 1] * (sums[1] + far1[1])
        sums = horizontal(far1[0], far1[1])
        far_w2[i] = far_level[1] * far1[1] - square[1] * (sums[1] + u1[i, 1])
    w2 = edge_w2
    site = lax.broadcasted_iota(jnp.int32, (count, LANES), 0)
    counted = {0: site >= count // 2, top: site < count // 2}
    pairs = bonds(scale, w2, (0,))
    pairs.update(bonds(scale, w2, (top,)))
    for i in (0, top):
        pairs[i, 0] = pairs[i, 0] + scale[i, 0] * w2[i, 0] * aid[i][6]
        pairs[i, 1] = pairs[i, 1] + scale[i, 1] * w2[i, 1] * jnp.where(counted[i], far_w2[i], 0.0)

    mu = [
        total([b[k] * w1[k] for k in outside]),
        total([w1[k] * w1[k] for k in outside]),
        total([w1[k] * w2[k] for k in outside]),
        total([w2[k] * w2[k] for k in outside]),
        total([level[k] * w2[k] * w2[k] - 2.0 * pairs[k] for k in outside]),
    ]
    zero = jnp.zeros_like(mu[0])
    mu = mu_in_ref[...] + jnp.concatenate([zero] + mu + [zero] * 2, axis=0)
    for i, p in outside:
        w_ref[0, i, p] = w1[i, p]
        w_ref[1, i, p] = w2[i, p]
    right_hi, right_lo = split(
        jnp.concatenate([jnp.concatenate([w1[k], w2[k]], axis=1) for k in outside], axis=0)
    )
    more = triple(left_hi_ref[...], left_lo_ref[...], right_hi, right_lo)
    row = lax.broadcasted_iota(jnp.int32, (LANES, LANES), 0)
    lane = lax.broadcasted_iota(jnp.int32, (LANES, LANES), 1)
    for j in range(3):
        lanes = slice(j * LANES, (j + 1) * LANES)
        first, second = gram_ref[:LANES, lanes], gram_ref[LANES:, lanes]
        if j:
            lanes = slice((j - 1) * LANES, j * LANES)
            first, second = first + more[:LANES, lanes], second + more[LANES:, lanes]
        own = jnp.where(half == 0, first, second)
        cross = jnp.where(half == 0, second, first)
        tile_ref[pl.ds(j * LANES, LANES), :] = jnp.where(row < lane, own, cross)
    size = 3 * LANES // parts
    for part, ref in enumerate(chunk_refs):
        start = pl.multiple_of((mine ^ part) * size if parts > 1 else 0, 8)
        ref[pl.ds(0, size), :] = tile_ref[pl.ds(start, size), :]
        ref[pl.ds(size, 8), :] = mu


def moments_kernel(points, b_ref, w_ref, v_ref, mu_ref, nu_ref, out_ref, coef_ref, made_ref, out_sem):
    quad = lax.axis_index("quad")
    half = lax.rem(quad, 2)
    _, rows, _, count, _ = b_ref.shape
    first = jnp.where(half == 0, mu_ref[...], nu_ref[...])
    second = jnp.where(half == 0, nu_ref[...], mu_ref[...])
    mu = jnp.concatenate([first, second], axis=1)
    coefs = coefficients([mu[n : n + 1] for n in range(6)], points, (quad + 1).astype(F32))
    lines = [line for part in coefs for line in part]
    coef_ref[...] = jnp.concatenate(lines + [jnp.zeros_like(lines[0])] * 2, axis=0)
    stores = []
    for i in range(rows):
        for side in range(2):
            lanes = slice(side * LANES, (side + 1) * LANES)
            for p in range(2):
                fields = [b_ref[side, i, p]]
                fields += [jnp.where(half == side, w_ref[j, i, p], v_ref[j, i, p]) for j in range(2)]
                for part in range(2):
                    terms = [lines[3 * part + j][:, lanes] * fields[j] for j in range(3)]
                    made_ref[part, i, side, pl.ds(p, count, stride=2), :] = terms[0] + terms[1] + terms[2]
            for part in range(2):
                copy = pltpu.make_async_copy(
                    made_ref.at[part, i, side],
                    out_ref.at[0, part, i, :, pl.ds(side * LANES, LANES)],
                    out_sem.at[part, i, side],
                )
                copy.start()
                stores.append(copy)
    for copy in stores:
        copy.wait()


def tile_blocks(half, tile, mu):
    row = lax.broadcasted_iota(jnp.int32, (LANES, LANES), 0)
    lane = lax.broadcasted_iota(jnp.int32, (LANES, LANES), 1)
    flip = tile.T
    same = jnp.where(row < lane, tile, jnp.where(row > lane, flip, mu))
    below = jnp.where(half == 0, jnp.where(row >= lane, tile, 0.0), jnp.where(row < lane, flip, 0.0))
    above = jnp.where(half == 0, jnp.where(row <= lane, flip, 0.0), jnp.where(row > lane, tile, 0.0))
    return same, below, above


def gather(parts, tile_ref, chunk_refs):
    size = 3 * LANES // parts
    for part, ref in zip([0, *range(parts - 1, 0, -1)], chunk_refs):
        start = pl.multiple_of((lax.axis_index("rows") ^ part) * size if parts > 1 else 0, 8)
        tile_ref[pl.ds(start, size), :] = ref[pl.ds(0, size), :]


def weighted(parts, orbitals, half, coef_ref, mu_ref, tile_ref):
    sums = {}
    for j in range(3):
        blocks = tile_blocks(half, tile_ref[j * LANES : (j + 1) * LANES, :], mu_ref[j : j + 1, :])
        for part in range(2):
            line = coef_ref[3 * part + j : 3 * part + j + 1, :] * F32(1.0 / orbitals)
            first, second = line[:, :LANES], line[:, LANES:]
            own = jnp.where(half == 0, first, second)
            for which, (lane_coef, value) in enumerate(zip((own, first, second), blocks)):
                term = lane_coef * value
                sums[part, which] = term if j == 0 else sums[part, which] + term
    return sums


def own_kernel(parts, orbitals, coef_ref, mu_ref, *refs):
    chunk_refs, (out_ref, tile_ref) = refs[:parts], refs[parts:]
    half = lax.rem(lax.axis_index("quad"), 2)
    gather(parts, tile_ref, chunk_refs)
    for (part, which), value in weighted(parts, orbitals, half, coef_ref, mu_ref, tile_ref).items():
        out_ref[part, which] = value


def far_kernel(parts, orbitals, coef_ref, mu_ref, own_ref, *refs):
    chunk_refs, (out_ref, tile_ref, made_ref, sem) = refs[:parts], refs[parts:]
    half = lax.rem(lax.axis_index("quad"), 2)
    gather(parts, tile_ref, chunk_refs)
    sums = weighted(parts, orbitals, 1 - half, coef_ref, mu_ref, tile_ref)
    copies = []
    for part in range(2):
        same = [own_ref[part, 0], sums[part, 0]]
        blocks = {
            (0, 0): jnp.where(half == 0, same[0], same[1]),
            (0, 1): own_ref[part, 2] + sums[part, 2],
            (1, 0): own_ref[part, 1] + sums[part, 1],
            (1, 1): jnp.where(half == 0, same[1], same[0]),
        }
        for (x, y), value in blocks.items():
            made_ref[part, x * LANES : (x + 1) * LANES, y * LANES : (y + 1) * LANES] = value
        copies.append(pltpu.make_async_copy(made_ref.at[part], out_ref.at[0, part], sem.at[part]))
        copies[-1].start()
    for copy in copies:
        copy.wait()


def struct(*shape, dtype=F32):
    return jax.ShapeDtypeStruct(shape, dtype)


def cost(flops, nbytes):
    return pl.CostEstimate(flops=flops, bytes_accessed=nbytes, transcendentals=0)


def body(sources, onsite, strain, present):
    n_rows = lax.axis_size("rows")
    n_quad = lax.axis_size("quad")
    points = PTS_DEV * n_quad
    rows, sites, columns = sources.shape
    count = sites // 2
    orbitals = rows * sites * n_rows
    tail = 2 * rows * (sites // LANES)
    payload = 2 * count + shared(count) + tail
    first, second, table = pl.pallas_call(
        edges_kernel,
        out_shape=(struct(payload, LANES), struct(payload, LANES), struct(sites, LANES)),
        in_specs=[HBM] * 4,
        out_specs=(VMEM, VMEM, VMEM),
        scratch_shapes=[
            pltpu.VMEM((4, sites, LANES), F32),
            pltpu.VMEM((rows, sites), F32),
            pltpu.VMEM((rows, sites), F32),
            pltpu.VMEM((rows, sites), jnp.int32),
            pltpu.SemaphoreType.DMA((7,)),
        ],
        compiler_params=PARAMS,
        name="edges",
    )(*(pltpu.with_memory_space_constraint(x, pltpu.HBM) for x in (sources, onsite, strain, present)))
    halo = []
    for value, start in ((first, 0), (second, 1)):
        bonds = [(i, i + 1) for i in range(start, n_rows - 1, 2)]
        halo.append(lax.ppermute(value, "rows", bonds + [(j, i) for i, j in bonds]))
    outer_depth = 4 * count
    inner = pl.pallas_call(
        inner_kernel,
        out_shape=(
            struct(2, rows, 2, count, LANES),
            struct(2, rows, 2, count, LANES),
            struct(2, 7, count, LANES),
            struct(8, LANES),
            struct(columns, 3 * LANES),
            struct(columns, outer_depth, dtype=BF16),
            struct(columns, outer_depth, dtype=BF16),
        ),
        in_specs=[ANY, VMEM],
        out_specs=(VMEM,) * 7,
        scratch_shapes=[pltpu.VMEM((2, rows, sites, LANES), F32), pltpu.SemaphoreType.DMA((2,))],
        compiler_params=PARAMS,
        cost_estimate=cost(10**9, 8 * 2**20),
        name="inner",
    )(sources, table)
    b_all = inner[0]

    pairwise = n_rows & (n_rows - 1) == 0 and (3 * LANES) % (8 * n_rows) == 0
    parts = n_rows if pairwise else 1
    far_first = list(range(parts - 1, 0, -1))
    size = 3 * LANES // parts
    *chunks, fields = pl.pallas_call(
        functools.partial(outer_kernel, parts),
        out_shape=(struct(size + 8, LANES),) * parts + (struct(2, rows, 2, count, LANES),),
        in_specs=[VMEM] * 9,
        out_specs=(VMEM,) * (parts + 1),
        input_output_aliases={1: parts},
        scratch_shapes=[pltpu.VMEM((2, sites, LANES), F32), pltpu.VMEM((3 * LANES, LANES), F32)],
        compiler_params=PARAMS,
        cost_estimate=cost(4 * 10**8, 4 * 2**20),
        name="outer",
    )(*inner, *halo)

    def partner(value):
        return lax.ppermute(value, "quad", [(i, i ^ 1) for i in range(n_quad)])

    def across(value, mask):
        return lax.ppermute(value, "rows", [(i, i ^ mask) for i in range(n_rows)])

    if pairwise:
        summed = chunks[0]
        for mask in far_first:
            summed = summed + across(chunks[mask], mask)
        sums = [summed[:size]] + [across(summed[:size], mask) for mask in far_first]
    else:
        summed = lax.psum(chunks[0], "rows")
        sums = [summed[:size]]
    summed, fields = lax.optimization_barrier((summed, fields))
    far_summed = partner(summed)
    far_fields = partner(fields)
    mu, far_mu = summed[size:], far_summed[size:]
    far_sums = [far_summed[:size]]
    moments, coefs = pl.pallas_call(
        functools.partial(moments_kernel, points),
        out_shape=(struct(1, 2, rows, sites, columns), struct(8, columns)),
        in_specs=[VMEM] * 5,
        out_specs=(ANY, VMEM),
        scratch_shapes=[pltpu.VMEM((2, rows, 2, sites, LANES), F32), pltpu.SemaphoreType.DMA((2, rows, 2))],
        compiler_params=PARAMS,
        cost_estimate=cost(10**7, 8 * 2**20),
        name="moments",
    )(b_all, fields, far_fields, mu, far_mu)
    *late, coefs = lax.optimization_barrier((*sums[2:], coefs))
    sums = sums[:2] + late
    far_sums += [partner(value) for value in sums[1:]]
    own = pl.pallas_call(
        functools.partial(own_kernel, parts, orbitals),
        out_shape=struct(2, 3, LANES, LANES),
        in_specs=[VMEM] * (2 + parts),
        out_specs=VMEM,
        scratch_shapes=[pltpu.VMEM((3 * LANES, LANES), F32)],
        compiler_params=PARAMS,
        cost_estimate=cost(10**6, 2**20),
        name="own",
    )(coefs, mu, *sums)
    reduced = pl.pallas_call(
        functools.partial(far_kernel, parts, orbitals),
        out_shape=struct(1, 2, columns, columns),
        in_specs=[VMEM] * (3 + parts),
        out_specs=ANY,
        scratch_shapes=[
            pltpu.VMEM((3 * LANES, LANES), F32),
            pltpu.VMEM((2, columns, columns), F32),
            pltpu.SemaphoreType.DMA((2,)),
        ],
        compiler_params=PARAMS,
        cost_estimate=cost(10**6, 2**20),
        name="reduced",
    )(coefs, far_mu, own, *far_sums)
    return moments, reduced


def solution(mesh):
    in_specs = (
        P(("groups", "rows"), None, None),
        P(("groups", "rows"), None),
        P(("groups", "rows"), None),
        P(("groups", "rows"), None),
    )
    out_specs = (P("quad", None, ("groups", "rows"), None, None), P("quad", None, "groups", None))
    return jax.shard_map(body, mesh=mesh, in_specs=in_specs, out_specs=out_specs, check_vma=False)
```

```python
import functools
import math

import jax
import jax.numpy as jnp
from jax import lax
from jax.experimental import pallas as pl
from jax.experimental.pallas import tpu as pltpu
from jax.sharding import PartitionSpec as P

TOTAL_PTS = 32
PTS_DEV = 2
CENTER = 0.4
RADIUS = 1.0
MU_ROWS = 16
LANES = 128
LARGE = 1e30
F32 = jnp.float32
BF16 = jnp.bfloat16
PARAMS = pltpu.CompilerParams(vmem_limit_bytes=32 * 1024 * 1024)
VMEM = pl.BlockSpec(memory_space=pltpu.VMEM)
HBM = pl.BlockSpec(memory_space=pltpu.HBM)
ANY = pl.BlockSpec(memory_space=pl.ANY)


def ratio(top, bottom, good):
    return jnp.where(good, top / jnp.where(good, bottom, 1.0), 0.0)


def cmul(a, b):
    return (a[0] * b[0] - a[1] * b[1], a[0] * b[1] + a[1] * b[0])


def inverse(a):
    size = a[0] * a[0] + a[1] * a[1]
    return (a[0] / size, -a[1] / size)


def two_sum(a, b):
    total = a + b
    part = total - a
    return total, (a - (total - part)) + (b - part)


def pair_add(a, b):
    total, rest = two_sum(a[0], b[0])
    return two_sum(total, rest + (a[1] + b[1]))


def halves(a):
    scaled = F32(4097.0) * a
    high = scaled - (scaled - a)
    return high, a - high


def pair_times(a, b):
    product = a[0] * b
    (ah, al), (bh, bl) = halves(a[0]), halves(b)
    rest = ((ah * bh - product) + ah * bl + al * bh) + al * bl
    return two_sum(product, rest + a[1] * b)


def coefficients(block, points, order):
    line = [block[n : n + 1] for n in range(MU_ROWS)]
    mu = [(line[n], line[8 + n]) for n in range(6)]
    ok0 = line[0] > 0
    reach = 3.0 * line[14] * line[14]
    top, bottom = line[6] + reach, -line[7] - reach
    centre = jnp.clip(ratio(line[1], line[0], ok0), bottom, top)
    central = [mu[0]]
    level = mu
    for _ in range(5):
        level = [
            pair_add(after, tuple(-x for x in pair_times(now, centre))) for now, after in zip(level[:-1], level[1:])
        ]
        central.append(level[0])
    m0, m1, m2, m3, m4, m5 = (x[0] + x[1] for x in central)
    tiny = F32(1e-7)
    low, high = bottom - centre, top - centre
    a0 = jnp.clip(ratio(m1, m0, ok0), low, high)
    s11 = m2 - a0 * m1
    s12 = m3 - a0 * m2
    s13 = m4 - a0 * m3
    s14 = m5 - a0 * m4
    ok1 = ok0 & (s11 > tiny * m2)
    widest = 0.25 * (high - low) * (high - low)
    b1 = jnp.clip(ratio(s11, m0, ok1), 0.0, widest)
    g1 = ratio(s12, s11, ok1)
    a1 = jnp.clip(jnp.where(ok1, g1 - a0, a0), low, high)
    s22 = s13 - a1 * s12 - b1 * m2
    s23 = s14 - a1 * s13 - b1 * m3
    ok2 = ok1 & (s22 > tiny * m4)
    b2 = jnp.clip(ratio(s22, s11, ok2), 0.0, widest)
    a2 = jnp.clip(jnp.where(ok2, ratio(s23, s22, ok2) - g1, a1), low, high)
    a0, a1, a2 = a0 + centre, a1 + centre, a2 + centre
    leading = TOTAL_PTS // 4 - points // 2
    p = lax.broadcasted_iota(jnp.int32, (points, m0.shape[1]), 0).astype(F32)
    angle = 2.0 * math.pi * (p + leading + 0.5) / TOTAL_PTS
    zr = CENTER + RADIUS * jnp.cos(angle)
    zi = RADIUS * jnp.sin(angle)
    wr = RADIUS / points * jnp.cos(order * angle)
    wi = RADIUS / points * jnp.sin(order * angle)
    i2 = inverse((zr - a2, zi))
    i1 = inverse((zr - a1 - b2 * i2[0], zi - b2 * i2[1]))
    y0 = inverse((zr - a0 - b1 * i1[0], zi - b1 * i1[1]))
    y0 = cmul((wr, wi), y0)
    y1 = cmul(y0, i1)
    y2 = cmul(y1, i2)
    out = []
    for part in range(2):
        t0, t1, t2 = (jnp.sum(y[part], axis=0, keepdims=True) for y in (y0, y1, y2))
        out.append((t0 - a0 * t1 + (a0 * a1 - b1) * t2, t1 - (a0 + a1) * t2, t2))
    return out


def spread(table_ref, parity, lane):
    half = table_ref.shape[0] // 2
    rows = table_ref[pl.ds(parity, half, stride=2), :]
    return jnp.broadcast_to(rows[:, lane : lane + 1], (half, LANES))


def horizontal(even, odd):
    size = even.shape[0]
    site = lax.broadcasted_iota(jnp.int32, even.shape, 0)
    left = jnp.where(site == 0, 0.0, pltpu.roll(odd, 1, 0))
    right = jnp.where(site == size - 1, 0.0, pltpu.roll(even, size - 1, 0))
    return odd + left, even + right


def site_table(onsite, strain, present):
    return jnp.concatenate([present.astype(F32) * strain, onsite], axis=0)


def bound_up(i, p):
    return (i + p) % 2 == 0


def fold(value):
    tiles = value.reshape(value.shape[0] // 32, 4, 8, value.shape[1])
    return [tiles[n, 0] + tiles[n, 1] + (tiles[n, 2] + tiles[n, 3]) for n in range(tiles.shape[0])]


def total(terms):
    first, *others = [part for term in terms for part in fold(term)]
    whole = (first, jnp.zeros((8, LANES), F32))
    for part in others:
        high, rest = two_sum(whole[0], part)
        whole = (high, whole[1] + rest)
    for size in (4, 2, 1):
        whole = pair_add(*((whole[0][k : k + size], whole[1][k : k + size]) for k in (0, size)))
    return whole


def joined(one, two):
    high, rest = two_sum(one[:8], two[:8])
    high, rest = two_sum(high, rest + (one[8:] + two[8:]))
    row = lax.broadcasted_iota(jnp.int32, high.shape, 0)
    return jnp.concatenate(
        [jnp.where(row < 6, high, jnp.maximum(one[:8], two[:8])), jnp.where(row < 6, rest, jnp.maximum(one[8:], two[8:]))],
        axis=0,
    )


def split(value):
    high = value.astype(BF16)
    return high, (value - high.astype(F32)).astype(BF16)


def edges_kernel(
    sources_ref, onsite_ref, strain_ref, present_ref, first_ref, second_ref, table_ref,
    rows_ref, onsite_in, strain_in, present_in, sem,
):
    rows, sites, _ = sources_ref.shape
    count = sites // 2
    columns = pl.ds(pl.multiple_of(lax.rem(lax.axis_index("quad"), 2) * LANES, LANES), LANES)
    pairs = [(onsite_ref, onsite_in), (strain_ref, strain_in), (present_ref, present_in)]
    for slot, row in enumerate((0, 1, rows - 1, rows - 2)):
        pairs.append((sources_ref.at[row, :, columns], rows_ref.at[slot]))
    copies = [pltpu.make_async_copy(src, dst, sem.at[k]) for k, (src, dst) in enumerate(pairs)]
    for copy in copies:
        copy.start()
    for copy in copies[:3]:
        copy.wait()
    table = site_table(onsite_in[...], strain_in[...], present_in[...])
    tail = table.shape[0]
    table_ref[:, :tail] = table.T
    for part in range(sites // LANES):
        at = pl.ds(2 * count + shared(count) + part * tail, tail)
        first_ref[at, :] = second_ref[at, :] = table[:, part * LANES : (part + 1) * LANES]
    for copy in copies[3:]:
        copy.wait()

    def scaled(slot, row, parity):
        return rows_ref[slot, pl.ds(parity, count, stride=2), :] * spread(table_ref, parity, row)

    size = shared(count)
    up = [scaled(2, rows - 1, 0), scaled(2, rows - 1, 1), scaled(3, rows - 2, 0)[count - size :]]
    down = [scaled(0, 0, 0), scaled(0, 0, 1), scaled(1, 1, 0)[:size]]
    even = lax.rem(lax.axis_index("rows"), 2) == 0
    for block in range(3):
        at = pl.ds(block * count, up[block].shape[0])
        first_ref[at, :] = jnp.where(even, up[block], down[block])
        second_ref[at, :] = jnp.where(even, down[block], up[block])


def shared(count):
    return count // 2 + 8


def near(u, wanted, up_halo, down_halo, top):
    out = {}
    for i in wanted:
        sums = horizontal(u[i, 0], u[i, 1])
        for p in range(2):
            if bound_up(i, p):
                other = u[i + 1, p] if i < top else up_halo
            else:
                other = u[i - 1, p] if i > 0 else down_halo
            out[i, p] = sums[p] if other is None else sums[p] + other
    return out


def bonds(scale, w, wanted):
    u = {(i, p): scale[i, p] * w[i, p] for i in wanted for p in range(2)}
    out = {}
    for i in wanted:
        out[i, 0] = u[i, 0] * horizontal(u[i, 0], u[i, 1])[0]
        out[i, 1] = jnp.zeros_like(u[i, 1])
        for p in range(2):
            if bound_up(i, p) and (i + 1, p) in u:
                out[i, p] = out[i, p] + u[i, p] * u[i + 1, p]
    return out


def beside(i, top):
    return (1, 0) if i == 0 else (top - 1, 0)


def inner_kernel(sources_ref, table_ref, b_ref, w_ref, aid_ref, mu_ref, gram_ref, left_hi_ref, left_lo_ref, full_ref, sem):
    rows, sites, _ = sources_ref.shape
    count = sites // 2
    top = rows - 1
    half = lax.rem(lax.axis_index("quad"), 2)
    copies = [
        pltpu.make_async_copy(sources_ref.at[:, :, pl.ds(side * LANES, LANES)], full_ref.at[side], sem.at[side])
        for side in range(2)
    ]
    for copy in copies:
        copy.start()
    for copy in copies:
        copy.wait()
    keys = [(i, p) for i in range(rows) for p in range(2)]
    for side in range(2):
        for i, p in keys:
            b_ref[side, i, p] = full_ref[side, i, pl.ds(p, count, stride=2), :]
    scale = {(i, p): spread(table_ref, p, i) for i, p in keys}
    level = {(i, p): spread(table_ref, p, rows + i) for i, p in keys}
    b = {(i, p): b_ref[half, i, p] for i, p in keys}
    u0 = {k: scale[k] * b[k] for k in keys}
    n0 = near(u0, range(rows), None, None, top)
    w1 = {k: level[k] * b[k] - scale[k] * n0[k] for k in keys}
    for i, p in keys:
        w_ref[0, i, p] = w1[i, p]
    u1 = {k: scale[k] * w1[k] for k in keys}
    inside = [(i, p) for i, p in keys if 0 < i < top]
    n1 = near(u1, range(1, top), None, None, top)
    w2 = {k: level[k] * w1[k] - scale[k] * n1[k] for k in inside}
    for i, p in inside:
        w_ref[1, i, p] = w2[i, p]
    for index, i in enumerate((0, top)):
        for p in range(2):
            aid_ref[index, p] = scale[i, p]
            aid_ref[index, 2 + p] = level[i, p]
        k = beside(i, top)
        aid_ref[index, 4] = u0[i, 1]
        aid_ref[index, 5] = u1[k]
        aid_ref[index, 6] = scale[k] * w2[k]
    mu = [
        total([b[k] * b[k] for k in keys]),
        total([b[k] * w1[k] for k in inside]),
        total([w1[k] * w1[k] for k in inside]),
        total([w1[k] * w2[k] for k in inside]),
        total([w2[k] * w2[k] for k in inside]),
        total([level[k] * w2[k] * w2[k] - 2.0 * x for k, x in bonds(scale, w2, range(1, top)).items()]),
    ]
    table = table_ref[...]
    lane = lax.broadcasted_iota(jnp.int32, table.shape, 1)
    scales = jnp.max(jnp.where(lane < rows, table, 0.0), keepdims=True)
    is_level = (lane >= rows) & (lane < 2 * rows)
    most = jnp.max(jnp.where(is_level, table, -LARGE), keepdims=True)
    least = jnp.max(jnp.where(is_level, -table, -LARGE), keepdims=True)
    limits = [jnp.broadcast_to(x, (1, LANES)) for x in (most, least, scales)]
    mu_ref[...] = jnp.concatenate(
        [x[0] for x in mu] + limits[:2] + [x[1] for x in mu] + [limits[2], jnp.zeros((1, LANES), F32)], axis=0
    )
    order = inside + [k for k in keys if k not in inside]
    left = jnp.concatenate([jnp.concatenate([b_ref[0, i, p], b_ref[1, i, p]], axis=1) for i, p in order], axis=0)
    left_hi, left_lo = (x.T for x in split(left))
    own_hi, own_lo = split(jnp.concatenate([b[k] for k in order], axis=0))
    depth = len(inside) * count
    in_hi, in_lo = split(
        jnp.concatenate([jnp.concatenate([w1[k], w2[k]], axis=1) for k in inside], axis=0)
    )
    gram_ref[:, :LANES] = triple(left_hi, left_lo, own_hi, own_lo)
    gram_ref[:, LANES:] = triple(left_hi[:, :depth], left_lo[:, :depth], in_hi, in_lo)
    left_hi_ref[...] = left_hi[:, depth:]
    left_lo_ref[...] = left_lo[:, depth:]


def triple(left_hi, left_lo, right_hi, right_lo):
    def product(left, right):
        return jnp.dot(left, right, preferred_element_type=F32)

    return product(left_hi, right_hi) + (product(left_hi, right_lo) + product(left_lo, right_hi))


def outer_kernel(
    parts, b_ref, w_in_ref, aid_ref, mu_in_ref, gram_ref, left_hi_ref, left_lo_ref, first_ref, second_ref, *refs
):
    chunk_refs, (w_ref, far_ref, tile_ref) = refs[:parts], refs[parts:]
    _, rows, _, count, _ = b_ref.shape
    sites = 2 * count
    top = rows - 1
    half = lax.rem(lax.axis_index("quad"), 2)
    mine = lax.axis_index("rows")
    tail = 2 * rows
    even = lax.rem(mine, 2) == 0
    size = shared(count)

    def arrived(start, size):
        one, two = first_ref[pl.ds(start, size), :], second_ref[pl.ds(start, size), :]
        return jnp.where(even, two, one), jnp.where(even, one, two)

    for part in range(sites // LANES):
        for slot, value in enumerate(arrived(2 * count + size + part * tail, tail)):
            far_ref[slot, pl.ds(part * LANES, LANES), :tail] = value.T

    outside = [(i, p) for i in (0, top) for p in range(2)]
    aid = {i: [aid_ref[index, n] for n in range(7)] for index, i in enumerate((0, top))}
    scale = {(i, p): aid[i][p] for i, p in outside}
    level = {(i, p): aid[i][2 + p] for i, p in outside}
    b = {k: b_ref[half, k[0], k[1]] for k in outside}
    w1 = {k: w_in_ref[0, k[0], k[1]] for k in outside}
    below0, above0 = zip(arrived(0, count), arrived(count, count))
    w1[0, 1] = w1[0, 1] - scale[0, 1] * below0[1]
    w1[top, 1] = w1[top, 1] - scale[top, 1] * above0[1]
    u1 = {k: scale[k] * w1[k] for k in outside}

    missing = jnp.zeros((count - size, LANES), F32)
    low, high = arrived(2 * count, size)
    edge_next = {0: jnp.concatenate([missing, low], axis=0), top: jnp.concatenate([high, missing], axis=0)}
    edge_w2, far_w2 = {}, {}
    for i, halo, slot, row in ((0, below0, 0, top), (top, above0, 1, 0)):
        far_table = far_ref.at[slot]
        square = [spread(far_table, p, row) for p in range(2)]
        square = [x * x for x in square]
        far_level = [spread(far_table, p, rows + row) for p in range(2)]
        sums = horizontal(halo[0], halo[1])
        far1 = [
            far_level[0] * halo[0] - square[0] * (sums[0] + edge_next[i]),
            far_level[1] * halo[1] - square[1] * (sums[1] + aid[i][4]),
        ]
        sums = horizontal(u1[i, 0], u1[i, 1])
        edge_w2[i, 0] = level[i, 0] * w1[i, 0] - scale[i, 0] * (sums[0] + aid[i][5])
        edge_w2[i, 1] = level[i, 1] * w1[i, 1] - scale[i, 1] * (sums[1] + far1[1])
        sums = horizontal(far1[0], far1[1])
        far_w2[i] = far_level[1] * far1[1] - square[1] * (sums[1] + u1[i, 1])
    w2 = edge_w2
    site = lax.broadcasted_iota(jnp.int32, (count, LANES), 0)
    counted = {0: site >= count // 2, top: site < count // 2}
    pairs = bonds(scale, w2, (0,))
    pairs.update(bonds(scale, w2, (top,)))
    for i in (0, top):
        pairs[i, 0] = pairs[i, 0] + scale[i, 0] * w2[i, 0] * aid[i][6]
        pairs[i, 1] = pairs[i, 1] + scale[i, 1] * w2[i, 1] * jnp.where(counted[i], far_w2[i], 0.0)

    mu = [
        total([b[k] * w1[k] for k in outside]),
        total([w1[k] * w1[k] for k in outside]),
        total([w1[k] * w2[k] for k in outside]),
        total([w2[k] * w2[k] for k in outside]),
        total([level[k] * w2[k] * w2[k] - 2.0 * pairs[k] for k in outside]),
    ]
    zero = jnp.zeros((1, LANES), F32)
    mu = joined(
        mu_in_ref[...],
        jnp.concatenate([zero] + [x[0] for x in mu] + [zero - LARGE] * 2 + [zero] + [x[1] for x in mu] + [zero] * 2, axis=0),
    )
    for i, p in outside:
        w_ref[0, i, p] = w1[i, p]
        w_ref[1, i, p] = w2[i, p]
    right_hi, right_lo = split(
        jnp.concatenate([jnp.concatenate([w1[k], w2[k]], axis=1) for k in outside], axis=0)
    )
    more = triple(left_hi_ref[...], left_lo_ref[...], right_hi, right_lo)
    row = lax.broadcasted_iota(jnp.int32, (LANES, LANES), 0)
    lane = lax.broadcasted_iota(jnp.int32, (LANES, LANES), 1)
    for j in range(3):
        lanes = slice(j * LANES, (j + 1) * LANES)
        first, second = gram_ref[:LANES, lanes], gram_ref[LANES:, lanes]
        if j:
            lanes = slice((j - 1) * LANES, j * LANES)
            first, second = first + more[:LANES, lanes], second + more[LANES:, lanes]
        own = jnp.where(half == 0, first, second)
        cross = jnp.where(half == 0, second, first)
        tile_ref[pl.ds(j * LANES, LANES), :] = jnp.where(row < lane, own, cross)
    size = 3 * LANES // parts
    for part, ref in enumerate(chunk_refs):
        start = pl.multiple_of((mine ^ part) * size if parts > 1 else 0, 8)
        ref[pl.ds(0, size), :] = tile_ref[pl.ds(start, size), :]
        ref[pl.ds(size, MU_ROWS), :] = mu


def sum_kernel(size, *refs):
    *shares, out_ref = refs
    at, tail = pl.ds(0, size), pl.ds(size, MU_ROWS)
    out_ref[at, :] = (shares[0][at, :] + shares[1][at, :]) + (shares[2][at, :] + shares[3][at, :])
    out_ref[tail, :] = joined(
        joined(shares[0][tail, :], shares[1][tail, :]), joined(shares[2][tail, :], shares[3][tail, :])
    )


def moments_kernel(points, b_ref, w_ref, v_ref, mu_ref, nu_ref, out_ref, coef_ref, made_ref, out_sem):
    quad = lax.axis_index("quad")
    half = lax.rem(quad, 2)
    _, rows, _, count, _ = b_ref.shape
    first = jnp.where(half == 0, mu_ref[...], nu_ref[...])
    second = jnp.where(half == 0, nu_ref[...], mu_ref[...])
    mu = jnp.concatenate([first, second], axis=1)
    coefs = coefficients(mu, points, (quad + 1).astype(F32))
    lines = [line for part in coefs for line in part]
    coef_ref[...] = jnp.concatenate(lines + [jnp.zeros_like(lines[0])] * 2, axis=0)
    stores = []
    for i in range(rows):
        for side in range(2):
            lanes = slice(side * LANES, (side + 1) * LANES)
            for p in range(2):
                fields = [b_ref[side, i, p]]
                fields += [jnp.where(half == side, w_ref[j, i, p], v_ref[j, i, p]) for j in range(2)]
                for part in range(2):
                    terms = [lines[3 * part + j][:, lanes] * fields[j] for j in range(3)]
                    made_ref[part, i, side, pl.ds(p, count, stride=2), :] = terms[0] + terms[1] + terms[2]
            for part in range(2):
                copy = pltpu.make_async_copy(
                    made_ref.at[part, i, side],
                    out_ref.at[0, part, i, :, pl.ds(side * LANES, LANES)],
                    out_sem.at[part, i, side],
                )
                copy.start()
                stores.append(copy)
    for copy in stores:
        copy.wait()


def tile_blocks(half, tile, mu):
    row = lax.broadcasted_iota(jnp.int32, (LANES, LANES), 0)
    lane = lax.broadcasted_iota(jnp.int32, (LANES, LANES), 1)
    flip = tile.T
    same = jnp.where(row < lane, tile, jnp.where(row > lane, flip, mu))
    below = jnp.where(half == 0, jnp.where(row >= lane, tile, 0.0), jnp.where(row < lane, flip, 0.0))
    above = jnp.where(half == 0, jnp.where(row <= lane, flip, 0.0), jnp.where(row > lane, tile, 0.0))
    return same, below, above


def gather(parts, tile_ref, chunk_refs):
    size = 3 * LANES // parts
    for part, ref in zip([0, *range(parts - 1, 0, -1)], chunk_refs):
        start = pl.multiple_of((lax.axis_index("rows") ^ part) * size if parts > 1 else 0, 8)
        tile_ref[pl.ds(start, size), :] = ref[pl.ds(0, size), :]


def weighted(parts, orbitals, half, coef_ref, mu_ref, tile_ref):
    sums = {}
    for j in range(3):
        blocks = tile_blocks(half, tile_ref[j * LANES : (j + 1) * LANES, :], mu_ref[j : j + 1, :])
        for part in range(2):
            line = coef_ref[3 * part + j : 3 * part + j + 1, :] * F32(1.0 / orbitals)
            first, second = line[:, :LANES], line[:, LANES:]
            own = jnp.where(half == 0, first, second)
            for which, (lane_coef, value) in enumerate(zip((own, first, second), blocks)):
                term = lane_coef * value
                sums[part, which] = term if j == 0 else sums[part, which] + term
    return sums


def own_kernel(parts, orbitals, coef_ref, mu_ref, *refs):
    chunk_refs, (out_ref, tile_ref) = refs[:parts], refs[parts:]
    half = lax.rem(lax.axis_index("quad"), 2)
    gather(parts, tile_ref, chunk_refs)
    for (part, which), value in weighted(parts, orbitals, half, coef_ref, mu_ref, tile_ref).items():
        out_ref[part, which] = value


def far_kernel(parts, orbitals, coef_ref, mu_ref, own_ref, *refs):
    chunk_refs, (out_ref, tile_ref, made_ref, sem) = refs[:parts], refs[parts:]
    half = lax.rem(lax.axis_index("quad"), 2)
    gather(parts, tile_ref, chunk_refs)
    sums = weighted(parts, orbitals, 1 - half, coef_ref, mu_ref, tile_ref)
    copies = []
    for part in range(2):
        same = [own_ref[part, 0], sums[part, 0]]
        blocks = {
            (0, 0): jnp.where(half == 0, same[0], same[1]),
            (0, 1): own_ref[part, 2] + sums[part, 2],
            (1, 0): own_ref[part, 1] + sums[part, 1],
            (1, 1): jnp.where(half == 0, same[1], same[0]),
        }
        for (x, y), value in blocks.items():
            made_ref[part, x * LANES : (x + 1) * LANES, y * LANES : (y + 1) * LANES] = value
        copies.append(pltpu.make_async_copy(made_ref.at[part], out_ref.at[0, part], sem.at[part]))
        copies[-1].start()
    for copy in copies:
        copy.wait()


def struct(*shape, dtype=F32):
    return jax.ShapeDtypeStruct(shape, dtype)


def cost(flops, nbytes):
    return pl.CostEstimate(flops=flops, bytes_accessed=nbytes, transcendentals=0)


def body(sources, onsite, strain, present):
    n_rows = lax.axis_size("rows")
    n_quad = lax.axis_size("quad")
    points = PTS_DEV * n_quad
    rows, sites, columns = sources.shape
    count = sites // 2
    orbitals = rows * sites * n_rows
    tail = 2 * rows * (sites // LANES)
    payload = 2 * count + shared(count) + tail
    first, second, table = pl.pallas_call(
        edges_kernel,
        out_shape=(struct(payload, LANES), struct(payload, LANES), struct(sites, LANES)),
        in_specs=[HBM] * 4,
        out_specs=(VMEM, VMEM, VMEM),
        scratch_shapes=[
            pltpu.VMEM((4, sites, LANES), F32),
            pltpu.VMEM((rows, sites), F32),
            pltpu.VMEM((rows, sites), F32),
            pltpu.VMEM((rows, sites), jnp.int32),
            pltpu.SemaphoreType.DMA((7,)),
        ],
        compiler_params=PARAMS,
        name="edges",
    )(*(pltpu.with_memory_space_constraint(x, pltpu.HBM) for x in (sources, onsite, strain, present)))
    halo = []
    for value, start in ((first, 0), (second, 1)):
        bonds = [(i, i + 1) for i in range(start, n_rows - 1, 2)]
        halo.append(lax.ppermute(value, "rows", bonds + [(j, i) for i, j in bonds]))
    outer_depth = 4 * count
    inner = pl.pallas_call(
        inner_kernel,
        out_shape=(
            struct(2, rows, 2, count, LANES),
            struct(2, rows, 2, count, LANES),
            struct(2, 7, count, LANES),
            struct(MU_ROWS, LANES),
            struct(columns, 3 * LANES),
            struct(columns, outer_depth, dtype=BF16),
            struct(columns, outer_depth, dtype=BF16),
        ),
        in_specs=[ANY, VMEM],
        out_specs=(VMEM,) * 7,
        scratch_shapes=[pltpu.VMEM((2, rows, sites, LANES), F32), pltpu.SemaphoreType.DMA((2,))],
        compiler_params=PARAMS,
        cost_estimate=cost(10**9, 8 * 2**20),
        name="inner",
    )(sources, table)
    b_all = inner[0]

    pairwise = n_rows == 4
    parts = n_rows if pairwise else 1
    far_first = list(range(parts - 1, 0, -1))
    size = 3 * LANES // parts
    *chunks, fields = pl.pallas_call(
        functools.partial(outer_kernel, parts),
        out_shape=(struct(size + MU_ROWS, LANES),) * parts + (struct(2, rows, 2, count, LANES),),
        in_specs=[VMEM] * 9,
        out_specs=(VMEM,) * (parts + 1),
        input_output_aliases={1: parts},
        scratch_shapes=[pltpu.VMEM((2, sites, LANES), F32), pltpu.VMEM((3 * LANES, LANES), F32)],
        compiler_params=PARAMS,
        cost_estimate=cost(4 * 10**8, 4 * 2**20),
        name="outer",
    )(*inner, *halo)

    def partner(value):
        return lax.ppermute(value, "quad", [(i, i ^ 1) for i in range(n_quad)])

    def across(value, mask):
        return lax.ppermute(value, "rows", [(i, i ^ mask) for i in range(n_rows)])

    if pairwise:
        summed = pl.pallas_call(
            functools.partial(sum_kernel, size),
            out_shape=struct(size + MU_ROWS, LANES),
            in_specs=[VMEM] * parts,
            out_specs=VMEM,
            compiler_params=PARAMS,
            cost_estimate=cost(10**5, 2**18),
            name="sum",
        )(chunks[0], *(across(chunks[mask], mask) for mask in far_first))
        sums = [summed[:size]] + [across(summed[:size], mask) for mask in far_first]
    else:
        shares = lax.all_gather(chunks[0][size:], "rows")
        mu = functools.reduce(joined, [shares[n] for n in range(n_rows)])
        summed = jnp.concatenate([lax.psum(chunks[0][:size], "rows"), mu], axis=0)
        sums = [summed[:size]]
    summed, fields = lax.optimization_barrier((summed, fields))
    far_summed = partner(summed)
    far_fields = partner(fields)
    mu, far_mu = summed[size:], far_summed[size:]
    far_sums = [far_summed[:size]]
    moments, coefs = pl.pallas_call(
        functools.partial(moments_kernel, points),
        out_shape=(struct(1, 2, rows, sites, columns), struct(8, columns)),
        in_specs=[VMEM] * 5,
        out_specs=(ANY, VMEM),
        scratch_shapes=[pltpu.VMEM((2, rows, 2, sites, LANES), F32), pltpu.SemaphoreType.DMA((2, rows, 2))],
        compiler_params=PARAMS,
        cost_estimate=cost(10**7, 8 * 2**20),
        name="moments",
    )(b_all, fields, far_fields, mu, far_mu)
    *late, coefs = lax.optimization_barrier((*sums[2:], coefs))
    sums = sums[:2] + late
    far_sums += [partner(value) for value in sums[1:]]
    own = pl.pallas_call(
        functools.partial(own_kernel, parts, orbitals),
        out_shape=struct(2, 3, LANES, LANES),
        in_specs=[VMEM] * (2 + parts),
        out_specs=VMEM,
        scratch_shapes=[pltpu.VMEM((3 * LANES, LANES), F32)],
        compiler_params=PARAMS,
        cost_estimate=cost(10**6, 2**20),
        name="own",
    )(coefs, mu, *sums)
    reduced = pl.pallas_call(
        functools.partial(far_kernel, parts, orbitals),
        out_shape=struct(1, 2, columns, columns),
        in_specs=[VMEM] * (3 + parts),
        out_specs=ANY,
        scratch_shapes=[
            pltpu.VMEM((3 * LANES, LANES), F32),
            pltpu.VMEM((2, columns, columns), F32),
            pltpu.SemaphoreType.DMA((2,)),
        ],
        compiler_params=PARAMS,
        cost_estimate=cost(10**6, 2**20),
        name="reduced",
    )(coefs, far_mu, own, *far_sums)
    return moments, reduced


def solution(mesh):
    in_specs = (
        P(("groups", "rows"), None, None),
        P(("groups", "rows"), None),
        P(("groups", "rows"), None),
        P(("groups", "rows"), None),
    )
    out_specs = (P("quad", None, ("groups", "rows"), None, None), P("quad", None, "groups", None))
    return jax.shard_map(body, mesh=mesh, in_specs=in_specs, out_specs=out_specs, check_vma=False)
```

```python
import functools
import math

import jax
import jax.numpy as jnp
from jax import lax
from jax.experimental import pallas as pl
from jax.experimental.pallas import tpu as pltpu
from jax.sharding import PartitionSpec as P

TOTAL_PTS = 32
PTS_DEV = 2
CENTER = 0.4
RADIUS = 1.0
MU_ROWS = 16
LANES = 128
LARGE = 1e30
F32 = jnp.float32
BF16 = jnp.bfloat16
PARAMS = pltpu.CompilerParams(vmem_limit_bytes=32 * 1024 * 1024)
VMEM = pl.BlockSpec(memory_space=pltpu.VMEM)
HBM = pl.BlockSpec(memory_space=pltpu.HBM)
ANY = pl.BlockSpec(memory_space=pl.ANY)


def ratio(top, bottom, good):
    return jnp.where(good, top / jnp.where(good, bottom, 1.0), 0.0)


def cmul(a, b):
    return (a[0] * b[0] - a[1] * b[1], a[0] * b[1] + a[1] * b[0])


def inverse(a):
    size = a[0] * a[0] + a[1] * a[1]
    return (a[0] / size, -a[1] / size)


def two_sum(a, b):
    total = a + b
    part = total - a
    return total, (a - (total - part)) + (b - part)


def pair_add(a, b):
    total, rest = two_sum(a[0], b[0])
    return two_sum(total, rest + (a[1] + b[1]))


def halves(a):
    scaled = F32(4097.0) * a
    high = scaled - (scaled - a)
    return high, a - high


def pair_times(a, b):
    product = a[0] * b
    (ah, al), (bh, bl) = halves(a[0]), halves(b)
    rest = ((ah * bh - product) + ah * bl + al * bh) + al * bl
    return two_sum(product, rest + a[1] * b)


def coefficients(block, points, order):
    line = [block[n : n + 1] for n in range(MU_ROWS)]
    mu = [(line[n], line[8 + n]) for n in range(6)]
    ok0 = line[0] > 0
    reach = 3.0 * line[14] * line[14]
    top, bottom = line[6] + reach, -line[7] - reach
    centre = jnp.clip(ratio(line[1], line[0], ok0), bottom, top)
    central = [mu[0]]
    level = mu
    for _ in range(5):
        level = [
            pair_add(after, tuple(-x for x in pair_times(now, centre))) for now, after in zip(level[:-1], level[1:])
        ]
        central.append(level[0])
    m0, m1, m2, m3, m4, m5 = (x[0] + x[1] for x in central)
    tiny = F32(1e-7)
    low, high = bottom - centre, top - centre
    a0 = jnp.clip(ratio(m1, m0, ok0), low, high)
    s11 = m2 - a0 * m1
    s12 = m3 - a0 * m2
    s13 = m4 - a0 * m3
    s14 = m5 - a0 * m4
    ok1 = ok0 & (s11 > tiny * m2)
    widest = 0.25 * (high - low) * (high - low)
    b1 = jnp.clip(ratio(s11, m0, ok1), 0.0, widest)
    g1 = ratio(s12, s11, ok1)
    a1 = jnp.clip(jnp.where(ok1, g1 - a0, a0), low, high)
    s22 = s13 - a1 * s12 - b1 * m2
    s23 = s14 - a1 * s13 - b1 * m3
    ok2 = ok1 & (s22 > tiny * m4)
    b2 = jnp.clip(ratio(s22, s11, ok2), 0.0, widest)
    a2 = jnp.clip(jnp.where(ok2, ratio(s23, s22, ok2) - g1, a1), low, high)
    a0, a1, a2 = a0 + centre, a1 + centre, a2 + centre
    leading = TOTAL_PTS // 4 - points // 2
    p = lax.broadcasted_iota(jnp.int32, (points, m0.shape[1]), 0).astype(F32)
    angle = 2.0 * math.pi * (p + leading + 0.5) / TOTAL_PTS
    zr = CENTER + RADIUS * jnp.cos(angle)
    zi = RADIUS * jnp.sin(angle)
    wr = RADIUS / points * jnp.cos(order * angle)
    wi = RADIUS / points * jnp.sin(order * angle)
    i2 = inverse((zr - a2, zi))
    i1 = inverse((zr - a1 - b2 * i2[0], zi - b2 * i2[1]))
    y0 = inverse((zr - a0 - b1 * i1[0], zi - b1 * i1[1]))
    y0 = cmul((wr, wi), y0)
    y1 = cmul(y0, i1)
    y2 = cmul(y1, i2)
    out = []
    for part in range(2):
        t0, t1, t2 = (jnp.sum(y[part], axis=0, keepdims=True) for y in (y0, y1, y2))
        out.append((t0 - a0 * t1 + (a0 * a1 - b1) * t2, t1 - (a0 + a1) * t2, t2))
    return out


def spread(table_ref, parity, lane):
    half = table_ref.shape[0] // 2
    rows = table_ref[pl.ds(parity, half, stride=2), :]
    return jnp.broadcast_to(rows[:, lane : lane + 1], (half, LANES))


def horizontal(even, odd):
    size = even.shape[0]
    site = lax.broadcasted_iota(jnp.int32, even.shape, 0)
    left = jnp.where(site == 0, 0.0, pltpu.roll(odd, 1, 0))
    right = jnp.where(site == size - 1, 0.0, pltpu.roll(even, size - 1, 0))
    return odd + left, even + right


def site_table(onsite, strain, present):
    return jnp.concatenate([present.astype(F32) * strain, onsite], axis=0)


def bound_up(i, p):
    return (i + p) % 2 == 0


def fold(value):
    tiles = value.reshape(value.shape[0] // 32, 4, 8, value.shape[1])
    return [tiles[n, 0] + tiles[n, 1] + (tiles[n, 2] + tiles[n, 3]) for n in range(tiles.shape[0])]


def total(terms):
    first, *others = [part for term in terms for part in fold(term)]
    whole = (first, jnp.zeros((8, LANES), F32))
    for part in others:
        high, rest = two_sum(whole[0], part)
        whole = (high, whole[1] + rest)
    for size in (4, 2, 1):
        whole = pair_add(*((whole[0][k : k + size], whole[1][k : k + size]) for k in (0, size)))
    return whole


def joined(one, two):
    high, rest = two_sum(one[:8], two[:8])
    high, rest = two_sum(high, rest + (one[8:] + two[8:]))
    row = lax.broadcasted_iota(jnp.int32, high.shape, 0)
    return jnp.concatenate(
        [jnp.where(row < 6, high, jnp.maximum(one[:8], two[:8])), jnp.where(row < 6, rest, jnp.maximum(one[8:], two[8:]))],
        axis=0,
    )


def split(value):
    high = value.astype(BF16)
    return high, (value - high.astype(F32)).astype(BF16)


def edges_kernel(
    sources_ref, onsite_ref, strain_ref, present_ref, first_ref, second_ref, table_ref,
    rows_ref, onsite_in, strain_in, present_in, sem,
):
    rows, sites, _ = sources_ref.shape
    count = sites // 2
    columns = pl.ds(pl.multiple_of(lax.rem(lax.axis_index("quad"), 2) * LANES, LANES), LANES)
    pairs = [(onsite_ref, onsite_in), (strain_ref, strain_in), (present_ref, present_in)]
    for slot, row in enumerate((0, 1, rows - 1, rows - 2)):
        pairs.append((sources_ref.at[row, :, columns], rows_ref.at[slot]))
    copies = [pltpu.make_async_copy(src, dst, sem.at[k]) for k, (src, dst) in enumerate(pairs)]
    for copy in copies:
        copy.start()
    for copy in copies[:3]:
        copy.wait()
    table = site_table(onsite_in[...], strain_in[...], present_in[...])
    tail = table.shape[0]
    table_ref[:, :tail] = table.T
    for part in range(sites // LANES):
        at = pl.ds(2 * count + shared(count) + part * tail, tail)
        first_ref[at, :] = second_ref[at, :] = table[:, part * LANES : (part + 1) * LANES]
    for copy in copies[3:]:
        copy.wait()

    def scaled(slot, row, parity):
        return rows_ref[slot, pl.ds(parity, count, stride=2), :] * spread(table_ref, parity, row)

    size = shared(count)
    up = [scaled(2, rows - 1, 0), scaled(2, rows - 1, 1), scaled(3, rows - 2, 0)[count - size :]]
    down = [scaled(0, 0, 0), scaled(0, 0, 1), scaled(1, 1, 0)[:size]]
    even = lax.rem(lax.axis_index("rows"), 2) == 0
    for block in range(3):
        at = pl.ds(block * count, up[block].shape[0])
        first_ref[at, :] = jnp.where(even, up[block], down[block])
        second_ref[at, :] = jnp.where(even, down[block], up[block])


def shared(count):
    return count // 2 + 8


def near(u, wanted, up_halo, down_halo, top):
    out = {}
    for i in wanted:
        sums = horizontal(u[i, 0], u[i, 1])
        for p in range(2):
            if bound_up(i, p):
                other = u[i + 1, p] if i < top else up_halo
            else:
                other = u[i - 1, p] if i > 0 else down_halo
            out[i, p] = sums[p] if other is None else sums[p] + other
    return out


def bonds(scale, w, wanted):
    u = {(i, p): scale[i, p] * w[i, p] for i in wanted for p in range(2)}
    out = {}
    for i in wanted:
        out[i, 0] = u[i, 0] * horizontal(u[i, 0], u[i, 1])[0]
        out[i, 1] = jnp.zeros_like(u[i, 1])
        for p in range(2):
            if bound_up(i, p) and (i + 1, p) in u:
                out[i, p] = out[i, p] + u[i, p] * u[i + 1, p]
    return out


def beside(i, top):
    return (1, 0) if i == 0 else (top - 1, 0)


def inner_kernel(sources_ref, table_ref, b_ref, w_ref, aid_ref, mu_ref, gram_ref, left_hi_ref, left_lo_ref, full_ref, sem):
    rows, sites, _ = sources_ref.shape
    count = sites // 2
    top = rows - 1
    half = lax.rem(lax.axis_index("quad"), 2)
    copies = [
        pltpu.make_async_copy(sources_ref.at[:, :, pl.ds(side * LANES, LANES)], full_ref.at[side], sem.at[side])
        for side in range(2)
    ]
    for copy in copies:
        copy.start()
    for copy in copies:
        copy.wait()
    keys = [(i, p) for i in range(rows) for p in range(2)]
    for side in range(2):
        for i, p in keys:
            b_ref[side, i, p] = full_ref[side, i, pl.ds(p, count, stride=2), :]
    scale = {(i, p): spread(table_ref, p, i) for i, p in keys}
    level = {(i, p): spread(table_ref, p, rows + i) for i, p in keys}
    b = {(i, p): b_ref[half, i, p] for i, p in keys}
    u0 = {k: scale[k] * b[k] for k in keys}
    n0 = near(u0, range(rows), None, None, top)
    w1 = {k: level[k] * b[k] - scale[k] * n0[k] for k in keys}
    for i, p in keys:
        w_ref[0, i, p] = w1[i, p]
    u1 = {k: scale[k] * w1[k] for k in keys}
    inside = [(i, p) for i, p in keys if 0 < i < top]
    n1 = near(u1, range(1, top), None, None, top)
    w2 = {k: level[k] * w1[k] - scale[k] * n1[k] for k in inside}
    for i, p in inside:
        w_ref[1, i, p] = w2[i, p]
    for index, i in enumerate((0, top)):
        for p in range(2):
            aid_ref[index, p] = scale[i, p]
            aid_ref[index, 2 + p] = level[i, p]
        k = beside(i, top)
        aid_ref[index, 4] = u0[i, 1]
        aid_ref[index, 5] = u1[k]
        aid_ref[index, 6] = scale[k] * w2[k]
    mu = [
        total([b[k] * b[k] for k in keys]),
        total([b[k] * w1[k] for k in inside]),
        total([w1[k] * w1[k] for k in inside]),
        total([w1[k] * w2[k] for k in inside]),
        total([w2[k] * w2[k] for k in inside]),
        total([level[k] * w2[k] * w2[k] - 2.0 * x for k, x in bonds(scale, w2, range(1, top)).items()]),
    ]
    table = table_ref[...]
    lane = lax.broadcasted_iota(jnp.int32, table.shape, 1)
    scales = jnp.max(jnp.where(lane < rows, table, 0.0), keepdims=True)
    is_level = (lane >= rows) & (lane < 2 * rows)
    most = jnp.max(jnp.where(is_level, table, -LARGE), keepdims=True)
    least = jnp.max(jnp.where(is_level, -table, -LARGE), keepdims=True)
    limits = [jnp.broadcast_to(x, (1, LANES)) for x in (most, least, scales)]
    mu_ref[...] = jnp.concatenate(
        [x[0] for x in mu] + limits[:2] + [x[1] for x in mu] + [limits[2], jnp.zeros((1, LANES), F32)], axis=0
    )
    order = inside + [k for k in keys if k not in inside]
    left = jnp.concatenate([jnp.concatenate([b_ref[0, i, p], b_ref[1, i, p]], axis=1) for i, p in order], axis=0)
    left_hi, left_lo = (x.T for x in split(left))
    own_hi, own_lo = split(jnp.concatenate([b[k] for k in order], axis=0))
    depth = len(inside) * count
    in_hi, in_lo = split(
        jnp.concatenate([jnp.concatenate([w1[k], w2[k]], axis=1) for k in inside], axis=0)
    )
    gram_ref[:, :LANES] = triple(left_hi, left_lo, own_hi, own_lo)
    gram_ref[:, LANES:] = triple(left_hi[:, :depth], left_lo[:, :depth], in_hi, in_lo)
    left_hi_ref[...] = left_hi[:, depth:]
    left_lo_ref[...] = left_lo[:, depth:]


def triple(left_hi, left_lo, right_hi, right_lo):
    def product(left, right):
        return jnp.dot(left, right, preferred_element_type=F32)

    return product(left_hi, right_hi) + (product(left_hi, right_lo) + product(left_lo, right_hi))


def outer_kernel(
    parts, b_ref, w_in_ref, aid_ref, mu_in_ref, gram_ref, left_hi_ref, left_lo_ref, first_ref, second_ref, *refs
):
    chunk_refs, (w_ref, far_ref, tile_ref) = refs[:parts], refs[parts:]
    _, rows, _, count, _ = b_ref.shape
    sites = 2 * count
    top = rows - 1
    half = lax.rem(lax.axis_index("quad"), 2)
    mine = lax.axis_index("rows")
    tail = 2 * rows
    even = lax.rem(mine, 2) == 0
    size = shared(count)

    def arrived(start, size):
        one, two = first_ref[pl.ds(start, size), :], second_ref[pl.ds(start, size), :]
        return jnp.where(even, two, one), jnp.where(even, one, two)

    for part in range(sites // LANES):
        for slot, value in enumerate(arrived(2 * count + size + part * tail, tail)):
            far_ref[slot, pl.ds(part * LANES, LANES), :tail] = value.T

    outside = [(i, p) for i in (0, top) for p in range(2)]
    aid = {i: [aid_ref[index, n] for n in range(7)] for index, i in enumerate((0, top))}
    scale = {(i, p): aid[i][p] for i, p in outside}
    level = {(i, p): aid[i][2 + p] for i, p in outside}
    b = {k: b_ref[half, k[0], k[1]] for k in outside}
    w1 = {k: w_in_ref[0, k[0], k[1]] for k in outside}
    below0, above0 = zip(arrived(0, count), arrived(count, count))
    w1[0, 1] = w1[0, 1] - scale[0, 1] * below0[1]
    w1[top, 1] = w1[top, 1] - scale[top, 1] * above0[1]
    u1 = {k: scale[k] * w1[k] for k in outside}

    missing = jnp.zeros((count - size, LANES), F32)
    low, high = arrived(2 * count, size)
    edge_next = {0: jnp.concatenate([missing, low], axis=0), top: jnp.concatenate([high, missing], axis=0)}
    edge_w2, far_w2 = {}, {}
    for i, halo, slot, row in ((0, below0, 0, top), (top, above0, 1, 0)):
        far_table = far_ref.at[slot]
        square = [spread(far_table, p, row) for p in range(2)]
        square = [x * x for x in square]
        far_level = [spread(far_table, p, rows + row) for p in range(2)]
        sums = horizontal(halo[0], halo[1])
        far1 = [
            far_level[0] * halo[0] - square[0] * (sums[0] + edge_next[i]),
            far_level[1] * halo[1] - square[1] * (sums[1] + aid[i][4]),
        ]
        sums = horizontal(u1[i, 0], u1[i, 1])
        edge_w2[i, 0] = level[i, 0] * w1[i, 0] - scale[i, 0] * (sums[0] + aid[i][5])
        edge_w2[i, 1] = level[i, 1] * w1[i, 1] - scale[i, 1] * (sums[1] + far1[1])
        sums = horizontal(far1[0], far1[1])
        far_w2[i] = far_level[1] * far1[1] - square[1] * (sums[1] + u1[i, 1])
    w2 = edge_w2
    site = lax.broadcasted_iota(jnp.int32, (count, LANES), 0)
    counted = {0: site >= count // 2, top: site < count // 2}
    pairs = bonds(scale, w2, (0,))
    pairs.update(bonds(scale, w2, (top,)))
    for i in (0, top):
        pairs[i, 0] = pairs[i, 0] + scale[i, 0] * w2[i, 0] * aid[i][6]
        pairs[i, 1] = pairs[i, 1] + scale[i, 1] * w2[i, 1] * jnp.where(counted[i], far_w2[i], 0.0)

    mu = [
        total([b[k] * w1[k] for k in outside]),
        total([w1[k] * w1[k] for k in outside]),
        total([w1[k] * w2[k] for k in outside]),
        total([w2[k] * w2[k] for k in outside]),
        total([level[k] * w2[k] * w2[k] - 2.0 * pairs[k] for k in outside]),
    ]
    zero = jnp.zeros((1, LANES), F32)
    mu = joined(
        mu_in_ref[...],
        jnp.concatenate([zero] + [x[0] for x in mu] + [zero - LARGE] * 2 + [zero] + [x[1] for x in mu] + [zero] * 2, axis=0),
    )
    for i, p in [(i, p) for i in range(rows) for p in range(2)]:
        w_ref[0, i, p] = w1[i, p] if (i, p) in w1 else w_in_ref[0, i, p]
        w_ref[1, i, p] = w2[i, p] if (i, p) in w2 else w_in_ref[1, i, p]
    right_hi, right_lo = split(
        jnp.concatenate([jnp.concatenate([w1[k], w2[k]], axis=1) for k in outside], axis=0)
    )
    more = triple(left_hi_ref[...], left_lo_ref[...], right_hi, right_lo)
    row = lax.broadcasted_iota(jnp.int32, (LANES, LANES), 0)
    lane = lax.broadcasted_iota(jnp.int32, (LANES, LANES), 1)
    for j in range(3):
        lanes = slice(j * LANES, (j + 1) * LANES)
        first, second = gram_ref[:LANES, lanes], gram_ref[LANES:, lanes]
        if j:
            lanes = slice((j - 1) * LANES, j * LANES)
            first, second = first + more[:LANES, lanes], second + more[LANES:, lanes]
        own = jnp.where(half == 0, first, second)
        cross = jnp.where(half == 0, second, first)
        tile_ref[pl.ds(j * LANES, LANES), :] = jnp.where(row < lane, own, cross)
    size = 3 * LANES // parts
    for part, ref in enumerate(chunk_refs):
        start = pl.multiple_of((mine ^ part) * size if parts > 1 else 0, 8)
        ref[pl.ds(0, size), :] = tile_ref[pl.ds(start, size), :]
        ref[pl.ds(size, MU_ROWS), :] = mu


def sum_kernel(size, *refs):
    *shares, out_ref = refs
    at, tail = pl.ds(0, size), pl.ds(size, MU_ROWS)
    out_ref[at, :] = (shares[0][at, :] + shares[1][at, :]) + (shares[2][at, :] + shares[3][at, :])
    out_ref[tail, :] = joined(
        joined(shares[0][tail, :], shares[1][tail, :]), joined(shares[2][tail, :], shares[3][tail, :])
    )


def moments_kernel(points, b_ref, w_ref, v_ref, mu_ref, nu_ref, out_ref, coef_ref, made_ref, out_sem):
    quad = lax.axis_index("quad")
    half = lax.rem(quad, 2)
    _, rows, _, count, _ = b_ref.shape
    first = jnp.where(half == 0, mu_ref[...], nu_ref[...])
    second = jnp.where(half == 0, nu_ref[...], mu_ref[...])
    mu = jnp.concatenate([first, second], axis=1)
    coefs = coefficients(mu, points, (quad + 1).astype(F32))
    lines = [line for part in coefs for line in part]
    coef_ref[...] = jnp.concatenate(lines + [jnp.zeros_like(lines[0])] * 2, axis=0)
    stores = []
    for i in range(rows):
        for side in range(2):
            lanes = slice(side * LANES, (side + 1) * LANES)
            for p in range(2):
                fields = [b_ref[side, i, p]]
                fields += [jnp.where(half == side, w_ref[j, i, p], v_ref[j, i, p]) for j in range(2)]
                for part in range(2):
                    terms = [lines[3 * part + j][:, lanes] * fields[j] for j in range(3)]
                    made_ref[part, i, side, pl.ds(p, count, stride=2), :] = terms[0] + terms[1] + terms[2]
            for part in range(2):
                copy = pltpu.make_async_copy(
                    made_ref.at[part, i, side],
                    out_ref.at[0, part, i, :, pl.ds(side * LANES, LANES)],
                    out_sem.at[part, i, side],
                )
                copy.start()
                stores.append(copy)
    for copy in stores:
        copy.wait()


def tile_blocks(half, tile, mu):
    row = lax.broadcasted_iota(jnp.int32, (LANES, LANES), 0)
    lane = lax.broadcasted_iota(jnp.int32, (LANES, LANES), 1)
    flip = tile.T
    same = jnp.where(row < lane, tile, jnp.where(row > lane, flip, mu))
    below = jnp.where(half == 0, jnp.where(row >= lane, tile, 0.0), jnp.where(row < lane, flip, 0.0))
    above = jnp.where(half == 0, jnp.where(row <= lane, flip, 0.0), jnp.where(row > lane, tile, 0.0))
    return same, below, above


def gather(parts, tile_ref, chunk_refs):
    size = 3 * LANES // parts
    for part, ref in zip([0, *range(parts - 1, 0, -1)], chunk_refs):
        start = pl.multiple_of((lax.axis_index("rows") ^ part) * size if parts > 1 else 0, 8)
        tile_ref[pl.ds(start, size), :] = ref[pl.ds(0, size), :]


def weighted(parts, orbitals, half, coef_ref, mu_ref, tile_ref):
    sums = {}
    for j in range(3):
        blocks = tile_blocks(half, tile_ref[j * LANES : (j + 1) * LANES, :], mu_ref[j : j + 1, :])
        for part in range(2):
            line = coef_ref[3 * part + j : 3 * part + j + 1, :] * F32(1.0 / orbitals)
            first, second = line[:, :LANES], line[:, LANES:]
            own = jnp.where(half == 0, first, second)
            for which, (lane_coef, value) in enumerate(zip((own, first, second), blocks)):
                term = lane_coef * value
                sums[part, which] = term if j == 0 else sums[part, which] + term
    return sums


def own_kernel(parts, orbitals, coef_ref, mu_ref, *refs):
    chunk_refs, (out_ref, tile_ref) = refs[:parts], refs[parts:]
    half = lax.rem(lax.axis_index("quad"), 2)
    gather(parts, tile_ref, chunk_refs)
    for (part, which), value in weighted(parts, orbitals, half, coef_ref, mu_ref, tile_ref).items():
        out_ref[part, which] = value


def far_kernel(parts, orbitals, coef_ref, mu_ref, own_ref, *refs):
    chunk_refs, (out_ref, tile_ref, made_ref, sem) = refs[:parts], refs[parts:]
    half = lax.rem(lax.axis_index("quad"), 2)
    gather(parts, tile_ref, chunk_refs)
    sums = weighted(parts, orbitals, 1 - half, coef_ref, mu_ref, tile_ref)
    copies = []
    for part in range(2):
        same = [own_ref[part, 0], sums[part, 0]]
        blocks = {
            (0, 0): jnp.where(half == 0, same[0], same[1]),
            (0, 1): own_ref[part, 2] + sums[part, 2],
            (1, 0): own_ref[part, 1] + sums[part, 1],
            (1, 1): jnp.where(half == 0, same[1], same[0]),
        }
        for (x, y), value in blocks.items():
            made_ref[part, x * LANES : (x + 1) * LANES, y * LANES : (y + 1) * LANES] = value
        copies.append(pltpu.make_async_copy(made_ref.at[part], out_ref.at[0, part], sem.at[part]))
        copies[-1].start()
    for copy in copies:
        copy.wait()


def struct(*shape, dtype=F32):
    return jax.ShapeDtypeStruct(shape, dtype)


def cost(flops, nbytes):
    return pl.CostEstimate(flops=flops, bytes_accessed=nbytes, transcendentals=0)


def body(sources, onsite, strain, present):
    n_rows = lax.axis_size("rows")
    n_quad = lax.axis_size("quad")
    points = PTS_DEV * n_quad
    rows, sites, columns = sources.shape
    count = sites // 2
    orbitals = rows * sites * n_rows
    tail = 2 * rows * (sites // LANES)
    payload = 2 * count + shared(count) + tail
    first, second, table = pl.pallas_call(
        edges_kernel,
        out_shape=(struct(payload, LANES), struct(payload, LANES), struct(sites, LANES)),
        in_specs=[HBM] * 4,
        out_specs=(VMEM, VMEM, VMEM),
        scratch_shapes=[
            pltpu.VMEM((4, sites, LANES), F32),
            pltpu.VMEM((rows, sites), F32),
            pltpu.VMEM((rows, sites), F32),
            pltpu.VMEM((rows, sites), jnp.int32),
            pltpu.SemaphoreType.DMA((7,)),
        ],
        compiler_params=PARAMS,
        name="edges",
    )(*(pltpu.with_memory_space_constraint(x, pltpu.HBM) for x in (sources, onsite, strain, present)))
    halo = []
    for value, start in ((first, 0), (second, 1)):
        bonds = [(i, i + 1) for i in range(start, n_rows - 1, 2)]
        halo.append(lax.ppermute(value, "rows", bonds + [(j, i) for i, j in bonds]))
    outer_depth = 4 * count
    inner = pl.pallas_call(
        inner_kernel,
        out_shape=(
            struct(2, rows, 2, count, LANES),
            struct(2, rows, 2, count, LANES),
            struct(2, 7, count, LANES),
            struct(MU_ROWS, LANES),
            struct(columns, 3 * LANES),
            struct(columns, outer_depth, dtype=BF16),
            struct(columns, outer_depth, dtype=BF16),
        ),
        in_specs=[ANY, VMEM],
        out_specs=(VMEM,) * 7,
        scratch_shapes=[pltpu.VMEM((2, rows, sites, LANES), F32), pltpu.SemaphoreType.DMA((2,))],
        compiler_params=PARAMS,
        cost_estimate=cost(10**9, 8 * 2**20),
        name="inner",
    )(sources, table)
    b_all = inner[0]

    pairwise = n_rows == 4
    parts = n_rows if pairwise else 1
    far_first = list(range(parts - 1, 0, -1))
    size = 3 * LANES // parts
    *chunks, fields = pl.pallas_call(
        functools.partial(outer_kernel, parts),
        out_shape=(struct(size + MU_ROWS, LANES),) * parts + (struct(2, rows, 2, count, LANES),),
        in_specs=[VMEM] * 9,
        out_specs=(VMEM,) * (parts + 1),
        scratch_shapes=[pltpu.VMEM((2, sites, LANES), F32), pltpu.VMEM((3 * LANES, LANES), F32)],
        compiler_params=PARAMS,
        cost_estimate=cost(4 * 10**8, 4 * 2**20),
        name="outer",
    )(*inner, *halo)

    def partner(value):
        return lax.ppermute(value, "quad", [(i, i ^ 1) for i in range(n_quad)])

    def across(value, mask):
        return lax.ppermute(value, "rows", [(i, i ^ mask) for i in range(n_rows)])

    if pairwise:
        summed = pl.pallas_call(
            functools.partial(sum_kernel, size),
            out_shape=struct(size + MU_ROWS, LANES),
            in_specs=[VMEM] * parts,
            out_specs=VMEM,
            compiler_params=PARAMS,
            cost_estimate=cost(10**5, 2**18),
            name="sum",
        )(chunks[0], *(across(chunks[mask], mask) for mask in far_first))
        sums = [summed[:size]] + [across(summed[:size], mask) for mask in far_first]
    else:
        shares = lax.all_gather(chunks[0][size:], "rows")
        mu = functools.reduce(joined, [shares[n] for n in range(n_rows)])
        summed = jnp.concatenate([lax.psum(chunks[0][:size], "rows"), mu], axis=0)
        sums = [summed[:size]]
    summed, fields = lax.optimization_barrier((summed, fields))
    far_summed = partner(summed)
    far_fields = partner(fields)
    mu, far_mu = summed[size:], far_summed[size:]
    far_sums = [far_summed[:size]]
    moments, coefs = pl.pallas_call(
        functools.partial(moments_kernel, points),
        out_shape=(struct(1, 2, rows, sites, columns), struct(8, columns)),
        in_specs=[VMEM] * 5,
        out_specs=(ANY, VMEM),
        scratch_shapes=[pltpu.VMEM((2, rows, 2, sites, LANES), F32), pltpu.SemaphoreType.DMA((2, rows, 2))],
        compiler_params=PARAMS,
        cost_estimate=cost(10**7, 8 * 2**20),
        name="moments",
    )(b_all, fields, far_fields, mu, far_mu)
    *late, coefs = lax.optimization_barrier((*sums[2:], coefs))
    sums = sums[:2] + late
    far_sums += [partner(value) for value in sums[1:]]
    own = pl.pallas_call(
        functools.partial(own_kernel, parts, orbitals),
        out_shape=struct(2, 3, LANES, LANES),
        in_specs=[VMEM] * (2 + parts),
        out_specs=VMEM,
        scratch_shapes=[pltpu.VMEM((3 * LANES, LANES), F32)],
        compiler_params=PARAMS,
        cost_estimate=cost(10**6, 2**20),
        name="own",
    )(coefs, mu, *sums)
    reduced = pl.pallas_call(
        functools.partial(far_kernel, parts, orbitals),
        out_shape=struct(1, 2, columns, columns),
        in_specs=[VMEM] * (3 + parts),
        out_specs=ANY,
        scratch_shapes=[
            pltpu.VMEM((3 * LANES, LANES), F32),
            pltpu.VMEM((2, columns, columns), F32),
            pltpu.SemaphoreType.DMA((2,)),
        ],
        compiler_params=PARAMS,
        cost_estimate=cost(10**6, 2**20),
        name="reduced",
    )(coefs, far_mu, own, *far_sums)
    return moments, reduced


def solution(mesh):
    in_specs = (
        P(("groups", "rows"), None, None),
        P(("groups", "rows"), None),
        P(("groups", "rows"), None),
        P(("groups", "rows"), None),
    )
    out_specs = (P("quad", None, ("groups", "rows"), None, None), P("quad", None, "groups", None))
    return jax.shard_map(body, mesh=mesh, in_specs=in_specs, out_specs=out_specs, check_vma=False)
```

```python
import functools
import math

import jax
import jax.numpy as jnp
from jax import lax
from jax.experimental import pallas as pl
from jax.experimental.pallas import tpu as pltpu
from jax.sharding import PartitionSpec as P

TOTAL_PTS = 32
PTS_DEV = 2
CENTER = 0.4
RADIUS = 1.0
MU_ROWS = 16
LANES = 128
LARGE = 1e30
F32 = jnp.float32
BF16 = jnp.bfloat16
PARAMS = pltpu.CompilerParams(vmem_limit_bytes=32 * 1024 * 1024)
VMEM = pl.BlockSpec(memory_space=pltpu.VMEM)
HBM = pl.BlockSpec(memory_space=pltpu.HBM)
ANY = pl.BlockSpec(memory_space=pl.ANY)


def ratio(top, bottom, good):
    return jnp.where(good, top / jnp.where(good, bottom, 1.0), 0.0)


def cmul(a, b):
    return (a[0] * b[0] - a[1] * b[1], a[0] * b[1] + a[1] * b[0])


def inverse(a):
    size = a[0] * a[0] + a[1] * a[1]
    return (a[0] / size, -a[1] / size)


def two_sum(a, b):
    total = a + b
    part = total - a
    return total, (a - (total - part)) + (b - part)


def pair_add(a, b):
    total, rest = two_sum(a[0], b[0])
    return two_sum(total, rest + (a[1] + b[1]))


def halves(a):
    scaled = F32(4097.0) * a
    high = scaled - (scaled - a)
    return high, a - high


def pair_times(a, b):
    product = a[0] * b
    (ah, al), (bh, bl) = halves(a[0]), halves(b)
    rest = ((ah * bh - product) + ah * bl + al * bh) + al * bl
    return two_sum(product, rest + a[1] * b)


def coefficients(block, points, order):
    line = [block[n : n + 1] for n in range(MU_ROWS)]
    mu = [(line[n], line[8 + n]) for n in range(6)]
    ok0 = line[0] > 0
    reach = 3.0 * line[14] * line[14]
    top, bottom = line[6] + reach, -line[7] - reach
    centre = jnp.clip(ratio(line[1], line[0], ok0), bottom, top)
    central = [mu[0]]
    level = mu
    for _ in range(5):
        level = [
            pair_add(after, tuple(-x for x in pair_times(now, centre))) for now, after in zip(level[:-1], level[1:])
        ]
        central.append(level[0])
    m0, m1, m2, m3, m4, m5 = (x[0] + x[1] for x in central)
    tiny = F32(1e-7)
    low, high = bottom - centre, top - centre
    a0 = jnp.clip(ratio(m1, m0, ok0), low, high)
    s11 = m2 - a0 * m1
    s12 = m3 - a0 * m2
    s13 = m4 - a0 * m3
    s14 = m5 - a0 * m4
    ok1 = ok0 & (s11 > tiny * m2)
    widest = 0.25 * (high - low) * (high - low)
    b1 = jnp.clip(ratio(s11, m0, ok1), 0.0, widest)
    g1 = ratio(s12, s11, ok1)
    a1 = jnp.clip(jnp.where(ok1, g1 - a0, a0), low, high)
    s22 = s13 - a1 * s12 - b1 * m2
    s23 = s14 - a1 * s13 - b1 * m3
    ok2 = ok1 & (s22 > tiny * m4)
    b2 = jnp.clip(ratio(s22, s11, ok2), 0.0, widest)
    a2 = jnp.clip(jnp.where(ok2, ratio(s23, s22, ok2) - g1, a1), low, high)
    a0, a1, a2 = a0 + centre, a1 + centre, a2 + centre
    leading = TOTAL_PTS // 4 - points // 2
    p = lax.broadcasted_iota(jnp.int32, (points, m0.shape[1]), 0).astype(F32)
    angle = 2.0 * math.pi * (p + leading + 0.5) / TOTAL_PTS
    zr = CENTER + RADIUS * jnp.cos(angle)
    zi = RADIUS * jnp.sin(angle)
    wr = RADIUS / points * jnp.cos(order * angle)
    wi = RADIUS / points * jnp.sin(order * angle)
    i2 = inverse((zr - a2, zi))
    i1 = inverse((zr - a1 - b2 * i2[0], zi - b2 * i2[1]))
    y0 = inverse((zr - a0 - b1 * i1[0], zi - b1 * i1[1]))
    y0 = cmul((wr, wi), y0)
    y1 = cmul(y0, i1)
    y2 = cmul(y1, i2)
    out = []
    for part in range(2):
        t0, t1, t2 = (jnp.sum(y[part], axis=0, keepdims=True) for y in (y0, y1, y2))
        out.append((t0 - a0 * t1 + (a0 * a1 - b1) * t2, t1 - (a0 + a1) * t2, t2))
    return out


def spread(table_ref, parity, lane):
    half = table_ref.shape[0] // 2
    rows = table_ref[pl.ds(parity, half, stride=2), :]
    return jnp.broadcast_to(rows[:, lane : lane + 1], (half, LANES))


def horizontal(even, odd):
    size = even.shape[0]
    site = lax.broadcasted_iota(jnp.int32, even.shape, 0)
    left = jnp.where(site == 0, 0.0, pltpu.roll(odd, 1, 0))
    right = jnp.where(site == size - 1, 0.0, pltpu.roll(even, size - 1, 0))
    return odd + left, even + right


def site_table(onsite, strain, present):
    return jnp.concatenate([present.astype(F32) * strain, onsite], axis=0)


def bound_up(i, p):
    return (i + p) % 2 == 0


def fold(value):
    tiles = value.reshape(value.shape[0] // 32, 4, 8, value.shape[1])
    return [tiles[n, 0] + tiles[n, 1] + (tiles[n, 2] + tiles[n, 3]) for n in range(tiles.shape[0])]


def total(terms):
    first, *others = [part for term in terms for part in fold(term)]
    whole = (first, jnp.zeros((8, LANES), F32))
    for part in others:
        high, rest = two_sum(whole[0], part)
        whole = (high, whole[1] + rest)
    for size in (4, 2, 1):
        whole = pair_add(*((whole[0][k : k + size], whole[1][k : k + size]) for k in (0, size)))
    return whole


def joined(one, two):
    high, rest = two_sum(one[:8], two[:8])
    high, rest = two_sum(high, rest + (one[8:] + two[8:]))
    row = lax.broadcasted_iota(jnp.int32, high.shape, 0)
    return jnp.concatenate(
        [jnp.where(row < 6, high, jnp.maximum(one[:8], two[:8])), jnp.where(row < 6, rest, jnp.maximum(one[8:], two[8:]))],
        axis=0,
    )


def split(value):
    high = value.astype(BF16)
    return high, (value - high.astype(F32)).astype(BF16)


def edges_kernel(
    sources_ref, onsite_ref, strain_ref, present_ref, first_ref, second_ref, table_ref,
    rows_ref, onsite_in, strain_in, present_in, sem,
):
    rows, sites, _ = sources_ref.shape
    count = sites // 2
    columns = pl.ds(pl.multiple_of(lax.rem(lax.axis_index("quad"), 2) * LANES, LANES), LANES)
    pairs = [(onsite_ref, onsite_in), (strain_ref, strain_in), (present_ref, present_in)]
    for start, slot in ((0, 0), (rows - 2, 2)):
        pairs.append((sources_ref.at[pl.ds(start, 2), :, columns], rows_ref.at[pl.ds(slot, 2)]))
    copies = [pltpu.make_async_copy(src, dst, sem.at[k]) for k, (src, dst) in enumerate(pairs)]
    for copy in copies:
        copy.start()
    for copy in copies[:3]:
        copy.wait()
    table = site_table(onsite_in[...], strain_in[...], present_in[...])
    tail = table.shape[0]
    table_ref[:, :tail] = table.T
    for part in range(sites // LANES):
        at = pl.ds(2 * count + shared(count) + part * tail, tail)
        first_ref[at, :] = second_ref[at, :] = table[:, part * LANES : (part + 1) * LANES]
    for copy in copies[3:]:
        copy.wait()

    def scaled(slot, row, parity):
        return rows_ref[slot, pl.ds(parity, count, stride=2), :] * spread(table_ref, parity, row)

    size = shared(count)
    up = [scaled(3, rows - 1, 0), scaled(3, rows - 1, 1), scaled(2, rows - 2, 0)[count - size :]]
    down = [scaled(0, 0, 0), scaled(0, 0, 1), scaled(1, 1, 0)[:size]]
    even = lax.rem(lax.axis_index("rows"), 2) == 0
    for block in range(3):
        at = pl.ds(block * count, up[block].shape[0])
        first_ref[at, :] = jnp.where(even, up[block], down[block])
        second_ref[at, :] = jnp.where(even, down[block], up[block])


def shared(count):
    return count // 2 + 8


def near(u, wanted, up_halo, down_halo, top):
    out = {}
    for i in wanted:
        sums = horizontal(u[i, 0], u[i, 1])
        for p in range(2):
            if bound_up(i, p):
                other = u[i + 1, p] if i < top else up_halo
            else:
                other = u[i - 1, p] if i > 0 else down_halo
            out[i, p] = sums[p] if other is None else sums[p] + other
    return out


def bonds(scale, w, wanted):
    u = {(i, p): scale[i, p] * w[i, p] for i in wanted for p in range(2)}
    out = {}
    for i in wanted:
        out[i, 0] = u[i, 0] * horizontal(u[i, 0], u[i, 1])[0]
        out[i, 1] = jnp.zeros_like(u[i, 1])
        for p in range(2):
            if bound_up(i, p) and (i + 1, p) in u:
                out[i, p] = out[i, p] + u[i, p] * u[i + 1, p]
    return out


def beside(i, top):
    return (1, 0) if i == 0 else (top - 1, 0)


def inner_kernel(sources_ref, table_ref, b_ref, w_ref, aid_ref, mu_ref, gram_ref, left_hi_ref, left_lo_ref, full_ref, sem):
    rows, sites, _ = sources_ref.shape
    count = sites // 2
    top = rows - 1
    half = lax.rem(lax.axis_index("quad"), 2)
    copies = [
        pltpu.make_async_copy(sources_ref.at[:, :, pl.ds(side * LANES, LANES)], full_ref.at[side], sem.at[side])
        for side in range(2)
    ]
    for copy in copies:
        copy.start()
    for copy in copies:
        copy.wait()
    keys = [(i, p) for i in range(rows) for p in range(2)]
    for side in range(2):
        for i, p in keys:
            b_ref[side, i, p] = full_ref[side, i, pl.ds(p, count, stride=2), :]
    scale = {(i, p): spread(table_ref, p, i) for i, p in keys}
    level = {(i, p): spread(table_ref, p, rows + i) for i, p in keys}
    b = {(i, p): b_ref[half, i, p] for i, p in keys}
    u0 = {k: scale[k] * b[k] for k in keys}
    n0 = near(u0, range(rows), None, None, top)
    w1 = {k: level[k] * b[k] - scale[k] * n0[k] for k in keys}
    for i, p in keys:
        w_ref[0, i, p] = w1[i, p]
    u1 = {k: scale[k] * w1[k] for k in keys}
    inside = [(i, p) for i, p in keys if 0 < i < top]
    n1 = near(u1, range(1, top), None, None, top)
    w2 = {k: level[k] * w1[k] - scale[k] * n1[k] for k in inside}
    for i, p in inside:
        w_ref[1, i, p] = w2[i, p]
    for index, i in enumerate((0, top)):
        for p in range(2):
            aid_ref[index, p] = scale[i, p]
            aid_ref[index, 2 + p] = level[i, p]
        k = beside(i, top)
        aid_ref[index, 4] = u0[i, 1]
        aid_ref[index, 5] = u1[k]
        aid_ref[index, 6] = scale[k] * w2[k]
    mu = [
        total([b[k] * b[k] for k in keys]),
        total([b[k] * w1[k] for k in inside]),
        total([w1[k] * w1[k] for k in inside]),
        total([w1[k] * w2[k] for k in inside]),
        total([w2[k] * w2[k] for k in inside]),
        total([level[k] * w2[k] * w2[k] - 2.0 * x for k, x in bonds(scale, w2, range(1, top)).items()]),
    ]
    table = table_ref[...]
    lane = lax.broadcasted_iota(jnp.int32, table.shape, 1)
    scales = jnp.max(jnp.where(lane < rows, table, 0.0), keepdims=True)
    is_level = (lane >= rows) & (lane < 2 * rows)
    most = jnp.max(jnp.where(is_level, table, -LARGE), keepdims=True)
    least = jnp.max(jnp.where(is_level, -table, -LARGE), keepdims=True)
    limits = [jnp.broadcast_to(x, (1, LANES)) for x in (most, least, scales)]
    mu_ref[...] = jnp.concatenate(
        [x[0] for x in mu] + limits[:2] + [x[1] for x in mu] + [limits[2], jnp.zeros((1, LANES), F32)], axis=0
    )
    order = inside + [k for k in keys if k not in inside]
    left = jnp.concatenate([jnp.concatenate([b_ref[0, i, p], b_ref[1, i, p]], axis=1) for i, p in order], axis=0)
    left_hi, left_lo = (x.T for x in split(left))
    own_hi, own_lo = split(jnp.concatenate([b[k] for k in order], axis=0))
    depth = len(inside) * count
    in_hi, in_lo = split(
        jnp.concatenate([jnp.concatenate([w1[k], w2[k]], axis=1) for k in inside], axis=0)
    )
    gram_ref[:, :LANES] = triple(left_hi, left_lo, own_hi, own_lo)
    gram_ref[:, LANES:] = triple(left_hi[:, :depth], left_lo[:, :depth], in_hi, in_lo)
    left_hi_ref[...] = left_hi[:, depth:]
    left_lo_ref[...] = left_lo[:, depth:]


def triple(left_hi, left_lo, right_hi, right_lo):
    def product(left, right):
        return jnp.dot(left, right, preferred_element_type=F32)

    return product(left_hi, right_hi) + (product(left_hi, right_lo) + product(left_lo, right_hi))


def outer_kernel(
    parts, b_ref, w_in_ref, aid_ref, mu_in_ref, gram_ref, left_hi_ref, left_lo_ref, first_ref, second_ref, *refs
):
    chunk_refs, (w_ref, far_ref, tile_ref) = refs[:parts], refs[parts:]
    _, rows, _, count, _ = b_ref.shape
    sites = 2 * count
    top = rows - 1
    half = lax.rem(lax.axis_index("quad"), 2)
    mine = lax.axis_index("rows")
    tail = 2 * rows
    even = lax.rem(mine, 2) == 0
    size = shared(count)

    def arrived(start, size):
        one, two = first_ref[pl.ds(start, size), :], second_ref[pl.ds(start, size), :]
        return jnp.where(even, two, one), jnp.where(even, one, two)

    for part in range(sites // LANES):
        for slot, value in enumerate(arrived(2 * count + size + part * tail, tail)):
            far_ref[slot, pl.ds(part * LANES, LANES), :tail] = value.T

    outside = [(i, p) for i in (0, top) for p in range(2)]
    aid = {i: [aid_ref[index, n] for n in range(7)] for index, i in enumerate((0, top))}
    scale = {(i, p): aid[i][p] for i, p in outside}
    level = {(i, p): aid[i][2 + p] for i, p in outside}
    b = {k: b_ref[half, k[0], k[1]] for k in outside}
    w1 = {k: w_in_ref[0, k[0], k[1]] for k in outside}
    below0, above0 = zip(arrived(0, count), arrived(count, count))
    w1[0, 1] = w1[0, 1] - scale[0, 1] * below0[1]
    w1[top, 1] = w1[top, 1] - scale[top, 1] * above0[1]
    u1 = {k: scale[k] * w1[k] for k in outside}

    missing = jnp.zeros((count - size, LANES), F32)
    low, high = arrived(2 * count, size)
    edge_next = {0: jnp.concatenate([missing, low], axis=0), top: jnp.concatenate([high, missing], axis=0)}
    edge_w2, far_w2 = {}, {}
    for i, halo, slot, row in ((0, below0, 0, top), (top, above0, 1, 0)):
        far_table = far_ref.at[slot]
        square = [spread(far_table, p, row) for p in range(2)]
        square = [x * x for x in square]
        far_level = [spread(far_table, p, rows + row) for p in range(2)]
        sums = horizontal(halo[0], halo[1])
        far1 = [
            far_level[0] * halo[0] - square[0] * (sums[0] + edge_next[i]),
            far_level[1] * halo[1] - square[1] * (sums[1] + aid[i][4]),
        ]
        sums = horizontal(u1[i, 0], u1[i, 1])
        edge_w2[i, 0] = level[i, 0] * w1[i, 0] - scale[i, 0] * (sums[0] + aid[i][5])
        edge_w2[i, 1] = level[i, 1] * w1[i, 1] - scale[i, 1] * (sums[1] + far1[1])
        sums = horizontal(far1[0], far1[1])
        far_w2[i] = far_level[1] * far1[1] - square[1] * (sums[1] + u1[i, 1])
    w2 = edge_w2
    site = lax.broadcasted_iota(jnp.int32, (count, LANES), 0)
    counted = {0: site >= count // 2, top: site < count // 2}
    pairs = bonds(scale, w2, (0,))
    pairs.update(bonds(scale, w2, (top,)))
    for i in (0, top):
        pairs[i, 0] = pairs[i, 0] + scale[i, 0] * w2[i, 0] * aid[i][6]
        pairs[i, 1] = pairs[i, 1] + scale[i, 1] * w2[i, 1] * jnp.where(counted[i], far_w2[i], 0.0)

    mu = [
        total([b[k] * w1[k] for k in outside]),
        total([w1[k] * w1[k] for k in outside]),
        total([w1[k] * w2[k] for k in outside]),
        total([w2[k] * w2[k] for k in outside]),
        total([level[k] * w2[k] * w2[k] - 2.0 * pairs[k] for k in outside]),
    ]
    zero = jnp.zeros((1, LANES), F32)
    mu = joined(
        mu_in_ref[...],
        jnp.concatenate([zero] + [x[0] for x in mu] + [zero - LARGE] * 2 + [zero] + [x[1] for x in mu] + [zero] * 2, axis=0),
    )
    for i, p in [(i, p) for i in range(rows) for p in range(2)]:
        w_ref[0, i, p] = w1[i, p] if (i, p) in w1 else w_in_ref[0, i, p]
        w_ref[1, i, p] = w2[i, p] if (i, p) in w2 else w_in_ref[1, i, p]
    right_hi, right_lo = split(
        jnp.concatenate([jnp.concatenate([w1[k], w2[k]], axis=1) for k in outside], axis=0)
    )
    more = triple(left_hi_ref[...], left_lo_ref[...], right_hi, right_lo)
    row = lax.broadcasted_iota(jnp.int32, (LANES, LANES), 0)
    lane = lax.broadcasted_iota(jnp.int32, (LANES, LANES), 1)
    for j in range(3):
        lanes = slice(j * LANES, (j + 1) * LANES)
        first, second = gram_ref[:LANES, lanes], gram_ref[LANES:, lanes]
        if j:
            lanes = slice((j - 1) * LANES, j * LANES)
            first, second = first + more[:LANES, lanes], second + more[LANES:, lanes]
        own = jnp.where(half == 0, first, second)
        cross = jnp.where(half == 0, second, first)
        tile_ref[pl.ds(j * LANES, LANES), :] = jnp.where(row < lane, own, cross)
    size = 3 * LANES // parts
    for part, ref in enumerate(chunk_refs):
        start = pl.multiple_of((mine ^ part) * size if parts > 1 else 0, 8)
        ref[pl.ds(0, size), :] = tile_ref[pl.ds(start, size), :]
        ref[pl.ds(size, MU_ROWS), :] = mu


def sum_kernel(size, *refs):
    *shares, out_ref = refs
    at, tail = pl.ds(0, size), pl.ds(size, MU_ROWS)
    out_ref[at, :] = (shares[0][at, :] + shares[1][at, :]) + (shares[2][at, :] + shares[3][at, :])
    out_ref[tail, :] = joined(
        joined(shares[0][tail, :], shares[1][tail, :]), joined(shares[2][tail, :], shares[3][tail, :])
    )


def moments_kernel(points, b_ref, w_ref, v_ref, mu_ref, nu_ref, out_ref, coef_ref, made_ref, out_sem):
    quad = lax.axis_index("quad")
    half = lax.rem(quad, 2)
    _, rows, _, count, _ = b_ref.shape
    first = jnp.where(half == 0, mu_ref[...], nu_ref[...])
    second = jnp.where(half == 0, nu_ref[...], mu_ref[...])
    mu = jnp.concatenate([first, second], axis=1)
    coefs = coefficients(mu, points, (quad + 1).astype(F32))
    lines = [line for part in coefs for line in part]
    coef_ref[...] = jnp.concatenate(lines + [jnp.zeros_like(lines[0])] * 2, axis=0)
    stores = []
    for i in range(rows):
        for side in range(2):
            lanes = slice(side * LANES, (side + 1) * LANES)
            for p in range(2):
                fields = [b_ref[side, i, p]]
                fields += [jnp.where(half == side, w_ref[j, i, p], v_ref[j, i, p]) for j in range(2)]
                for part in range(2):
                    terms = [lines[3 * part + j][:, lanes] * fields[j] for j in range(3)]
                    made_ref[part, i, side, pl.ds(p, count, stride=2), :] = terms[0] + terms[1] + terms[2]
            for part in range(2):
                copy = pltpu.make_async_copy(
                    made_ref.at[part, i, side],
                    out_ref.at[0, part, i, :, pl.ds(side * LANES, LANES)],
                    out_sem.at[part, i, side],
                )
                copy.start()
                stores.append(copy)
    for copy in stores:
        copy.wait()


def tile_blocks(half, tile, mu):
    row = lax.broadcasted_iota(jnp.int32, (LANES, LANES), 0)
    lane = lax.broadcasted_iota(jnp.int32, (LANES, LANES), 1)
    flip = tile.T
    same = jnp.where(row < lane, tile, jnp.where(row > lane, flip, mu))
    below = jnp.where(half == 0, jnp.where(row >= lane, tile, 0.0), jnp.where(row < lane, flip, 0.0))
    above = jnp.where(half == 0, jnp.where(row <= lane, flip, 0.0), jnp.where(row > lane, tile, 0.0))
    return same, below, above


def gather(parts, tile_ref, chunk_refs):
    size = 3 * LANES // parts
    for part, ref in zip(range(parts), chunk_refs):
        start = pl.multiple_of((lax.axis_index("rows") ^ part) * size if parts > 1 else 0, 8)
        tile_ref[pl.ds(start, size), :] = ref[pl.ds(0, size), :]


def weighted(parts, orbitals, half, coef_ref, mu_ref, tile_ref):
    sums = {}
    for j in range(3):
        blocks = tile_blocks(half, tile_ref[j * LANES : (j + 1) * LANES, :], mu_ref[j : j + 1, :])
        for part in range(2):
            line = coef_ref[3 * part + j : 3 * part + j + 1, :] * F32(1.0 / orbitals)
            first, second = line[:, :LANES], line[:, LANES:]
            own = jnp.where(half == 0, first, second)
            for which, (lane_coef, value) in enumerate(zip((own, first, second), blocks)):
                term = lane_coef * value
                sums[part, which] = term if j == 0 else sums[part, which] + term
    return sums


def own_kernel(parts, orbitals, coef_ref, mu_ref, *refs):
    chunk_refs, (out_ref, tile_ref) = refs[:parts], refs[parts:]
    half = lax.rem(lax.axis_index("quad"), 2)
    gather(parts, tile_ref, chunk_refs)
    for (part, which), value in weighted(parts, orbitals, half, coef_ref, mu_ref, tile_ref).items():
        out_ref[part, which] = value


def far_kernel(parts, orbitals, coef_ref, mu_ref, own_ref, *refs):
    chunk_refs, (out_ref, tile_ref, made_ref, sem) = refs[:parts], refs[parts:]
    half = lax.rem(lax.axis_index("quad"), 2)
    gather(parts, tile_ref, chunk_refs)
    sums = weighted(parts, orbitals, 1 - half, coef_ref, mu_ref, tile_ref)
    copies = []
    for part in range(2):
        same = [own_ref[part, 0], sums[part, 0]]
        blocks = {
            (0, 0): jnp.where(half == 0, same[0], same[1]),
            (0, 1): own_ref[part, 2] + sums[part, 2],
            (1, 0): own_ref[part, 1] + sums[part, 1],
            (1, 1): jnp.where(half == 0, same[1], same[0]),
        }
        for (x, y), value in blocks.items():
            made_ref[part, x * LANES : (x + 1) * LANES, y * LANES : (y + 1) * LANES] = value
        copies.append(pltpu.make_async_copy(made_ref.at[part], out_ref.at[0, part], sem.at[part]))
        copies[-1].start()
    for copy in copies:
        copy.wait()


def struct(*shape, dtype=F32):
    return jax.ShapeDtypeStruct(shape, dtype)


def cost(flops, nbytes):
    return pl.CostEstimate(flops=flops, bytes_accessed=nbytes, transcendentals=0)


def body(sources, onsite, strain, present):
    n_rows = lax.axis_size("rows")
    n_quad = lax.axis_size("quad")
    points = PTS_DEV * n_quad
    rows, sites, columns = sources.shape
    count = sites // 2
    orbitals = rows * sites * n_rows
    tail = 2 * rows * (sites // LANES)
    payload = 2 * count + shared(count) + tail
    first, second, table = pl.pallas_call(
        edges_kernel,
        out_shape=(struct(payload, LANES), struct(payload, LANES), struct(sites, LANES)),
        in_specs=[HBM] * 4,
        out_specs=(VMEM, VMEM, VMEM),
        scratch_shapes=[
            pltpu.VMEM((4, sites, LANES), F32),
            pltpu.VMEM((rows, sites), F32),
            pltpu.VMEM((rows, sites), F32),
            pltpu.VMEM((rows, sites), jnp.int32),
            pltpu.SemaphoreType.DMA((5,)),
        ],
        compiler_params=PARAMS,
        name="edges",
    )(*(pltpu.with_memory_space_constraint(x, pltpu.HBM) for x in (sources, onsite, strain, present)))
    halo = []
    for value, start in ((first, 0), (second, 1)):
        bonds = [(i, i + 1) for i in range(start, n_rows - 1, 2)]
        halo.append(lax.ppermute(value, "rows", bonds + [(j, i) for i, j in bonds]))
    outer_depth = 4 * count
    inner = pl.pallas_call(
        inner_kernel,
        out_shape=(
            struct(2, rows, 2, count, LANES),
            struct(2, rows, 2, count, LANES),
            struct(2, 7, count, LANES),
            struct(MU_ROWS, LANES),
            struct(columns, 3 * LANES),
            struct(columns, outer_depth, dtype=BF16),
            struct(columns, outer_depth, dtype=BF16),
        ),
        in_specs=[ANY, VMEM],
        out_specs=(VMEM,) * 7,
        scratch_shapes=[pltpu.VMEM((2, rows, sites, LANES), F32), pltpu.SemaphoreType.DMA((2,))],
        compiler_params=PARAMS,
        cost_estimate=cost(10**9, 8 * 2**20),
        name="inner",
    )(sources, table)
    b_all = inner[0]

    pairwise = n_rows == 4
    parts = n_rows if pairwise else 1
    far_first = list(range(parts - 1, 0, -1))
    size = 3 * LANES // parts
    *chunks, fields = pl.pallas_call(
        functools.partial(outer_kernel, parts),
        out_shape=(struct(size + MU_ROWS, LANES),) * parts + (struct(2, rows, 2, count, LANES),),
        in_specs=[VMEM] * 9,
        out_specs=(VMEM,) * (parts + 1),
        scratch_shapes=[pltpu.VMEM((2, sites, LANES), F32), pltpu.VMEM((3 * LANES, LANES), F32)],
        compiler_params=PARAMS,
        cost_estimate=cost(4 * 10**8, 4 * 2**20),
        name="outer",
    )(*inner, *halo)

    def partner(value):
        return lax.ppermute(value, "quad", [(i, i ^ 1) for i in range(n_quad)])

    def across(value, mask):
        return lax.ppermute(value, "rows", [(i, i ^ mask) for i in range(n_rows)])

    if pairwise:
        summed = pl.pallas_call(
            functools.partial(sum_kernel, size),
            out_shape=struct(size + MU_ROWS, LANES),
            in_specs=[VMEM] * parts,
            out_specs=VMEM,
            compiler_params=PARAMS,
            cost_estimate=cost(10**5, 2**18),
            name="sum",
        )(chunks[0], *(across(chunks[mask], mask) for mask in far_first))
        sums = [summed[:size]] + [across(summed[:size], mask) for mask in far_first[::-1]]
    else:
        shares = lax.all_gather(chunks[0][size:], "rows")
        mu = functools.reduce(joined, [shares[n] for n in range(n_rows)])
        summed = jnp.concatenate([lax.psum(chunks[0][:size], "rows"), mu], axis=0)
        sums = [summed[:size]]
    summed, fields = lax.optimization_barrier((summed, fields))
    far_summed = partner(summed)
    far_fields = partner(fields)
    mu, far_mu = summed[size:], far_summed[size:]
    far_sums = [far_summed[:size]]
    moments, coefs = pl.pallas_call(
        functools.partial(moments_kernel, points),
        out_shape=(struct(1, 2, rows, sites, columns), struct(8, columns)),
        in_specs=[VMEM] * 5,
        out_specs=(ANY, VMEM),
        scratch_shapes=[pltpu.VMEM((2, rows, 2, sites, LANES), F32), pltpu.SemaphoreType.DMA((2, rows, 2))],
        compiler_params=PARAMS,
        cost_estimate=cost(10**7, 8 * 2**20),
        name="moments",
    )(b_all, fields, far_fields, mu, far_mu)
    *late, coefs = lax.optimization_barrier((*sums[1:], coefs))
    sums = sums[:1] + late
    far_sums += [partner(value) for value in sums[1:]]
    own = pl.pallas_call(
        functools.partial(own_kernel, parts, orbitals),
        out_shape=struct(2, 3, LANES, LANES),
        in_specs=[VMEM] * (2 + parts),
        out_specs=VMEM,
        scratch_shapes=[pltpu.VMEM((3 * LANES, LANES), F32)],
        compiler_params=PARAMS,
        cost_estimate=cost(10**6, 2**20),
        name="own",
    )(coefs, mu, *sums)
    reduced = pl.pallas_call(
        functools.partial(far_kernel, parts, orbitals),
        out_shape=struct(1, 2, columns, columns),
        in_specs=[VMEM] * (3 + parts),
        out_specs=ANY,
        scratch_shapes=[
            pltpu.VMEM((3 * LANES, LANES), F32),
            pltpu.VMEM((2, columns, columns), F32),
            pltpu.SemaphoreType.DMA((2,)),
        ],
        compiler_params=PARAMS,
        cost_estimate=cost(10**6, 2**20),
        name="reduced",
    )(coefs, far_mu, own, *far_sums)
    return moments, reduced


def solution(mesh):
    in_specs = (
        P(("groups", "rows"), None, None),
        P(("groups", "rows"), None),
        P(("groups", "rows"), None),
        P(("groups", "rows"), None),
    )
    out_specs = (P("quad", None, ("groups", "rows"), None, None), P("quad", None, "groups", None))
    return jax.shard_map(body, mesh=mesh, in_specs=in_specs, out_specs=out_specs, check_vma=False)
```

```python
import functools
import math

import jax
import jax.numpy as jnp
from jax import lax
from jax.experimental import pallas as pl
from jax.experimental.pallas import tpu as pltpu
from jax.sharding import PartitionSpec as P

TOTAL_PTS = 32
PTS_DEV = 2
CENTER = 0.4
RADIUS = 1.0
MU_ROWS = 16
LANES = 128
LARGE = 1e30
F32 = jnp.float32
BF16 = jnp.bfloat16
PARAMS = pltpu.CompilerParams(vmem_limit_bytes=32 * 1024 * 1024)
VMEM = pl.BlockSpec(memory_space=pltpu.VMEM)
HBM = pl.BlockSpec(memory_space=pltpu.HBM)
ANY = pl.BlockSpec(memory_space=pl.ANY)


def ratio(top, bottom, good):
    return jnp.where(good, top / jnp.where(good, bottom, 1.0), 0.0)


def cmul(a, b):
    return (a[0] * b[0] - a[1] * b[1], a[0] * b[1] + a[1] * b[0])


def inverse(a):
    size = a[0] * a[0] + a[1] * a[1]
    return (a[0] / size, -a[1] / size)


def two_sum(a, b):
    total = a + b
    part = total - a
    return total, (a - (total - part)) + (b - part)


def pair_add(a, b):
    total, rest = two_sum(a[0], b[0])
    return two_sum(total, rest + (a[1] + b[1]))


def halves(a):
    scaled = F32(4097.0) * a
    high = scaled - (scaled - a)
    return high, a - high


def pair_times(a, b):
    product = a[0] * b
    (ah, al), (bh, bl) = halves(a[0]), halves(b)
    rest = ((ah * bh - product) + ah * bl + al * bh) + al * bl
    return two_sum(product, rest + a[1] * b)


def coefficients(block, points, order):
    line = [block[n : n + 1] for n in range(MU_ROWS)]
    mu = [(line[n], line[8 + n]) for n in range(6)]
    ok0 = line[0] > 0
    reach = 3.0 * line[14] * line[14]
    top, bottom = line[6] + reach, -line[7] - reach
    centre = jnp.clip(ratio(line[1], line[0], ok0), bottom, top)
    central = [mu[0]]
    level = mu
    for _ in range(5):
        level = [
            pair_add(after, tuple(-x for x in pair_times(now, centre))) for now, after in zip(level[:-1], level[1:])
        ]
        central.append(level[0])
    m0, m1, m2, m3, m4, m5 = (x[0] + x[1] for x in central)
    tiny = F32(1e-7)
    low, high = bottom - centre, top - centre
    a0 = jnp.clip(ratio(m1, m0, ok0), low, high)
    s11 = m2 - a0 * m1
    s12 = m3 - a0 * m2
    s13 = m4 - a0 * m3
    s14 = m5 - a0 * m4
    ok1 = ok0 & (s11 > tiny * m2)
    widest = 0.25 * (high - low) * (high - low)
    b1 = jnp.clip(ratio(s11, m0, ok1), 0.0, widest)
    g1 = ratio(s12, s11, ok1)
    a1 = jnp.clip(jnp.where(ok1, g1 - a0, a0), low, high)
    s22 = s13 - a1 * s12 - b1 * m2
    s23 = s14 - a1 * s13 - b1 * m3
    ok2 = ok1 & (s22 > tiny * m4)
    b2 = jnp.clip(ratio(s22, s11, ok2), 0.0, widest)
    a2 = jnp.clip(jnp.where(ok2, ratio(s23, s22, ok2) - g1, a1), low, high)
    a0, a1, a2 = a0 + centre, a1 + centre, a2 + centre
    leading = TOTAL_PTS // 4 - points // 2
    p = lax.broadcasted_iota(jnp.int32, (points, m0.shape[1]), 0).astype(F32)
    angle = 2.0 * math.pi * (p + leading + 0.5) / TOTAL_PTS
    zr = CENTER + RADIUS * jnp.cos(angle)
    zi = RADIUS * jnp.sin(angle)
    wr = RADIUS / points * jnp.cos(order * angle)
    wi = RADIUS / points * jnp.sin(order * angle)
    i2 = inverse((zr - a2, zi))
    i1 = inverse((zr - a1 - b2 * i2[0], zi - b2 * i2[1]))
    y0 = inverse((zr - a0 - b1 * i1[0], zi - b1 * i1[1]))
    y0 = cmul((wr, wi), y0)
    y1 = cmul(y0, i1)
    y2 = cmul(y1, i2)
    out = []
    for part in range(2):
        t0, t1, t2 = (jnp.sum(y[part], axis=0, keepdims=True) for y in (y0, y1, y2))
        out.append((t0 - a0 * t1 + (a0 * a1 - b1) * t2, t1 - (a0 + a1) * t2, t2))
    return out


def spread(table_ref, parity, lane):
    half = table_ref.shape[0] // 2
    rows = table_ref[pl.ds(parity, half, stride=2), :]
    return jnp.broadcast_to(rows[:, lane : lane + 1], (half, LANES))


def horizontal(even, odd):
    size = even.shape[0]
    site = lax.broadcasted_iota(jnp.int32, even.shape, 0)
    left = jnp.where(site == 0, 0.0, pltpu.roll(odd, 1, 0))
    right = jnp.where(site == size - 1, 0.0, pltpu.roll(even, size - 1, 0))
    return odd + left, even + right


def site_table(onsite, strain, present):
    return jnp.concatenate([present.astype(F32) * strain, onsite], axis=0)


def bound_up(i, p):
    return (i + p) % 2 == 0


def fold(value):
    tiles = value.reshape(value.shape[0] // 32, 4, 8, value.shape[1])
    return [tiles[n, 0] + tiles[n, 1] + (tiles[n, 2] + tiles[n, 3]) for n in range(tiles.shape[0])]


def total(terms):
    first, *others = [part for term in terms for part in fold(term)]
    whole = (first, jnp.zeros((8, LANES), F32))
    for part in others:
        high, rest = two_sum(whole[0], part)
        whole = (high, whole[1] + rest)
    for size in (4, 2, 1):
        whole = pair_add(*((whole[0][k : k + size], whole[1][k : k + size]) for k in (0, size)))
    return whole


def joined(one, two):
    high, rest = two_sum(one[:8], two[:8])
    high, rest = two_sum(high, rest + (one[8:] + two[8:]))
    row = lax.broadcasted_iota(jnp.int32, high.shape, 0)
    return jnp.concatenate(
        [jnp.where(row < 6, high, jnp.maximum(one[:8], two[:8])), jnp.where(row < 6, rest, jnp.maximum(one[8:], two[8:]))],
        axis=0,
    )


def split(value):
    high = value.astype(BF16)
    return high, (value - high.astype(F32)).astype(BF16)


def edges_kernel(
    sources_ref, onsite_ref, strain_ref, present_ref, first_ref, second_ref, table_ref,
    rows_ref, onsite_in, strain_in, present_in, sem,
):
    rows, sites, _ = sources_ref.shape
    count = sites // 2
    columns = pl.ds(pl.multiple_of(lax.rem(lax.axis_index("quad"), 2) * LANES, LANES), LANES)
    pairs = [(onsite_ref, onsite_in), (strain_ref, strain_in), (present_ref, present_in)]
    for start, slot in ((0, 0), (rows - 2, 2)):
        pairs.append((sources_ref.at[pl.ds(start, 2), :, columns], rows_ref.at[pl.ds(slot, 2)]))
    copies = [pltpu.make_async_copy(src, dst, sem.at[k]) for k, (src, dst) in enumerate(pairs)]
    for copy in copies:
        copy.start()
    for copy in copies[:3]:
        copy.wait()
    table = site_table(onsite_in[...], strain_in[...], present_in[...])
    tail = table.shape[0]
    table_ref[:, :tail] = table.T
    for part in range(sites // LANES):
        at = pl.ds(2 * count + shared(count) + part * tail, tail)
        first_ref[at, :] = second_ref[at, :] = table[:, part * LANES : (part + 1) * LANES]
    for copy in copies[3:]:
        copy.wait()

    def scaled(slot, row, parity):
        return rows_ref[slot, pl.ds(parity, count, stride=2), :] * spread(table_ref, parity, row)

    size = shared(count)
    up = [scaled(3, rows - 1, 0), scaled(3, rows - 1, 1), scaled(2, rows - 2, 0)[count - size :]]
    down = [scaled(0, 0, 0), scaled(0, 0, 1), scaled(1, 1, 0)[:size]]
    even = lax.rem(lax.axis_index("rows"), 2) == 0
    for block in range(3):
        at = pl.ds(block * count, up[block].shape[0])
        first_ref[at, :] = jnp.where(even, up[block], down[block])
        second_ref[at, :] = jnp.where(even, down[block], up[block])


def shared(count):
    return count // 2 + 8


def near(u, wanted, up_halo, down_halo, top):
    out = {}
    for i in wanted:
        sums = horizontal(u[i, 0], u[i, 1])
        for p in range(2):
            if bound_up(i, p):
                other = u[i + 1, p] if i < top else up_halo
            else:
                other = u[i - 1, p] if i > 0 else down_halo
            out[i, p] = sums[p] if other is None else sums[p] + other
    return out


def bonds(scale, w, wanted):
    u = {(i, p): scale[i, p] * w[i, p] for i in wanted for p in range(2)}
    out = {}
    for i in wanted:
        out[i, 0] = u[i, 0] * horizontal(u[i, 0], u[i, 1])[0]
        out[i, 1] = jnp.zeros_like(u[i, 1])
        for p in range(2):
            if bound_up(i, p) and (i + 1, p) in u:
                out[i, p] = out[i, p] + u[i, p] * u[i + 1, p]
    return out


def beside(i, top):
    return (1, 0) if i == 0 else (top - 1, 0)


def inner_kernel(sources_ref, table_ref, b_ref, w_ref, aid_ref, mu_ref, gram_ref, left_hi_ref, left_lo_ref, full_ref, sem):
    rows, sites, _ = sources_ref.shape
    count = sites // 2
    top = rows - 1
    half = lax.rem(lax.axis_index("quad"), 2)
    copies = [
        pltpu.make_async_copy(sources_ref.at[:, :, pl.ds(side * LANES, LANES)], full_ref.at[side], sem.at[side])
        for side in range(2)
    ]
    for copy in copies:
        copy.start()
    for copy in copies:
        copy.wait()
    keys = [(i, p) for i in range(rows) for p in range(2)]
    for side in range(2):
        for i, p in keys:
            b_ref[side, i, p] = full_ref[side, i, pl.ds(p, count, stride=2), :]
    scale = {(i, p): spread(table_ref, p, i) for i, p in keys}
    level = {(i, p): spread(table_ref, p, rows + i) for i, p in keys}
    b = {(i, p): b_ref[half, i, p] for i, p in keys}
    u0 = {k: scale[k] * b[k] for k in keys}
    n0 = near(u0, range(rows), None, None, top)
    w1 = {k: level[k] * b[k] - scale[k] * n0[k] for k in keys}
    for i, p in keys:
        w_ref[0, i, p] = w1[i, p]
    u1 = {k: scale[k] * w1[k] for k in keys}
    inside = [(i, p) for i, p in keys if 0 < i < top]
    n1 = near(u1, range(1, top), None, None, top)
    w2 = {k: level[k] * w1[k] - scale[k] * n1[k] for k in inside}
    for i, p in inside:
        w_ref[1, i, p] = w2[i, p]
    for index, i in enumerate((0, top)):
        for p in range(2):
            aid_ref[index, p] = scale[i, p]
            aid_ref[index, 2 + p] = level[i, p]
        k = beside(i, top)
        aid_ref[index, 4] = u0[i, 1]
        aid_ref[index, 5] = u1[k]
        aid_ref[index, 6] = scale[k] * w2[k]
    mu = [
        total([b[k] * b[k] for k in keys]),
        total([b[k] * w1[k] for k in inside]),
        total([w1[k] * w1[k] for k in inside]),
        total([w1[k] * w2[k] for k in inside]),
        total([w2[k] * w2[k] for k in inside]),
        total([level[k] * w2[k] * w2[k] - 2.0 * x for k, x in bonds(scale, w2, range(1, top)).items()]),
    ]
    table = table_ref[...]
    lane = lax.broadcasted_iota(jnp.int32, table.shape, 1)
    scales = jnp.max(jnp.where(lane < rows, table, 0.0), keepdims=True)
    is_level = (lane >= rows) & (lane < 2 * rows)
    most = jnp.max(jnp.where(is_level, table, -LARGE), keepdims=True)
    least = jnp.max(jnp.where(is_level, -table, -LARGE), keepdims=True)
    limits = [jnp.broadcast_to(x, (1, LANES)) for x in (most, least, scales)]
    mu_ref[...] = jnp.concatenate(
        [x[0] for x in mu] + limits[:2] + [x[1] for x in mu] + [limits[2], jnp.zeros((1, LANES), F32)], axis=0
    )
    order = inside + [k for k in keys if k not in inside]
    left = jnp.concatenate([jnp.concatenate([b_ref[0, i, p], b_ref[1, i, p]], axis=1) for i, p in order], axis=0)
    left_hi, left_lo = (x.T for x in split(left))
    own_hi, own_lo = split(jnp.concatenate([b[k] for k in order], axis=0))
    depth = len(inside) * count
    in_hi, in_lo = split(
        jnp.concatenate([jnp.concatenate([w1[k], w2[k]], axis=1) for k in inside], axis=0)
    )
    gram_ref[:, :LANES] = triple(left_hi, left_lo, own_hi, own_lo)
    gram_ref[:, LANES:] = triple(left_hi[:, :depth], left_lo[:, :depth], in_hi, in_lo)
    left_hi_ref[...] = left_hi[:, depth:]
    left_lo_ref[...] = left_lo[:, depth:]


def triple(left_hi, left_lo, right_hi, right_lo):
    def product(left, right):
        return jnp.dot(left, right, preferred_element_type=F32)

    return product(left_hi, right_hi) + (product(left_hi, right_lo) + product(left_lo, right_hi))


def outer_kernel(
    parts, b_ref, w_in_ref, aid_ref, mu_in_ref, gram_ref, left_hi_ref, left_lo_ref, first_ref, second_ref, *refs
):
    chunk_refs, (w_ref, far_ref, tile_ref) = refs[:parts], refs[parts:]
    _, rows, _, count, _ = b_ref.shape
    sites = 2 * count
    top = rows - 1
    half = lax.rem(lax.axis_index("quad"), 2)
    mine = lax.axis_index("rows")
    tail = 2 * rows
    even = lax.rem(mine, 2) == 0
    size = shared(count)

    def arrived(start, size):
        one, two = first_ref[pl.ds(start, size), :], second_ref[pl.ds(start, size), :]
        return jnp.where(even, two, one), jnp.where(even, one, two)

    for part in range(sites // LANES):
        for slot, value in enumerate(arrived(2 * count + size + part * tail, tail)):
            far_ref[slot, pl.ds(part * LANES, LANES), :tail] = value.T

    outside = [(i, p) for i in (0, top) for p in range(2)]
    aid = {i: [aid_ref[index, n] for n in range(7)] for index, i in enumerate((0, top))}
    scale = {(i, p): aid[i][p] for i, p in outside}
    level = {(i, p): aid[i][2 + p] for i, p in outside}
    b = {k: b_ref[half, k[0], k[1]] for k in outside}
    w1 = {k: w_in_ref[0, k[0], k[1]] for k in outside}
    below0, above0 = zip(arrived(0, count), arrived(count, count))
    w1[0, 1] = w1[0, 1] - scale[0, 1] * below0[1]
    w1[top, 1] = w1[top, 1] - scale[top, 1] * above0[1]
    u1 = {k: scale[k] * w1[k] for k in outside}

    missing = jnp.zeros((count - size, LANES), F32)
    low, high = arrived(2 * count, size)
    edge_next = {0: jnp.concatenate([missing, low], axis=0), top: jnp.concatenate([high, missing], axis=0)}
    edge_w2, far_w2 = {}, {}
    for i, halo, slot, row in ((0, below0, 0, top), (top, above0, 1, 0)):
        far_table = far_ref.at[slot]
        square = [spread(far_table, p, row) for p in range(2)]
        square = [x * x for x in square]
        far_level = [spread(far_table, p, rows + row) for p in range(2)]
        sums = horizontal(halo[0], halo[1])
        far1 = [
            far_level[0] * halo[0] - square[0] * (sums[0] + edge_next[i]),
            far_level[1] * halo[1] - square[1] * (sums[1] + aid[i][4]),
        ]
        sums = horizontal(u1[i, 0], u1[i, 1])
        edge_w2[i, 0] = level[i, 0] * w1[i, 0] - scale[i, 0] * (sums[0] + aid[i][5])
        edge_w2[i, 1] = level[i, 1] * w1[i, 1] - scale[i, 1] * (sums[1] + far1[1])
        sums = horizontal(far1[0], far1[1])
        far_w2[i] = far_level[1] * far1[1] - square[1] * (sums[1] + u1[i, 1])
    w2 = edge_w2
    site = lax.broadcasted_iota(jnp.int32, (count, LANES), 0)
    counted = {0: site >= count // 2, top: site < count // 2}
    pairs = bonds(scale, w2, (0,))
    pairs.update(bonds(scale, w2, (top,)))
    for i in (0, top):
        pairs[i, 0] = pairs[i, 0] + scale[i, 0] * w2[i, 0] * aid[i][6]
        pairs[i, 1] = pairs[i, 1] + scale[i, 1] * w2[i, 1] * jnp.where(counted[i], far_w2[i], 0.0)

    mu = [
        total([b[k] * w1[k] for k in outside]),
        total([w1[k] * w1[k] for k in outside]),
        total([w1[k] * w2[k] for k in outside]),
        total([w2[k] * w2[k] for k in outside]),
        total([level[k] * w2[k] * w2[k] - 2.0 * pairs[k] for k in outside]),
    ]
    zero = jnp.zeros((1, LANES), F32)
    mu = joined(
        mu_in_ref[...],
        jnp.concatenate([zero] + [x[0] for x in mu] + [zero - LARGE] * 2 + [zero] + [x[1] for x in mu] + [zero] * 2, axis=0),
    )
    for i, p in [(i, p) for i in range(rows) for p in range(2)]:
        w_ref[0, i, p] = w1[i, p] if (i, p) in w1 else w_in_ref[0, i, p]
        w_ref[1, i, p] = w2[i, p] if (i, p) in w2 else w_in_ref[1, i, p]
    right_hi, right_lo = split(
        jnp.concatenate([jnp.concatenate([w1[k], w2[k]], axis=1) for k in outside], axis=0)
    )
    more = triple(left_hi_ref[...], left_lo_ref[...], right_hi, right_lo)
    row = lax.broadcasted_iota(jnp.int32, (LANES, LANES), 0)
    lane = lax.broadcasted_iota(jnp.int32, (LANES, LANES), 1)
    for j in range(3):
        lanes = slice(j * LANES, (j + 1) * LANES)
        first, second = gram_ref[:LANES, lanes], gram_ref[LANES:, lanes]
        if j:
            lanes = slice((j - 1) * LANES, j * LANES)
            first, second = first + more[:LANES, lanes], second + more[LANES:, lanes]
        own = jnp.where(half == 0, first, second)
        cross = jnp.where(half == 0, second, first)
        tile_ref[pl.ds(j * LANES, LANES), :] = jnp.where(row < lane, own, cross)
    size = 3 * LANES // parts
    for part, ref in enumerate(chunk_refs):
        start = pl.multiple_of((mine ^ part) * size if parts > 1 else 0, 8)
        ref[pl.ds(0, size), :] = tile_ref[pl.ds(start, size), :]
        ref[pl.ds(size, MU_ROWS), :] = mu


def sum_kernel(size, *refs):
    *shares, out_ref = refs
    at, tail = pl.ds(0, size), pl.ds(size, MU_ROWS)
    out_ref[at, :] = (shares[0][at, :] + shares[1][at, :]) + (shares[2][at, :] + shares[3][at, :])
    out_ref[tail, :] = joined(
        joined(shares[0][tail, :], shares[1][tail, :]), joined(shares[2][tail, :], shares[3][tail, :])
    )


def moments_kernel(points, b_ref, w_ref, v_ref, mu_ref, nu_ref, out_ref, coef_ref, made_ref, out_sem):
    quad = lax.axis_index("quad")
    half = lax.rem(quad, 2)
    _, rows, _, count, _ = b_ref.shape
    first = jnp.where(half == 0, mu_ref[...], nu_ref[...])
    second = jnp.where(half == 0, nu_ref[...], mu_ref[...])
    mu = jnp.concatenate([first, second], axis=1)
    coefs = coefficients(mu, points, (quad + 1).astype(F32))
    lines = [line for part in coefs for line in part]
    coef_ref[...] = jnp.concatenate(lines + [jnp.zeros_like(lines[0])] * 2, axis=0)
    stores = []
    for i in range(rows):
        for side in range(2):
            lanes = slice(side * LANES, (side + 1) * LANES)
            for p in range(2):
                fields = [b_ref[side, i, p]]
                fields += [jnp.where(half == side, w_ref[j, i, p], v_ref[j, i, p]) for j in range(2)]
                for part in range(2):
                    terms = [lines[3 * part + j][:, lanes] * fields[j] for j in range(3)]
                    made_ref[part, i, side, pl.ds(p, count, stride=2), :] = terms[0] + terms[1] + terms[2]
            for part in range(2):
                copy = pltpu.make_async_copy(
                    made_ref.at[part, i, side],
                    out_ref.at[0, part, i, :, pl.ds(side * LANES, LANES)],
                    out_sem.at[part, i, side],
                )
                copy.start()
                stores.append(copy)
    for copy in stores:
        copy.wait()


def tile_blocks(half, tile, mu):
    row = lax.broadcasted_iota(jnp.int32, (LANES, LANES), 0)
    lane = lax.broadcasted_iota(jnp.int32, (LANES, LANES), 1)
    flip = tile.T
    same = jnp.where(row < lane, tile, jnp.where(row > lane, flip, mu))
    below = jnp.where(half == 0, jnp.where(row >= lane, tile, 0.0), jnp.where(row < lane, flip, 0.0))
    above = jnp.where(half == 0, jnp.where(row <= lane, flip, 0.0), jnp.where(row > lane, tile, 0.0))
    return same, below, above


def gather(parts, tile_ref, chunk_refs):
    size = 3 * LANES // parts
    for part, ref in zip(range(parts), chunk_refs):
        start = pl.multiple_of((lax.axis_index("rows") ^ part) * size if parts > 1 else 0, 8)
        tile_ref[pl.ds(start, size), :] = ref[pl.ds(0, size), :]


def weighted(parts, orbitals, half, coef_ref, mu_ref, tile_ref):
    sums = {}
    for j in range(3):
        blocks = tile_blocks(half, tile_ref[j * LANES : (j + 1) * LANES, :], mu_ref[j : j + 1, :])
        for part in range(2):
            line = coef_ref[3 * part + j : 3 * part + j + 1, :] * F32(1.0 / orbitals)
            first, second = line[:, :LANES], line[:, LANES:]
            own = jnp.where(half == 0, first, second)
            for which, (lane_coef, value) in enumerate(zip((own, first, second), blocks)):
                term = lane_coef * value
                sums[part, which] = term if j == 0 else sums[part, which] + term
    return sums


def own_kernel(parts, orbitals, coef_ref, mu_ref, *refs):
    chunk_refs, (out_ref, tile_ref) = refs[:parts], refs[parts:]
    half = lax.rem(lax.axis_index("quad"), 2)
    gather(parts, tile_ref, chunk_refs)
    for (part, which), value in weighted(parts, orbitals, half, coef_ref, mu_ref, tile_ref).items():
        out_ref[part, which] = value


def far_kernel(parts, orbitals, coef_ref, mu_ref, own_ref, *refs):
    chunk_refs, (out_ref, tile_ref, made_ref, sem) = refs[:parts], refs[parts:]
    half = lax.rem(lax.axis_index("quad"), 2)
    gather(parts, tile_ref, chunk_refs)
    sums = weighted(parts, orbitals, 1 - half, coef_ref, mu_ref, tile_ref)
    copies = []
    for part in range(2):
        same = [own_ref[part, 0], sums[part, 0]]
        blocks = {
            (0, 0): jnp.where(half == 0, same[0], same[1]),
            (0, 1): own_ref[part, 2] + sums[part, 2],
            (1, 0): own_ref[part, 1] + sums[part, 1],
            (1, 1): jnp.where(half == 0, same[1], same[0]),
        }
        for (x, y), value in blocks.items():
            made_ref[part, x * LANES : (x + 1) * LANES, y * LANES : (y + 1) * LANES] = value
        copies.append(pltpu.make_async_copy(made_ref.at[part], out_ref.at[0, part], sem.at[part]))
        copies[-1].start()
    for copy in copies:
        copy.wait()


def struct(*shape, dtype=F32):
    return jax.ShapeDtypeStruct(shape, dtype)


def cost(flops, nbytes):
    return pl.CostEstimate(flops=flops, bytes_accessed=nbytes, transcendentals=0)


def body(sources, onsite, strain, present):
    n_rows = lax.axis_size("rows")
    n_quad = lax.axis_size("quad")
    points = PTS_DEV * n_quad
    rows, sites, columns = sources.shape
    count = sites // 2
    orbitals = rows * sites * n_rows
    tail = 2 * rows * (sites // LANES)
    payload = 2 * count + shared(count) + tail
    first, second, table = pl.pallas_call(
        edges_kernel,
        out_shape=(struct(payload, LANES), struct(payload, LANES), struct(sites, LANES)),
        in_specs=[HBM] * 4,
        out_specs=(VMEM, VMEM, VMEM),
        scratch_shapes=[
            pltpu.VMEM((4, sites, LANES), F32),
            pltpu.VMEM((rows, sites), F32),
            pltpu.VMEM((rows, sites), F32),
            pltpu.VMEM((rows, sites), jnp.int32),
            pltpu.SemaphoreType.DMA((5,)),
        ],
        compiler_params=PARAMS,
        name="edges",
    )(*(pltpu.with_memory_space_constraint(x, pltpu.HBM) for x in (sources, onsite, strain, present)))
    halo = []
    for value, start in ((first, 0), (second, 1)):
        bonds = [(i, i + 1) for i in range(start, n_rows - 1, 2)]
        halo.append(lax.ppermute(value, "rows", bonds + [(j, i) for i, j in bonds]))
    outer_depth = 4 * count
    inner = pl.pallas_call(
        inner_kernel,
        out_shape=(
            struct(2, rows, 2, count, LANES),
            struct(2, rows, 2, count, LANES),
            struct(2, 7, count, LANES),
            struct(MU_ROWS, LANES),
            struct(columns, 3 * LANES),
            struct(columns, outer_depth, dtype=BF16),
            struct(columns, outer_depth, dtype=BF16),
        ),
        in_specs=[ANY, VMEM],
        out_specs=(VMEM,) * 7,
        scratch_shapes=[pltpu.VMEM((2, rows, sites, LANES), F32), pltpu.SemaphoreType.DMA((2,))],
        compiler_params=PARAMS,
        cost_estimate=cost(10**9, 8 * 2**20),
        name="inner",
    )(sources, table)
    b_all = inner[0]

    pairwise = n_rows == 4
    parts = n_rows if pairwise else 1
    far_first = list(range(parts - 1, 0, -1))
    size = 3 * LANES // parts
    *chunks, fields = pl.pallas_call(
        functools.partial(outer_kernel, parts),
        out_shape=(struct(size + MU_ROWS, LANES),) * parts + (struct(2, rows, 2, count, LANES),),
        in_specs=[VMEM] * 9,
        out_specs=(VMEM,) * (parts + 1),
        scratch_shapes=[pltpu.VMEM((2, sites, LANES), F32), pltpu.VMEM((3 * LANES, LANES), F32)],
        compiler_params=PARAMS,
        cost_estimate=cost(4 * 10**8, 4 * 2**20),
        name="outer",
    )(*inner, *halo)

    def partner(value):
        return lax.ppermute(value, "quad", [(i, i ^ 1) for i in range(n_quad)])

    def across(value, mask):
        return lax.ppermute(value, "rows", [(i, i ^ mask) for i in range(n_rows)])

    if pairwise:
        summed = pl.pallas_call(
            functools.partial(sum_kernel, size),
            out_shape=struct(size + MU_ROWS, LANES),
            in_specs=[VMEM] * parts,
            out_specs=VMEM,
            compiler_params=PARAMS,
            cost_estimate=cost(10**5, 2**18),
            name="sum",
        )(chunks[0], *(across(chunks[mask], mask) for mask in far_first))
        sums = [summed[:size]] + [across(summed[:size], mask) for mask in far_first[::-1]]
    else:
        shares = lax.all_gather(chunks[0][size:], "rows")
        mu = functools.reduce(joined, [shares[n] for n in range(n_rows)])
        summed = jnp.concatenate([lax.psum(chunks[0][:size], "rows"), mu], axis=0)
        sums = [summed[:size]]
    summed, fields = lax.optimization_barrier((summed, fields))
    far_summed = partner(summed)
    far_fields = partner(fields)
    mu, far_mu = summed[size:], far_summed[size:]
    far_sums = [far_summed[:size]]
    moments, coefs = pl.pallas_call(
        functools.partial(moments_kernel, points),
        out_shape=(struct(1, 2, rows, sites, columns), struct(8, columns)),
        in_specs=[VMEM] * 5,
        out_specs=(ANY, VMEM),
        scratch_shapes=[pltpu.VMEM((2, rows, 2, sites, LANES), F32), pltpu.SemaphoreType.DMA((2, rows, 2))],
        compiler_params=PARAMS,
        cost_estimate=cost(10**7, 8 * 2**20),
        name="moments",
    )(b_all, fields, far_fields, mu, far_mu)
    *late, coefs = lax.optimization_barrier((*sums[1:], coefs))
    sums = sums[:1] + late
    if late:
        far_late = partner(jnp.concatenate(late, axis=0))
        far_sums += [far_late[n * size : (n + 1) * size] for n in range(len(late))]
    own = pl.pallas_call(
        functools.partial(own_kernel, parts, orbitals),
        out_shape=struct(2, 3, LANES, LANES),
        in_specs=[VMEM] * (2 + parts),
        out_specs=VMEM,
        scratch_shapes=[pltpu.VMEM((3 * LANES, LANES), F32)],
        compiler_params=PARAMS,
        cost_estimate=cost(10**6, 2**20),
        name="own",
    )(coefs, mu, *sums)
    reduced = pl.pallas_call(
        functools.partial(far_kernel, parts, orbitals),
        out_shape=struct(1, 2, columns, columns),
        in_specs=[VMEM] * (3 + parts),
        out_specs=ANY,
        scratch_shapes=[
            pltpu.VMEM((3 * LANES, LANES), F32),
            pltpu.VMEM((2, columns, columns), F32),
            pltpu.SemaphoreType.DMA((2,)),
        ],
        compiler_params=PARAMS,
        cost_estimate=cost(10**6, 2**20),
        name="reduced",
    )(coefs, far_mu, own, *far_sums)
    return moments, reduced


def solution(mesh):
    in_specs = (
        P(("groups", "rows"), None, None),
        P(("groups", "rows"), None),
        P(("groups", "rows"), None),
        P(("groups", "rows"), None),
    )
    out_specs = (P("quad", None, ("groups", "rows"), None, None), P("quad", None, "groups", None))
    return jax.shard_map(body, mesh=mesh, in_specs=in_specs, out_specs=out_specs, check_vma=False)
```

```python
import functools
import math

import jax
import jax.numpy as jnp
from jax import lax
from jax.experimental import pallas as pl
from jax.experimental.pallas import tpu as pltpu
from jax.sharding import PartitionSpec as P

TOTAL_PTS = 32
PTS_DEV = 2
CENTER = 0.4
RADIUS = 1.0
MU_ROWS = 16
LANES = 128
LARGE = 1e30
F32 = jnp.float32
BF16 = jnp.bfloat16
PARAMS = pltpu.CompilerParams(vmem_limit_bytes=32 * 1024 * 1024)
VMEM = pl.BlockSpec(memory_space=pltpu.VMEM)
HBM = pl.BlockSpec(memory_space=pltpu.HBM)
ANY = pl.BlockSpec(memory_space=pl.ANY)


def ratio(top, bottom, good):
    return jnp.where(good, top / jnp.where(good, bottom, 1.0), 0.0)


def cmul(a, b):
    return (a[0] * b[0] - a[1] * b[1], a[0] * b[1] + a[1] * b[0])


def inverse(a):
    size = a[0] * a[0] + a[1] * a[1]
    return (a[0] / size, -a[1] / size)


def two_sum(a, b):
    total = a + b
    part = total - a
    return total, (a - (total - part)) + (b - part)


def pair_add(a, b):
    total, rest = two_sum(a[0], b[0])
    return two_sum(total, rest + (a[1] + b[1]))


def halves(a):
    scaled = F32(4097.0) * a
    high = scaled - (scaled - a)
    return high, a - high


def pair_times(a, b):
    product = a[0] * b
    (ah, al), (bh, bl) = halves(a[0]), halves(b)
    rest = ((ah * bh - product) + ah * bl + al * bh) + al * bl
    return two_sum(product, rest + a[1] * b)


def coefficients(block, points, order):
    line = [block[n : n + 1] for n in range(MU_ROWS)]
    mu = [(line[n], line[8 + n]) for n in range(6)]
    ok0 = line[0] > 0
    reach = 3.0 * line[14] * line[14]
    top, bottom = line[6] + reach, -line[7] - reach
    centre = jnp.clip(ratio(line[1], line[0], ok0), bottom, top)
    central = [mu[0]]
    level = mu
    for _ in range(5):
        level = [
            pair_add(after, tuple(-x for x in pair_times(now, centre))) for now, after in zip(level[:-1], level[1:])
        ]
        central.append(level[0])
    m0, m1, m2, m3, m4, m5 = (x[0] + x[1] for x in central)
    tiny = F32(1e-7)
    low, high = bottom - centre, top - centre
    a0 = jnp.clip(ratio(m1, m0, ok0), low, high)
    s11 = m2 - a0 * m1
    s12 = m3 - a0 * m2
    s13 = m4 - a0 * m3
    s14 = m5 - a0 * m4
    ok1 = ok0 & (s11 > tiny * m2)
    widest = 0.25 * (high - low) * (high - low)
    b1 = jnp.clip(ratio(s11, m0, ok1), 0.0, widest)
    g1 = ratio(s12, s11, ok1)
    a1 = jnp.clip(jnp.where(ok1, g1 - a0, a0), low, high)
    s22 = s13 - a1 * s12 - b1 * m2
    s23 = s14 - a1 * s13 - b1 * m3
    ok2 = ok1 & (s22 > tiny * m4)
    b2 = jnp.clip(ratio(s22, s11, ok2), 0.0, widest)
    a2 = jnp.clip(jnp.where(ok2, ratio(s23, s22, ok2) - g1, a1), low, high)
    a0, a1, a2 = a0 + centre, a1 + centre, a2 + centre
    leading = TOTAL_PTS // 4 - points // 2
    p = lax.broadcasted_iota(jnp.int32, (points, m0.shape[1]), 0).astype(F32)
    angle = 2.0 * math.pi * (p + leading + 0.5) / TOTAL_PTS
    zr = CENTER + RADIUS * jnp.cos(angle)
    zi = RADIUS * jnp.sin(angle)
    wr = RADIUS / points * jnp.cos(order * angle)
    wi = RADIUS / points * jnp.sin(order * angle)
    i2 = inverse((zr - a2, zi))
    i1 = inverse((zr - a1 - b2 * i2[0], zi - b2 * i2[1]))
    y0 = inverse((zr - a0 - b1 * i1[0], zi - b1 * i1[1]))
    y0 = cmul((wr, wi), y0)
    y1 = cmul(y0, i1)
    y2 = cmul(y1, i2)
    out = []
    for part in range(2):
        t0, t1, t2 = (jnp.sum(y[part], axis=0, keepdims=True) for y in (y0, y1, y2))
        out.append((t0 - a0 * t1 + (a0 * a1 - b1) * t2, t1 - (a0 + a1) * t2, t2))
    return out


def spread(table_ref, parity, lane):
    half = table_ref.shape[0] // 2
    rows = table_ref[pl.ds(parity, half, stride=2), :]
    return jnp.broadcast_to(rows[:, lane : lane + 1], (half, LANES))


def horizontal(even, odd):
    size = even.shape[0]
    site = lax.broadcasted_iota(jnp.int32, even.shape, 0)
    left = jnp.where(site == 0, 0.0, pltpu.roll(odd, 1, 0))
    right = jnp.where(site == size - 1, 0.0, pltpu.roll(even, size - 1, 0))
    return odd + left, even + right


def site_table(onsite, strain, present):
    return jnp.concatenate([present.astype(F32) * strain, onsite], axis=0)


def bound_up(i, p):
    return (i + p) % 2 == 0


def fold(value):
    tiles = value.reshape(value.shape[0] // 32, 4, 8, value.shape[1])
    return [tiles[n, 0] + tiles[n, 1] + (tiles[n, 2] + tiles[n, 3]) for n in range(tiles.shape[0])]


def total(terms):
    first, *others = [part for term in terms for part in fold(term)]
    whole = (first, jnp.zeros((8, LANES), F32))
    for part in others:
        high, rest = two_sum(whole[0], part)
        whole = (high, whole[1] + rest)
    for size in (4, 2, 1):
        whole = pair_add(*((whole[0][k : k + size], whole[1][k : k + size]) for k in (0, size)))
    return whole


def joined(one, two):
    high, rest = two_sum(one[:8], two[:8])
    high, rest = two_sum(high, rest + (one[8:] + two[8:]))
    row = lax.broadcasted_iota(jnp.int32, high.shape, 0)
    return jnp.concatenate(
        [jnp.where(row < 6, high, jnp.maximum(one[:8], two[:8])), jnp.where(row < 6, rest, jnp.maximum(one[8:], two[8:]))],
        axis=0,
    )


def split(value):
    high = value.astype(BF16)
    return high, (value - high.astype(F32)).astype(BF16)


def edges_kernel(
    sources_ref, onsite_ref, strain_ref, present_ref, first_ref, second_ref, table_ref,
    rows_ref, onsite_in, strain_in, present_in, sem,
):
    rows, sites, _ = sources_ref.shape
    count = sites // 2
    columns = pl.ds(pl.multiple_of(lax.rem(lax.axis_index("quad"), 2) * LANES, LANES), LANES)
    pairs = [(onsite_ref, onsite_in), (strain_ref, strain_in), (present_ref, present_in)]
    for start, slot in ((0, 0), (rows - 2, 2)):
        pairs.append((sources_ref.at[pl.ds(start, 2), :, columns], rows_ref.at[pl.ds(slot, 2)]))
    copies = [pltpu.make_async_copy(src, dst, sem.at[k]) for k, (src, dst) in enumerate(pairs)]
    for copy in copies:
        copy.start()
    for copy in copies[:3]:
        copy.wait()
    table = site_table(onsite_in[...], strain_in[...], present_in[...])
    tail = table.shape[0]
    table_ref[:, :tail] = table.T
    for part in range(sites // LANES):
        at = pl.ds(2 * count + shared(count) + part * tail, tail)
        first_ref[at, :] = second_ref[at, :] = table[:, part * LANES : (part + 1) * LANES]
    for copy in copies[3:]:
        copy.wait()

    def scaled(slot, row, parity):
        return rows_ref[slot, pl.ds(parity, count, stride=2), :] * spread(table_ref, parity, row)

    size = shared(count)
    up = [scaled(3, rows - 1, 0), scaled(3, rows - 1, 1), scaled(2, rows - 2, 0)[count - size :]]
    down = [scaled(0, 0, 0), scaled(0, 0, 1), scaled(1, 1, 0)[:size]]
    even = lax.rem(lax.axis_index("rows"), 2) == 0
    for block in range(3):
        at = pl.ds(block * count, up[block].shape[0])
        first_ref[at, :] = jnp.where(even, up[block], down[block])
        second_ref[at, :] = jnp.where(even, down[block], up[block])


def shared(count):
    return count // 2 + 8


def near(u, wanted, up_halo, down_halo, top):
    out = {}
    for i in wanted:
        sums = horizontal(u[i, 0], u[i, 1])
        for p in range(2):
            if bound_up(i, p):
                other = u[i + 1, p] if i < top else up_halo
            else:
                other = u[i - 1, p] if i > 0 else down_halo
            out[i, p] = sums[p] if other is None else sums[p] + other
    return out


def bonds(scale, w, wanted):
    u = {(i, p): scale[i, p] * w[i, p] for i in wanted for p in range(2)}
    out = {}
    for i in wanted:
        out[i, 0] = u[i, 0] * horizontal(u[i, 0], u[i, 1])[0]
        out[i, 1] = jnp.zeros_like(u[i, 1])
        for p in range(2):
            if bound_up(i, p) and (i + 1, p) in u:
                out[i, p] = out[i, p] + u[i, p] * u[i + 1, p]
    return out


def beside(i, top):
    return (1, 0) if i == 0 else (top - 1, 0)


def inner_kernel(sources_ref, table_ref, b_ref, w_ref, aid_ref, mu_ref, gram_ref, left_hi_ref, left_lo_ref, full_ref, sem):
    rows, sites, _ = sources_ref.shape
    count = sites // 2
    top = rows - 1
    half = lax.rem(lax.axis_index("quad"), 2)
    copies = [
        pltpu.make_async_copy(sources_ref.at[:, :, pl.ds(side * LANES, LANES)], full_ref.at[side], sem.at[side])
        for side in range(2)
    ]
    for copy in copies:
        copy.start()
    for copy in copies:
        copy.wait()
    keys = [(i, p) for i in range(rows) for p in range(2)]
    for side in range(2):
        for i, p in keys:
            b_ref[side, i, p] = full_ref[side, i, pl.ds(p, count, stride=2), :]
    scale = {(i, p): spread(table_ref, p, i) for i, p in keys}
    level = {(i, p): spread(table_ref, p, rows + i) for i, p in keys}
    b = {(i, p): b_ref[half, i, p] for i, p in keys}
    u0 = {k: scale[k] * b[k] for k in keys}
    n0 = near(u0, range(rows), None, None, top)
    w1 = {k: level[k] * b[k] - scale[k] * n0[k] for k in keys}
    for i, p in keys:
        w_ref[0, i, p] = w1[i, p]
    u1 = {k: scale[k] * w1[k] for k in keys}
    inside = [(i, p) for i, p in keys if 0 < i < top]
    n1 = near(u1, range(1, top), None, None, top)
    w2 = {k: level[k] * w1[k] - scale[k] * n1[k] for k in inside}
    for i, p in inside:
        w_ref[1, i, p] = w2[i, p]
    for index, i in enumerate((0, top)):
        for p in range(2):
            aid_ref[index, p] = scale[i, p]
            aid_ref[index, 2 + p] = level[i, p]
        k = beside(i, top)
        aid_ref[index, 4] = u0[i, 1]
        aid_ref[index, 5] = u1[k]
        aid_ref[index, 6] = scale[k] * w2[k]
    mu = [
        total([b[k] * b[k] for k in keys]),
        total([b[k] * w1[k] for k in inside]),
        total([w1[k] * w1[k] for k in inside]),
        total([w1[k] * w2[k] for k in inside]),
        total([w2[k] * w2[k] for k in inside]),
        total([level[k] * w2[k] * w2[k] - 2.0 * x for k, x in bonds(scale, w2, range(1, top)).items()]),
    ]
    table = table_ref[...]
    lane = lax.broadcasted_iota(jnp.int32, table.shape, 1)
    scales = jnp.max(jnp.where(lane < rows, table, 0.0), keepdims=True)
    is_level = (lane >= rows) & (lane < 2 * rows)
    most = jnp.max(jnp.where(is_level, table, -LARGE), keepdims=True)
    least = jnp.max(jnp.where(is_level, -table, -LARGE), keepdims=True)
    limits = [jnp.broadcast_to(x, (1, LANES)) for x in (most, least, scales)]
    mu_ref[...] = jnp.concatenate(
        [x[0] for x in mu] + limits[:2] + [x[1] for x in mu] + [limits[2], jnp.zeros((1, LANES), F32)], axis=0
    )
    order = inside + [k for k in keys if k not in inside]
    left = jnp.concatenate([jnp.concatenate([b_ref[0, i, p], b_ref[1, i, p]], axis=1) for i, p in order], axis=0)
    left_hi, left_lo = (x.T for x in split(left))
    own_hi, own_lo = split(jnp.concatenate([b[k] for k in order], axis=0))
    depth = len(inside) * count
    in_hi, in_lo = split(
        jnp.concatenate([jnp.concatenate([w1[k], w2[k]], axis=1) for k in inside], axis=0)
    )
    gram_ref[:, :LANES] = triple(left_hi, left_lo, own_hi, own_lo)
    gram_ref[:, LANES:] = triple(left_hi[:, :depth], left_lo[:, :depth], in_hi, in_lo)
    left_hi_ref[...] = left_hi[:, depth:]
    left_lo_ref[...] = left_lo[:, depth:]


def triple(left_hi, left_lo, right_hi, right_lo):
    def product(left, right):
        return jnp.dot(left, right, preferred_element_type=F32)

    return product(left_hi, right_hi) + (product(left_hi, right_lo) + product(left_lo, right_hi))


def outer_kernel(
    parts, b_ref, w_in_ref, aid_ref, mu_in_ref, gram_ref, left_hi_ref, left_lo_ref, first_ref, second_ref, *refs
):
    chunk_refs, (w_ref, far_ref, tile_ref) = refs[:parts], refs[parts:]
    _, rows, _, count, _ = b_ref.shape
    sites = 2 * count
    top = rows - 1
    half = lax.rem(lax.axis_index("quad"), 2)
    mine = lax.axis_index("rows")
    tail = 2 * rows
    even = lax.rem(mine, 2) == 0
    size = shared(count)

    def arrived(start, size):
        one, two = first_ref[pl.ds(start, size), :], second_ref[pl.ds(start, size), :]
        return jnp.where(even, two, one), jnp.where(even, one, two)

    for part in range(sites // LANES):
        for slot, value in enumerate(arrived(2 * count + size + part * tail, tail)):
            far_ref[slot, pl.ds(part * LANES, LANES), :tail] = value.T

    outside = [(i, p) for i in (0, top) for p in range(2)]
    aid = {i: [aid_ref[index, n] for n in range(7)] for index, i in enumerate((0, top))}
    scale = {(i, p): aid[i][p] for i, p in outside}
    level = {(i, p): aid[i][2 + p] for i, p in outside}
    b = {k: b_ref[half, k[0], k[1]] for k in outside}
    w1 = {k: w_in_ref[0, k[0], k[1]] for k in outside}
    below0, above0 = zip(arrived(0, count), arrived(count, count))
    w1[0, 1] = w1[0, 1] - scale[0, 1] * below0[1]
    w1[top, 1] = w1[top, 1] - scale[top, 1] * above0[1]
    u1 = {k: scale[k] * w1[k] for k in outside}

    missing = jnp.zeros((count - size, LANES), F32)
    low, high = arrived(2 * count, size)
    edge_next = {0: jnp.concatenate([missing, low], axis=0), top: jnp.concatenate([high, missing], axis=0)}
    edge_w2, far_w2 = {}, {}
    for i, halo, slot, row in ((0, below0, 0, top), (top, above0, 1, 0)):
        far_table = far_ref.at[slot]
        square = [spread(far_table, p, row) for p in range(2)]
        square = [x * x for x in square]
        far_level = [spread(far_table, p, rows + row) for p in range(2)]
        sums = horizontal(halo[0], halo[1])
        far1 = [
            far_level[0] * halo[0] - square[0] * (sums[0] + edge_next[i]),
            far_level[1] * halo[1] - square[1] * (sums[1] + aid[i][4]),
        ]
        sums = horizontal(u1[i, 0], u1[i, 1])
        edge_w2[i, 0] = level[i, 0] * w1[i, 0] - scale[i, 0] * (sums[0] + aid[i][5])
        edge_w2[i, 1] = level[i, 1] * w1[i, 1] - scale[i, 1] * (sums[1] + far1[1])
        sums = horizontal(far1[0], far1[1])
        far_w2[i] = far_level[1] * far1[1] - square[1] * (sums[1] + u1[i, 1])
    w2 = edge_w2
    site = lax.broadcasted_iota(jnp.int32, (count, LANES), 0)
    counted = {0: site >= count // 2, top: site < count // 2}
    pairs = bonds(scale, w2, (0,))
    pairs.update(bonds(scale, w2, (top,)))
    for i in (0, top):
        pairs[i, 0] = pairs[i, 0] + scale[i, 0] * w2[i, 0] * aid[i][6]
        pairs[i, 1] = pairs[i, 1] + scale[i, 1] * w2[i, 1] * jnp.where(counted[i], far_w2[i], 0.0)

    mu = [
        total([b[k] * w1[k] for k in outside]),
        total([w1[k] * w1[k] for k in outside]),
        total([w1[k] * w2[k] for k in outside]),
        total([w2[k] * w2[k] for k in outside]),
        total([level[k] * w2[k] * w2[k] - 2.0 * pairs[k] for k in outside]),
    ]
    zero = jnp.zeros((1, LANES), F32)
    mu = joined(
        mu_in_ref[...],
        jnp.concatenate([zero] + [x[0] for x in mu] + [zero - LARGE] * 2 + [zero] + [x[1] for x in mu] + [zero] * 2, axis=0),
    )
    for i, p in [(i, p) for i in range(rows) for p in range(2)]:
        w_ref[0, i, p] = w1[i, p] if (i, p) in w1 else w_in_ref[0, i, p]
        w_ref[1, i, p] = w2[i, p] if (i, p) in w2 else w_in_ref[1, i, p]
    right_hi, right_lo = split(
        jnp.concatenate([jnp.concatenate([w1[k], w2[k]], axis=1) for k in outside], axis=0)
    )
    more = triple(left_hi_ref[...], left_lo_ref[...], right_hi, right_lo)
    row = lax.broadcasted_iota(jnp.int32, (LANES, LANES), 0)
    lane = lax.broadcasted_iota(jnp.int32, (LANES, LANES), 1)
    for j in range(3):
        lanes = slice(j * LANES, (j + 1) * LANES)
        first, second = gram_ref[:LANES, lanes], gram_ref[LANES:, lanes]
        if j:
            lanes = slice((j - 1) * LANES, j * LANES)
            first, second = first + more[:LANES, lanes], second + more[LANES:, lanes]
        own = jnp.where(half == 0, first, second)
        cross = jnp.where(half == 0, second, first)
        tile_ref[pl.ds(j * LANES, LANES), :] = jnp.where(row < lane, own, cross)
    size = 3 * LANES // parts
    for part, ref in enumerate(chunk_refs):
        start = pl.multiple_of((mine ^ part) * size if parts > 1 else 0, 8)
        ref[pl.ds(0, size), :] = tile_ref[pl.ds(start, size), :]
        ref[pl.ds(size, MU_ROWS), :] = mu


def sum_kernel(size, *refs):
    *shares, out_ref = refs
    at, tail = pl.ds(0, size), pl.ds(size, MU_ROWS)
    out_ref[at, :] = (shares[0][at, :] + shares[1][at, :]) + (shares[2][at, :] + shares[3][at, :])
    out_ref[tail, :] = joined(
        joined(shares[0][tail, :], shares[1][tail, :]), joined(shares[2][tail, :], shares[3][tail, :])
    )


def moments_kernel(points, b_ref, w_ref, v_ref, mu_ref, nu_ref, out_ref, coef_ref, made_ref, out_sem):
    quad = lax.axis_index("quad")
    half = lax.rem(quad, 2)
    _, rows, _, count, _ = b_ref.shape
    first = jnp.where(half == 0, mu_ref[...], nu_ref[...])
    second = jnp.where(half == 0, nu_ref[...], mu_ref[...])
    mu = jnp.concatenate([first, second], axis=1)
    coefs = coefficients(mu, points, (quad + 1).astype(F32))
    lines = [line for part in coefs for line in part]
    coef_ref[...] = jnp.concatenate(lines + [jnp.zeros_like(lines[0])] * 2, axis=0)
    stores = []
    for i in range(rows):
        for side in range(2):
            lanes = slice(side * LANES, (side + 1) * LANES)
            for p in range(2):
                fields = [b_ref[side, i, p]]
                fields += [jnp.where(half == side, w_ref[j, i, p], v_ref[j, i, p]) for j in range(2)]
                for part in range(2):
                    terms = [lines[3 * part + j][:, lanes] * fields[j] for j in range(3)]
                    made_ref[part, i, side, pl.ds(p, count, stride=2), :] = terms[0] + terms[1] + terms[2]
            for part in range(2):
                copy = pltpu.make_async_copy(
                    made_ref.at[part, i, side],
                    out_ref.at[0, part, i, :, pl.ds(side * LANES, LANES)],
                    out_sem.at[part, i, side],
                )
                copy.start()
                stores.append(copy)
    for copy in stores:
        copy.wait()


def tile_blocks(half, tile, mu):
    row = lax.broadcasted_iota(jnp.int32, (LANES, LANES), 0)
    lane = lax.broadcasted_iota(jnp.int32, (LANES, LANES), 1)
    flip = tile.T
    same = jnp.where(row < lane, tile, jnp.where(row > lane, flip, mu))
    below = jnp.where(half == 0, jnp.where(row >= lane, tile, 0.0), jnp.where(row < lane, flip, 0.0))
    above = jnp.where(half == 0, jnp.where(row <= lane, flip, 0.0), jnp.where(row > lane, tile, 0.0))
    return same, below, above


def gather(parts, tile_ref, chunk_refs):
    size = 3 * LANES // parts
    for part, ref in zip(range(parts), chunk_refs):
        start = pl.multiple_of((lax.axis_index("rows") ^ part) * size if parts > 1 else 0, 8)
        tile_ref[pl.ds(start, size), :] = ref[pl.ds(0, size), :]


def weighted(parts, orbitals, half, coef_ref, mu_ref, tile_ref):
    sums = {}
    for j in range(3):
        blocks = tile_blocks(half, tile_ref[j * LANES : (j + 1) * LANES, :], mu_ref[j : j + 1, :])
        for part in range(2):
            line = coef_ref[3 * part + j : 3 * part + j + 1, :] * F32(1.0 / orbitals)
            first, second = line[:, :LANES], line[:, LANES:]
            own = jnp.where(half == 0, first, second)
            for which, (lane_coef, value) in enumerate(zip((own, first, second), blocks)):
                term = lane_coef * value
                sums[part, which] = term if j == 0 else sums[part, which] + term
    return sums


def own_kernel(parts, orbitals, coef_ref, mu_ref, *refs):
    chunk_refs, (out_ref, tile_ref) = refs[:parts], refs[parts:]
    half = lax.rem(lax.axis_index("quad"), 2)
    gather(parts, tile_ref, chunk_refs)
    for (part, which), value in weighted(parts, orbitals, half, coef_ref, mu_ref, tile_ref).items():
        out_ref[part, which] = value


def far_kernel(parts, orbitals, coef_ref, mu_ref, own_ref, *refs):
    chunk_refs, (out_ref, tile_ref, made_ref, sem) = refs[:parts], refs[parts:]
    half = lax.rem(lax.axis_index("quad"), 2)
    gather(parts, tile_ref, chunk_refs)
    sums = weighted(parts, orbitals, 1 - half, coef_ref, mu_ref, tile_ref)
    copies = []
    for part in range(2):
        same = [own_ref[part, 0], sums[part, 0]]
        blocks = {
            (0, 0): jnp.where(half == 0, same[0], same[1]),
            (0, 1): own_ref[part, 2] + sums[part, 2],
            (1, 0): own_ref[part, 1] + sums[part, 1],
            (1, 1): jnp.where(half == 0, same[1], same[0]),
        }
        for (x, y), value in blocks.items():
            made_ref[part, x * LANES : (x + 1) * LANES, y * LANES : (y + 1) * LANES] = value
        copies.append(pltpu.make_async_copy(made_ref.at[part], out_ref.at[0, part], sem.at[part]))
        copies[-1].start()
    for copy in copies:
        copy.wait()


def struct(*shape, dtype=F32):
    return jax.ShapeDtypeStruct(shape, dtype)


def cost(flops, nbytes):
    return pl.CostEstimate(flops=flops, bytes_accessed=nbytes, transcendentals=0)


def body(sources, onsite, strain, present):
    n_rows = lax.axis_size("rows")
    n_quad = lax.axis_size("quad")
    points = PTS_DEV * n_quad
    rows, sites, columns = sources.shape
    count = sites // 2
    orbitals = rows * sites * n_rows
    tail = 2 * rows * (sites // LANES)
    payload = 2 * count + shared(count) + tail
    first, second, table = pl.pallas_call(
        edges_kernel,
        out_shape=(struct(payload, LANES), struct(payload, LANES), struct(sites, LANES)),
        in_specs=[HBM] * 4,
        out_specs=(VMEM, VMEM, VMEM),
        scratch_shapes=[
            pltpu.VMEM((4, sites, LANES), F32),
            pltpu.VMEM((rows, sites), F32),
            pltpu.VMEM((rows, sites), F32),
            pltpu.VMEM((rows, sites), jnp.int32),
            pltpu.SemaphoreType.DMA((5,)),
        ],
        compiler_params=PARAMS,
        name="edges",
    )(*(pltpu.with_memory_space_constraint(x, pltpu.HBM) for x in (sources, onsite, strain, present)))
    halo = []
    for value, start in ((first, 0), (second, 1)):
        bonds = [(i, i + 1) for i in range(start, n_rows - 1, 2)]
        halo.append(lax.ppermute(value, "rows", bonds + [(j, i) for i, j in bonds]))
    outer_depth = 4 * count
    inner = pl.pallas_call(
        inner_kernel,
        out_shape=(
            struct(2, rows, 2, count, LANES),
            struct(2, rows, 2, count, LANES),
            struct(2, 7, count, LANES),
            struct(MU_ROWS, LANES),
            struct(columns, 3 * LANES),
            struct(columns, outer_depth, dtype=BF16),
            struct(columns, outer_depth, dtype=BF16),
        ),
        in_specs=[ANY, VMEM],
        out_specs=(VMEM,) * 7,
        scratch_shapes=[pltpu.VMEM((2, rows, sites, LANES), F32), pltpu.SemaphoreType.DMA((2,))],
        compiler_params=PARAMS,
        cost_estimate=cost(10**9, 8 * 2**20),
        name="inner",
    )(sources, table)
    b_all = inner[0]

    pairwise = n_rows == 4
    parts = n_rows if pairwise else 1
    far_first = list(range(parts - 1, 0, -1))
    size = 3 * LANES // parts
    *chunks, fields = pl.pallas_call(
        functools.partial(outer_kernel, parts),
        out_shape=(struct(size + MU_ROWS, LANES),) * parts + (struct(2, rows, 2, count, LANES),),
        in_specs=[VMEM] * 9,
        out_specs=(VMEM,) * (parts + 1),
        scratch_shapes=[pltpu.VMEM((2, sites, LANES), F32), pltpu.VMEM((3 * LANES, LANES), F32)],
        compiler_params=PARAMS,
        cost_estimate=cost(4 * 10**8, 4 * 2**20),
        name="outer",
    )(*inner, *halo)

    def partner(value):
        return lax.ppermute(value, "quad", [(i, i ^ 1) for i in range(n_quad)])

    def across(value, mask):
        return lax.ppermute(value, "rows", [(i, i ^ mask) for i in range(n_rows)])

    if pairwise:
        summed = pl.pallas_call(
            functools.partial(sum_kernel, size),
            out_shape=struct(size + MU_ROWS, LANES),
            in_specs=[VMEM] * parts,
            out_specs=VMEM,
            compiler_params=PARAMS,
            cost_estimate=cost(10**5, 2**18),
            name="sum",
        )(chunks[0], *(across(chunks[mask], mask) for mask in far_first))
        sums = [summed[:size]] + [across(summed[:size], mask) for mask in far_first[::-1]]
    else:
        shares = lax.all_gather(chunks[0][size:], "rows")
        mu = functools.reduce(joined, [shares[n] for n in range(n_rows)])
        summed = jnp.concatenate([lax.psum(chunks[0][:size], "rows"), mu], axis=0)
        sums = [summed[:size]]
    summed, fields = lax.optimization_barrier((summed, fields))
    far_fields = partner(fields)
    far_summed = partner(summed)
    mu, far_mu = summed[size:], far_summed[size:]
    far_sums = [far_summed[:size]]
    moments, coefs = pl.pallas_call(
        functools.partial(moments_kernel, points),
        out_shape=(struct(1, 2, rows, sites, columns), struct(8, columns)),
        in_specs=[VMEM] * 5,
        out_specs=(ANY, VMEM),
        scratch_shapes=[pltpu.VMEM((2, rows, 2, sites, LANES), F32), pltpu.SemaphoreType.DMA((2, rows, 2))],
        compiler_params=PARAMS,
        cost_estimate=cost(10**7, 8 * 2**20),
        name="moments",
    )(b_all, fields, far_fields, mu, far_mu)
    *late, coefs = lax.optimization_barrier((*sums[1:], coefs))
    sums = sums[:1] + late
    if late:
        far_late = partner(jnp.concatenate(late, axis=0))
        far_sums += [far_late[n * size : (n + 1) * size] for n in range(len(late))]
    own = pl.pallas_call(
        functools.partial(own_kernel, parts, orbitals),
        out_shape=struct(2, 3, LANES, LANES),
        in_specs=[VMEM] * (2 + parts),
        out_specs=VMEM,
        scratch_shapes=[pltpu.VMEM((3 * LANES, LANES), F32)],
        compiler_params=PARAMS,
        cost_estimate=cost(10**6, 2**20),
        name="own",
    )(coefs, mu, *sums)
    reduced = pl.pallas_call(
        functools.partial(far_kernel, parts, orbitals),
        out_shape=struct(1, 2, columns, columns),
        in_specs=[VMEM] * (3 + parts),
        out_specs=ANY,
        scratch_shapes=[
            pltpu.VMEM((3 * LANES, LANES), F32),
            pltpu.VMEM((2, columns, columns), F32),
            pltpu.SemaphoreType.DMA((2,)),
        ],
        compiler_params=PARAMS,
        cost_estimate=cost(10**6, 2**20),
        name="reduced",
    )(coefs, far_mu, own, *far_sums)
    return moments, reduced


def solution(mesh):
    in_specs = (
        P(("groups", "rows"), None, None),
        P(("groups", "rows"), None),
        P(("groups", "rows"), None),
        P(("groups", "rows"), None),
    )
    out_specs = (P("quad", None, ("groups", "rows"), None, None), P("quad", None, "groups", None))
    return jax.shard_map(body, mesh=mesh, in_specs=in_specs, out_specs=out_specs, check_vma=False)
```
